256 devices in a mesh: img: 4 (over x), band: 64 (over y, z, core).
Axes of the slice: x: 4, y: 4, z: 8, core: 2. Of those that a mesh axis runs over, the one named last changes fastest.
Arguments:
- features: bfloat16 [4, 512, 512, 256], P('img', 'band'), may hold values from -6 to 6
- w_rpn: bfloat16 [3, 3, 256, 256], replicated, may hold values from -0.125 to 0.125
- w_anchor: bfloat16 [256, 15], replicated, may hold values from -0.375 to 0.375
- pixel_slots: int32 [4, 64, 64, 32], P('img', None, 'band'), may hold values from 0 to 4095
- sample_slot: int32 [4, 512, 49, 4], P('img', 'band'), may hold values from 0 to 2047
- sample_weight: float32 [4, 512, 49, 4], P('img', 'band'), may hold values from 0 to 1, as said below
- roi_labels: int32 [4, 512], P('img', 'band'), may hold values from 0 to 80
- w_fc1: bfloat16 [12544, 1024], P('band'), may hold values from -0.0546875 to 0.0546875
- w_fc2: bfloat16 [1024, 1024], replicated, may hold values from -0.1875 to 0.1875
- w_class: bfloat16 [1024, 81], replicated, may hold values from -6 to 6
Outputs:
- rpn_out: bfloat16 [4, 15, 512, 512], P('img', None, 'band')
- grad_fc1: float32 [12544, 1024], P('band')
- grad_fc2: float32 [1024, 1024], replicated
- grad_class: float32 [1024, 81], replicated
The draws below stay inside these ranges and needn't reach their ends.
Inputs may be any that keep to these rules, and one draw needn't show every extreme that they name: `pixel_slots`: a pixel of band b given as its row within the band times 512 plus its column. `sample_slot`: a slot of the proposal's head rank, band times 32 plus slot. `sample_weight`: nonnegative bilinear weights, the four of a bin summing to one.
All inputs are finite; a program needn't handle non-finite values.
Results may differ from the reference program's by a relative error of at most 0.015.
Values may be sent and summed in bfloat16 or wider, within the bound.
No kernel may reach another device: no remote copies, remote signals or barrier semaphores. Data moves between devices by JAX's collectives and lax.ppermute only.
A program may use at most 128 MiB of HBM per device.

```python
import jax
import jax.numpy as jnp
from jax import lax

C = 256
HID = 1024
BINS = 49
NCLS = 81
ANCH = 15
W = 512
ROWS_DEV = 8
ROI_DEV = 8
H = 512
ROIS = 512
CAP = 32
SLOTS = 2048
IMAGES = 4
N_BAND = 64


def draw_sample_weight(key, part):
    key = jax.random.fold_in(key, 7)
    key_x, key_y = jax.random.split(key)
    frac_x = jax.random.uniform(key_x, (IMAGES, ROIS, BINS), jnp.float32)
    frac_y = jax.random.uniform(key_y, (IMAGES, ROIS, BINS), jnp.float32)
    corners = [(1.0 - frac_x) * (1.0 - frac_y), frac_x * (1.0 - frac_y), (1.0 - frac_x) * frac_y, frac_x * frac_y]
    return jnp.stack(corners, axis=-1)


def place_ends(values, stream_key, least, largest):
    place = [jax.random.randint(jax.random.fold_in(stream_key, axis), (), 0, length) for axis, length in enumerate(values.shape)]
    longest = values.shape.index(max(values.shape))
    neighbour = place[:longest] + [(place[longest] + 1) % values.shape[longest]] + place[longest + 1:]
    return values.at[tuple(place)].set(least).at[tuple(neighbour)].set(largest)


def level_of(own_key, shape, cuts, least, top_value):
    def one(axis_at, parts):
        heights = jax.random.uniform(jax.random.fold_in(jax.random.fold_in(own_key, 6), axis_at), (parts,), jnp.float32, least / len(cuts), top_value / len(cuts))
        return jnp.repeat(jnp.exp(heights), shape[axis_at] // parts).reshape((-1,) + (1,) * (len(shape) - axis_at - 1))

    gain = one(*cuts[0])
    for cut in cuts[1:]:
        gain = gain * one(*cut)
    return gain


def normal_values(key, shape, width, bound, cuts=(), held_as=jnp.bfloat16):
    drawn = jax.random.normal(key, shape, jnp.float32) * width
    if len(cuts) > 0:
        drawn = level_of(key, shape, cuts, -0.22, 0.18) * drawn
    return jnp.clip(drawn, min=-bound, max=bound).astype(held_as)


def setup_inputs(seed: int = 0) -> dict:
    key_list = jax.random.split(jax.random.key(seed), 11)
    return {
        "features": normal_values(key_list[0], (IMAGES, H, W, C), 1.0, 6.0, ((0, 4), (1, 64))),
        "w_rpn": normal_values(key_list[1], (3, 3, C, C), (9 * C) ** -0.5, 0.125),
        "w_anchor": normal_values(key_list[2], (C, ANCH), C ** -0.5, 0.375),
        "pixel_slots": place_ends(jax.random.randint(key_list[3], (IMAGES, N_BAND, N_BAND, CAP), 0, ROWS_DEV * W), jax.random.fold_in(key_list[3], 1), 0, (ROWS_DEV * W) - 1).astype(jnp.int32),
        "sample_slot": place_ends(jax.random.randint(key_list[4], (IMAGES, ROIS, BINS, 4), 0, SLOTS), jax.random.fold_in(key_list[4], 1), 0, SLOTS - 1).astype(jnp.int32),
        "sample_weight": draw_sample_weight(jax.random.fold_in(key_list[10], 71), 0),
        "roi_labels": place_ends(jax.random.randint(key_list[6], (IMAGES, ROIS), 0, NCLS), jax.random.fold_in(key_list[6], 1), 0, NCLS - 1).astype(jnp.int32),
        "w_fc1": normal_values(key_list[7], (C * BINS, HID), (C * BINS) ** -0.5, 0.0546875, ((0, 64),)),
        "w_fc2": normal_values(key_list[8], (HID, HID), HID ** -0.5, 0.1875),
        "w_class": normal_values(key_list[9], (HID, NCLS), 0.45, 6.0),
    }


def gelu_slope(value):
    out, pull = jax.vjp(jax.nn.gelu, value)
    return pull(jnp.ones_like(value))[0]

def matmul(left, right):
    return jnp.dot(left.astype(jnp.float32), right.astype(jnp.float32), precision=lax.Precision.HIGHEST, preferred_element_type=jnp.float32)

def inner_rows(left, right):
    return lax.dot_general(left.astype(jnp.float32), right.astype(jnp.float32), (((0,), (0,)), ((), ())), precision=lax.Precision.HIGHEST, preferred_element_type=jnp.float32)

def outer_cols(left, right):
    return lax.dot_general(left.astype(jnp.float32), right.astype(jnp.float32), (((1,), (1,)), ((), ())), precision=lax.Precision.HIGHEST, preferred_element_type=jnp.float32)

def rpn_image(feature, w_rpn, w_anchor):
    padded = jnp.pad(feature, ((1, 1), (1, 1), (0, 0)))
    total = jnp.zeros((H * W, C), jnp.float32)
    for dy in range(3):
        for dx in range(3):
            window = padded[dy:dy + H, dx:dx + W, :].reshape(H * W, C)
            total = total + matmul(window, w_rpn[dy, dx])
    hidden = jnp.maximum(total, 0.0).astype(jnp.bfloat16)
    result = matmul(hidden, w_anchor)
    return result.T.reshape(ANCH, H, W).astype(jnp.bfloat16)

def roi_image(feature, slots, sample_slot, sample_weight):
    flat = feature.reshape(H * W, C)
    base = (jnp.arange(N_BAND, dtype=jnp.int32) * (ROWS_DEV * W))[None, :, None]
    where = (slots + base).reshape(N_BAND, SLOTS).astype(jnp.int32)
    buffers = flat[where]
    heads = sample_slot.reshape(N_BAND, ROI_DEV * BINS * 4).astype(jnp.int32)
    picked = jax.vmap(lambda rows, index: rows[index])(buffers, heads)
    picked = picked.reshape(ROIS, BINS, 4, C).astype(jnp.float32)
    pooled = lax.optimization_barrier(jnp.sum(picked * sample_weight[..., None], axis=2)).astype(jnp.bfloat16)
    return jnp.transpose(pooled, (0, 2, 1)).reshape(ROIS, C * BINS)

def reference(features, w_rpn, w_anchor, pixel_slots, sample_slot, sample_weight, roi_labels, w_fc1, w_fc2, w_class):
    rpn_out = jnp.stack([rpn_image(features[i], w_rpn, w_anchor) for i in range(IMAGES)])
    grad_fc1 = jnp.zeros((C * BINS, HID), jnp.float32)
    grad_fc2 = jnp.zeros((HID, HID), jnp.float32)
    grad_class = jnp.zeros((HID, NCLS), jnp.float32)
    for i in range(IMAGES):
        x = roi_image(features[i], pixel_slots[i], sample_slot[i], sample_weight[i])
        a1 = matmul(x, w_fc1)
        h1 = jax.nn.gelu(a1).astype(jnp.bfloat16)
        a2 = matmul(h1, w_fc2)
        h2 = jax.nn.gelu(a2).astype(jnp.bfloat16)
        logits = matmul(h2, w_class)
        expo = jnp.exp(logits)
        prob = expo / lax.optimization_barrier(jnp.sum(expo, axis=1, keepdims=True))
        onehot = (roi_labels[i][:, None] == jnp.arange(NCLS, dtype=jnp.int32)[None, :]).astype(jnp.float32)
        dlogits = (prob - onehot).astype(jnp.bfloat16)
        grad_class = grad_class + inner_rows(h2, dlogits)
        dh2 = outer_cols(dlogits, w_class)
        da2 = (dh2 * gelu_slope(a2)).astype(jnp.bfloat16)
        grad_fc2 = grad_fc2 + inner_rows(h1, da2)
        dh1 = outer_cols(da2, w_fc2)
        da1 = (dh1 * gelu_slope(a1)).astype(jnp.bfloat16)
        grad_fc1 = grad_fc1 + inner_rows(x, da1)
    return (rpn_out, grad_fc1, grad_fc2, grad_class)
```

```python
import jax
import jax.numpy as jnp
from jax import lax
from jax.sharding import PartitionSpec as P

NY, NZ, NC = 4, 8, 2
BAND = NY * NZ * NC
F32, BF16 = jnp.float32, jnp.bfloat16
CORE_SWAP = [(b, b ^ 1) for b in range(BAND)]
Z_GROUPS = [[(y * NZ + z) * NC + c for z in range(NZ)] for y in range(NY) for c in range(NC)]
Y_GROUPS = [[(y * NZ + z) * NC + c for y in range(NY)] for z in range(NZ) for c in range(NC)]


def halo(array):
    devices = lax.axis_size("band")
    up = [(i, i + 1) for i in range(devices - 1)]
    down = [(j, i) for i, j in up]
    before = lax.ppermute(array[:, -1:], "band", up)
    after = lax.ppermute(array[:, :1], "band", down)
    return jnp.concatenate([before, array, after], axis=1)


def side_pad(array):
    return jnp.pad(array, ((0, 0), (0, 0), (1, 1), (0, 0)))


def conv_rows(source, w_rpn, count):
    batch = source.shape[0]
    width = source.shape[2] - 2
    channels = source.shape[3]
    total = jnp.zeros((batch * count * width, w_rpn.shape[3]), F32)
    for dy in range(3):
        for dx in range(3):
            window = source[:, dy : dy + count, dx : dx + width, :].reshape(
                batch * count * width, channels
            )
            total = total + jnp.dot(window, w_rpn[dy, dx], preferred_element_type=F32)
    return total


def rpn(features, w_rpn, w_anchor):
    batch, rows, width, channels = features.shape
    conv = conv_rows(side_pad(halo(features)), w_rpn, rows)
    hidden = jnp.maximum(conv, 0.0).astype(BF16)
    anchors = w_anchor.shape[1]
    flat = jnp.dot(hidden, w_anchor, preferred_element_type=F32)
    return jnp.transpose(flat.reshape(batch, rows, width, anchors), (0, 3, 1, 2)).astype(BF16)


def gelu_and_slope(value):
    out, pull = jax.vjp(jax.nn.gelu, value)
    return out.astype(BF16), pull(jnp.ones_like(value))[0]


def exchange(array, groups):
    return lax.all_to_all(
        array, "band", split_axis=0, concat_axis=0, tiled=True, axis_index_groups=groups
    )


def dot(left, right, contract):
    return lax.dot_general(left, right, ((contract[:1], contract[1:]), ((), ())), preferred_element_type=F32)


def shift_img(array, step):
    size = lax.axis_size("img")
    return lax.ppermute(array, "img", [(i, (i + step) % size) for i in range(size)])


def sum_chunks(chunks, image):
    size = chunks.shape[0]
    sent = chunks.astype(BF16)
    got = [
        shift_img(lax.dynamic_index_in_dim(sent, (image + step) % size, 0, False), step)
        for step in range(1, size)
    ]
    total = lax.dynamic_index_in_dim(chunks, image, 0, False)
    for part in got:
        total = total + part.astype(F32)
    return total


def spread_chunks(chunk, image):
    size = lax.axis_size("img")
    parts = [chunk] + [shift_img(chunk, step) for step in range(1, size)]
    stacked = jnp.stack(parts)
    order = (image - jnp.arange(size, dtype=jnp.int32)) % size
    return [lax.dynamic_index_in_dim(stacked, order[k], 0, False) for k in range(size)]


def shards(
    features,
    w_rpn,
    w_anchor,
    pixel_slots,
    sample_slot,
    sample_weight,
    roi_labels,
    w_fc1,
    w_fc2,
    w_class,
):
    rows, width, channels = features.shape[1:]
    nband = lax.axis_size("band")
    band, image = lax.axis_index("band"), lax.axis_index("img")
    core = band % NC
    hid = w_fc2.shape[0]
    half = hid // NC
    labels = lax.all_gather(roi_labels[0], "band", axis=0, tiled=True)

    flat = features.reshape(rows * width, channels)
    capacity = pixel_slots.shape[3]
    wanted = pixel_slots[0, :, 0, :].reshape(nband * capacity)
    sending = flat[wanted].reshape(nband, capacity, channels)
    received = lax.all_to_all(sending, "band", split_axis=0, concat_axis=0, tiled=True)

    rpn_out = rpn(features, w_rpn, w_anchor)
    w_mine = lax.dynamic_slice_in_dim(w_fc1, core * half, half, 1)
    w_theirs = lax.dynamic_slice_in_dim(w_fc1, (1 - core) * half, half, 1)
    w_other = lax.ppermute(w_theirs, "band", CORE_SWAP)
    received, rpn_out, w_other = lax.optimization_barrier((received, rpn_out, w_other))

    received = received.reshape(nband * capacity, channels).astype(F32)
    roi_count, bins = sample_slot.shape[1:3]
    corner_slots = sample_slot[0].reshape(roi_count * bins, 4)
    corner_weights = sample_weight[0].reshape(roi_count * bins, 4)
    slot_ids = jnp.arange(nband * capacity, dtype=jnp.int32)[None, :]
    pooling = jnp.zeros((roi_count * bins, nband * capacity), F32)
    for corner in range(4):
        hits = (corner_slots[:, corner : corner + 1] == slot_ids).astype(F32)
        pooling = pooling + hits * corner_weights[:, corner : corner + 1]
    pooled = jnp.dot(pooling, received, precision=lax.Precision.HIGHEST, preferred_element_type=F32)
    pooled = pooled.astype(BF16).reshape(roi_count, bins, channels)
    x_local = jnp.transpose(pooled, (0, 2, 1)).reshape(roi_count, channels * bins)
    x_cols = lax.all_to_all(x_local, "band", split_axis=1, concat_axis=0, tiled=True)

    x_other = lax.ppermute(x_cols, "band", CORE_SWAP)
    partial = dot(x_cols, w_mine, (1, 0)) + dot(x_other, w_other, (1, 0))
    count = x_cols.shape[0]
    by_y = exchange(partial.astype(BF16).reshape(NY, count // NY, half), Y_GROUPS)
    by_y = jnp.sum(by_y.astype(F32), axis=0).astype(BF16)
    by_z = exchange(by_y.reshape(NZ, count // NY // NZ, half), Z_GROUPS)
    a1_own = jnp.sum(by_z.astype(F32), axis=0).astype(BF16)
    a1_z = exchange(jnp.broadcast_to(a1_own[None], (NZ,) + a1_own.shape), Z_GROUPS)
    a1_z = a1_z.reshape(1, count // NY, half)
    a1_mine = exchange(jnp.broadcast_to(a1_z, (NY,) + a1_z.shape[1:]), Y_GROUPS).reshape(count, half)
    a1_other = lax.ppermute(a1_mine, "band", CORE_SWAP)
    first = core == 0
    a1 = jnp.concatenate(
        [jnp.where(first, a1_mine, a1_other), jnp.where(first, a1_other, a1_mine)], axis=1
    ).astype(F32)

    h1, slope1 = gelu_and_slope(a1)
    a2 = dot(h1, w_fc2, (1, 0))
    h2, slope2 = gelu_and_slope(a2)
    logits = dot(h2, w_class, (1, 0))
    expo = jnp.exp(logits)
    prob = expo / jnp.sum(expo, axis=1, keepdims=True)
    classes = w_class.shape[1]
    onehot = (labels[:, None] == jnp.arange(classes, dtype=jnp.int32)[None, :]).astype(F32)
    dlogits = (prob - onehot).astype(BF16)
    da2 = (dot(dlogits, w_class, (1, 1)) * slope2).astype(BF16)

    nimg = lax.axis_size("img")
    wide = hid // nimg
    h1_mine = lax.dynamic_slice_in_dim(h1, core * half, half, 1)
    h2_mine = lax.dynamic_slice_in_dim(h2, core * half, half, 1)
    part_fc2 = dot(h1_mine, da2, (0, 0)).reshape(half, nimg, wide).transpose(1, 0, 2)
    part_class = jnp.pad(dot(h2_mine, dlogits, (0, 0)), ((0, 0), (0, 128 - classes)))
    part_class = part_class.reshape(nimg, NC, half // nimg // NC, 128).transpose(0, 2, 1, 3)
    part_class = part_class.reshape(nimg, half // nimg // NC, wide)
    total_head = sum_chunks(jnp.concatenate([part_fc2, part_class], axis=1), image)

    da1 = (dot(da2, w_fc2, (1, 1)) * slope1).astype(BF16)
    part_fc1 = dot(x_cols, da1, (0, 0))
    part_fc1 = part_fc1.reshape(-1, nimg, wide).transpose(1, 0, 2)
    total_fc1 = sum_chunks(part_fc1, image)

    heads = spread_chunks(total_head.astype(BF16), image)
    grad_fc1 = jnp.concatenate(spread_chunks(total_fc1.astype(BF16), image), axis=1).astype(F32)
    fc2_mine = jnp.concatenate([chunk[:half] for chunk in heads], axis=1)
    class_mine = jnp.stack([chunk[half:] for chunk in heads])
    class_mine = class_mine.reshape(nimg, half // nimg // NC, NC, 128).transpose(0, 2, 1, 3)
    class_mine = class_mine.reshape(half, 128)
    mine = jnp.concatenate([fc2_mine, class_mine], axis=1)
    other = lax.ppermute(mine, "band", CORE_SWAP)
    whole = jnp.concatenate(
        [jnp.where(first, mine, other), jnp.where(first, other, mine)], axis=0
    ).astype(F32)
    return (rpn_out, grad_fc1, whole[:, :hid], whole[:, hid : hid + classes])


def solution(mesh):
    return jax.shard_map(
        shards,
        mesh=mesh,
        in_specs=(
            P("img", "band", None, None),
            P(),
            P(),
            P("img", None, "band", None),
            P("img", "band", None, None),
            P("img", "band", None, None),
            P("img", "band"),
            P("band", None),
            P(),
            P(),
        ),
        out_specs=(P("img", None, "band", None), P("band", None), P(), P()),
        check_vma=False,
    )
```

```python
import functools

import jax
import jax.numpy as jnp
from jax import lax
from jax.experimental import pallas as pl
from jax.experimental.pallas import tpu as pltpu
from jax.sharding import PartitionSpec as P

NY, NZ, NC = 4, 8, 2
BAND = NY * NZ * NC
F32, BF16 = jnp.float32, jnp.bfloat16
CORE_SWAP = [(b, b ^ 1) for b in range(BAND)]
Z_GROUPS = [[(y * NZ + z) * NC + c for z in range(NZ)] for y in range(NY) for c in range(NC)]
Y_GROUPS = [[(y * NZ + z) * NC + c for y in range(NY)] for z in range(NZ) for c in range(NC)]


def halo(array):
    devices = lax.axis_size("band")
    up = [(i, i + 1) for i in range(devices - 1)]
    down = [(j, i) for i, j in up]
    before = lax.ppermute(array[:, -1:], "band", up)
    after = lax.ppermute(array[:, :1], "band", down)
    return jnp.concatenate([before, array, after], axis=1)


def side_pad(array):
    return jnp.pad(array, ((0, 0), (0, 0), (1, 1), (0, 0)))


def conv_rows(source, w_rpn, count):
    batch = source.shape[0]
    width = source.shape[2] - 2
    channels = source.shape[3]
    total = jnp.zeros((batch * count * width, w_rpn.shape[3]), F32)
    for dy in range(3):
        for dx in range(3):
            window = source[:, dy : dy + count, dx : dx + width, :].reshape(
                batch * count * width, channels
            )
            total = total + jnp.dot(window, w_rpn[dy, dx], preferred_element_type=F32)
    return total


def rpn(features, w_rpn, w_anchor):
    batch, rows, width, channels = features.shape
    conv = conv_rows(side_pad(halo(features)), w_rpn, rows)
    hidden = jnp.maximum(conv, 0.0).astype(BF16)
    anchors = w_anchor.shape[1]
    flat = jnp.dot(hidden, w_anchor, preferred_element_type=F32)
    return jnp.transpose(flat.reshape(batch, rows, width, anchors), (0, 3, 1, 2)).astype(BF16)


def exchange(array, groups):
    return lax.all_to_all(
        array, "band", split_axis=0, concat_axis=0, tiled=True, axis_index_groups=groups
    )


def dot(left, right, contract):
    return lax.dot_general(left, right, ((contract[:1], contract[1:]), ((), ())), preferred_element_type=F32)


def shift_img(array, step):
    size = lax.axis_size("img")
    return lax.ppermute(array, "img", [(i, (i + step) % size) for i in range(size)])


def gelu_parts(value):
    cubic = 0.044715 * (value * value * value)
    tanh = jnp.tanh(0.7978845608028654 * (value + cubic))
    return tanh


def gelu_of(value):
    return 0.5 * value * (1.0 + gelu_parts(value))


def slope_of(value):
    tanh = gelu_parts(value)
    inner = 0.7978845608028654 * (1.0 + 3.0 * 0.044715 * (value * value))
    return 0.5 * (1.0 + tanh) + 0.5 * value * (1.0 - tanh * tanh) * inner


ROW_BLOCK = 128


def join_halves(core, mine_ref, other_ref, whole_ref):
    half = mine_ref.shape[1]
    whole_ref[:, pl.ds(pl.multiple_of(core * half, half), half)] = mine_ref[...]
    whole_ref[:, pl.ds(pl.multiple_of((1 - core) * half, half), half)] = other_ref[...]


def head_kernel(classes, place, mine_ref, other_ref, labels_ref, fc2_ref, class_ref,
                da2_ref, own_ref, s1_ref, s2_ref, s3_ref, a1, h1, h2, dlog):
    core, image = place[0], place[1]
    join_halves(core, mine_ref, other_ref, a1)
    count, hid = a1.shape
    lanes = class_ref.shape[1]

    def block(step, carry):
        rows = pl.ds(pl.multiple_of(step * ROW_BLOCK, ROW_BLOCK), ROW_BLOCK)
        hidden = gelu_of(a1[rows, :].astype(F32)).astype(BF16)
        h1[rows, :] = hidden
        a2 = dot(hidden, fc2_ref[...], (1, 0))
        second = gelu_of(a2).astype(BF16)
        h2[rows, :] = second
        logits = dot(second, class_ref[...], (1, 0))
        column = lax.broadcasted_iota(jnp.int32, (ROW_BLOCK, lanes), 1)
        expo = jnp.where(column < classes, jnp.exp(logits), 0.0)
        prob = expo / jnp.sum(expo, axis=1, keepdims=True)
        onehot = (labels_ref[rows, :] == column).astype(F32)
        dlogits = (prob - onehot).astype(BF16)
        dlog[rows, :] = dlogits
        dh2 = dot(dlogits, class_ref[...], (1, 1))
        da2_ref[rows, :] = (dh2 * slope_of(a2)).astype(BF16)
        return carry

    lax.fori_loop(0, count // ROW_BLOCK, block, 0)
    images = 4
    wide = hid // NC // images
    for step, out in enumerate((own_ref, s1_ref, s2_ref, s3_ref)):
        chunk = lax.rem(image + step, images)
        cols = pl.ds(pl.multiple_of(core * (hid // NC) + chunk * wide, wide), wide)
        out[:, :hid] = dot(h1[:, cols], da2_ref[...], (0, 0)).astype(out.dtype)
        out[:, hid:] = dot(dlog[...], h2[:, cols], (0, 0)).astype(out.dtype)


def vmem_spec(count):
    return [pl.BlockSpec(memory_space=pltpu.VMEM)] * count


SMEM_SPEC = pl.BlockSpec(memory_space=pltpu.SMEM)


def head(place, mine, other, labels, w_fc2, w_class, classes):
    count, half = mine.shape
    hid = w_fc2.shape[0]
    lanes = w_class.shape[1]
    wide = half // 4
    struct = jax.ShapeDtypeStruct
    return pl.pallas_call(
        functools.partial(head_kernel, classes),
        out_shape=[struct((count, hid), BF16), struct((wide, hid + lanes), F32)]
        + [struct((wide, hid + lanes), BF16)] * 3,
        in_specs=[SMEM_SPEC] + vmem_spec(5),
        out_specs=vmem_spec(5),
        scratch_shapes=[
            pltpu.VMEM((count, hid), BF16),
            pltpu.VMEM((count, hid), BF16),
            pltpu.VMEM((count, hid), BF16),
            pltpu.VMEM((count, lanes), BF16),
        ],
        compiler_params=pltpu.CompilerParams(vmem_limit_bytes=40 * 2**20),
        name="head",
    )(place, mine, other, labels, w_fc2, w_class)


def first_kernel(place, mine_ref, other_ref, da2_ref, fc2_ref, x_ref,
                 own_ref, s1_ref, s2_ref, s3_ref, a1, da1):
    core, image = place[0], place[1]
    join_halves(core, mine_ref, other_ref, a1)
    count, hid = a1.shape

    def block(step, carry):
        rows = pl.ds(pl.multiple_of(step * ROW_BLOCK, ROW_BLOCK), ROW_BLOCK)
        dh1 = dot(da2_ref[rows, :], fc2_ref[...], (1, 1))
        da1[rows, :] = (dh1 * slope_of(a1[rows, :].astype(F32))).astype(BF16)
        return carry

    lax.fori_loop(0, count // ROW_BLOCK, block, 0)
    images = 4
    wide = hid // images
    for step, out in enumerate((own_ref, s1_ref, s2_ref, s3_ref)):
        chunk = lax.rem(image + step, images)
        cols = pl.ds(pl.multiple_of(chunk * wide, wide), wide)
        out[...] = dot(x_ref[...], da1[:, cols], (0, 0)).astype(out.dtype)


def first_layer(place, mine, other, da2, w_fc2, x_cols):
    count, hid = da2.shape
    depth = x_cols.shape[1]
    wide = hid // 4
    struct = jax.ShapeDtypeStruct
    return pl.pallas_call(
        first_kernel,
        out_shape=[struct((depth, wide), F32)] + [struct((depth, wide), BF16)] * 3,
        in_specs=[SMEM_SPEC] + vmem_spec(5),
        out_specs=vmem_spec(4),
        scratch_shapes=[pltpu.VMEM((count, hid), BF16), pltpu.VMEM((count, hid), BF16)],
        compiler_params=pltpu.CompilerParams(vmem_limit_bytes=40 * 2**20),
        name="first_layer",
    )(place, mine, other, da2, w_fc2, x_cols)


def assemble_kernel(depth, place, *refs):
    core, image = place[0], place[1]
    mine, other, first = refs[:4], refs[4:8], refs[8:12]
    fc1_ref, fc2_ref, class_ref = refs[12:]
    hid = fc2_ref.shape[1]
    images = 4
    classes = class_ref.shape[0]
    tall = mine[0].shape[0]
    for step in range(images):
        chunk = lax.rem(image + images - step, images)
        for side, ref in ((core, mine[step]), (1 - core, other[step])):
            at = pl.ds(pl.multiple_of(side * (hid // NC) + chunk * tall, tall), tall)
            fc2_ref[at, :] = ref[:, :hid].astype(F32)
            class_ref[:, at] = ref[:classes, hid:].astype(F32)
        wide = hid // images
        cols = pl.ds(pl.multiple_of(chunk * wide, wide), wide)
        fc1_ref[:, cols] = first[step][...].astype(F32)


def assemble(place, mine, other, first, classes):
    hid = mine[0].shape[1] - 128
    depth = first[0].shape[0]
    struct = jax.ShapeDtypeStruct
    return pl.pallas_call(
        functools.partial(assemble_kernel, depth),
        out_shape=[struct((depth, hid), F32), struct((hid, hid), F32), struct((classes, hid), F32)],
        in_specs=[SMEM_SPEC] + vmem_spec(12),
        out_specs=vmem_spec(3),
        compiler_params=pltpu.CompilerParams(vmem_limit_bytes=40 * 2**20),
        name="assemble",
    )(place, *mine, *other, *first)


def sum_img(own, sent):
    total = own
    for step, part in enumerate(sent, 1):
        total = total + shift_img(part, step).astype(F32)
    return total.astype(BF16)


def spread_img(chunk):
    return [chunk] + [shift_img(chunk, step) for step in range(1, lax.axis_size("img"))]


def shards(
    features,
    w_rpn,
    w_anchor,
    pixel_slots,
    sample_slot,
    sample_weight,
    roi_labels,
    w_fc1,
    w_fc2,
    w_class,
):
    rows, width, channels = features.shape[1:]
    nband = lax.axis_size("band")
    band, image = lax.axis_index("band"), lax.axis_index("img")
    core = band % NC
    hid = w_fc2.shape[0]
    half = hid // NC
    place = jnp.stack([core, image]).astype(jnp.int32)

    flat = features.reshape(rows * width, channels)
    capacity = pixel_slots.shape[3]
    wanted = pixel_slots[0, :, 0, :].reshape(nband * capacity)
    sending = flat[wanted].reshape(nband, capacity, channels)
    received = lax.all_to_all(sending, "band", split_axis=0, concat_axis=0, tiled=True)

    rpn_out = rpn(features, w_rpn, w_anchor)
    w_mine = lax.dynamic_slice_in_dim(w_fc1, core * half, half, 1)
    w_theirs = lax.dynamic_slice_in_dim(w_fc1, (1 - core) * half, half, 1)
    w_other = lax.ppermute(w_theirs, "band", CORE_SWAP)
    received, rpn_out, w_other = lax.optimization_barrier((received, rpn_out, w_other))

    received = received.reshape(nband * capacity, channels).astype(F32)
    roi_count, bins = sample_slot.shape[1:3]
    corner_slots = sample_slot[0].reshape(roi_count * bins, 4)
    corner_weights = sample_weight[0].reshape(roi_count * bins, 4)
    slot_ids = jnp.arange(nband * capacity, dtype=jnp.int32)[None, :]
    pooling = jnp.zeros((roi_count * bins, nband * capacity), F32)
    for corner in range(4):
        hits = (corner_slots[:, corner : corner + 1] == slot_ids).astype(F32)
        pooling = pooling + hits * corner_weights[:, corner : corner + 1]
    pooled = jnp.dot(pooling, received, precision=lax.Precision.HIGHEST, preferred_element_type=F32)
    pooled = pooled.astype(BF16).reshape(roi_count, bins, channels)
    depth = w_fc1.shape[0]
    x_local = jnp.transpose(pooled, (0, 2, 1)).reshape(roi_count, nband, depth)
    label_column = jnp.broadcast_to(roi_labels[0].astype(BF16)[:, None, None], (roi_count, nband, 1))
    x_local = jnp.concatenate([x_local, label_column], axis=2).reshape(roi_count, nband * (depth + 1))
    x_cols = lax.all_to_all(x_local, "band", split_axis=1, concat_axis=0, tiled=True)
    labels = x_cols[:, depth:].astype(jnp.int32)
    x_cols = x_cols[:, :depth]

    x_other = lax.ppermute(x_cols, "band", CORE_SWAP)
    partial = dot(x_cols, w_mine, (1, 0)) + dot(x_other, w_other, (1, 0))
    count = x_cols.shape[0]
    by_y = exchange(partial.astype(BF16).reshape(NY, count // NY, half), Y_GROUPS)
    by_y = jnp.sum(by_y.astype(F32), axis=0).astype(BF16)
    by_z = exchange(by_y.reshape(NZ, count // NY // NZ, half), Z_GROUPS)
    a1_own = jnp.sum(by_z.astype(F32), axis=0).astype(BF16)
    a1_z = exchange(jnp.broadcast_to(a1_own[None], (NZ,) + a1_own.shape), Z_GROUPS)
    a1_z = a1_z.reshape(1, count // NY, half)
    a1_mine = exchange(jnp.broadcast_to(a1_z, (NY,) + a1_z.shape[1:]), Y_GROUPS).reshape(count, half)
    a1_other = lax.ppermute(a1_mine, "band", CORE_SWAP)
    classes = w_class.shape[1]
    class_wide = jnp.pad(w_class, ((0, 0), (0, 128 - classes)))
    da2, *parts = head(place, a1_mine, a1_other, labels, w_fc2, class_wide, classes)
    total_head = sum_img(parts[0], parts[1:])
    parts = first_layer(place, a1_mine, a1_other, da2, w_fc2, x_cols)
    total_fc1 = sum_img(parts[0], parts[1:])
    mine = spread_img(total_head)
    other = [lax.ppermute(part, "band", CORE_SWAP) for part in mine]
    fc1 = spread_img(total_fc1)
    grad_fc1, grad_fc2, grad_class = assemble(place, mine, other, fc1, classes)
    return (rpn_out, grad_fc1, grad_fc2, grad_class.T)


def solution(mesh):
    return jax.shard_map(
        shards,
        mesh=mesh,
        in_specs=(
            P("img", "band", None, None),
            P(),
            P(),
            P("img", None, "band", None),
            P("img", "band", None, None),
            P("img", "band", None, None),
            P("img", "band"),
            P("band", None),
            P(),
            P(),
        ),
        out_specs=(P("img", None, "band", None), P("band", None), P(), P()),
        check_vma=False,
    )
```

```python
import functools

import jax
import jax.numpy as jnp
from jax import lax
from jax.experimental import pallas as pl
from jax.experimental.pallas import tpu as pltpu
from jax.sharding import PartitionSpec as P

NY, NZ, NC = 4, 8, 2
BAND = NY * NZ * NC
F32, BF16 = jnp.float32, jnp.bfloat16
CORE_SWAP = [(b, b ^ 1) for b in range(BAND)]
Z_GROUPS = [[(y * NZ + z) * NC + c for z in range(NZ)] for y in range(NY) for c in range(NC)]
Y_GROUPS = [[(y * NZ + z) * NC + c for y in range(NY)] for z in range(NZ) for c in range(NC)]


def halo(array):
    devices = lax.axis_size("band")
    up = [(i, i + 1) for i in range(devices - 1)]
    down = [(j, i) for i, j in up]
    before = lax.ppermute(array[0, -1:], "band", up)
    after = lax.ppermute(array[0, :1], "band", down)
    return before, after


def rpn_kernel(before_ref, feat_ref, after_ref, rpn_ref, anchor_ref, out_ref, rows, held):
    count = feat_ref.shape[0]
    width = feat_ref.shape[1]
    rows[0] = before_ref[0]
    rows[pl.ds(1, count)] = feat_ref[...]
    rows[count + 1] = after_ref[0]

    def line(y, carry):
        sides = []
        for dx in range(3):
            total = dot(rows[y], rpn_ref[0, dx], (1, 0))
            total = total + dot(rows[y + 1], rpn_ref[1, dx], (1, 0))
            sides.append(total + dot(rows[y + 2], rpn_ref[2, dx], (1, 0)))
        place = lax.broadcasted_iota(jnp.int32, sides[0].shape, 0)
        left = jnp.where(place == 0, 0.0, pltpu.roll(sides[0], 1, 0))
        right = jnp.where(place == width - 1, 0.0, pltpu.roll(sides[2], width - 1, 0))
        hidden = jnp.maximum(left + sides[1] + right, 0.0).astype(BF16)
        held[y] = dot(anchor_ref[...], hidden, (1, 1))
        return carry

    lax.fori_loop(0, count, line, 0)
    for y in range(count):
        for a in range(out_ref.shape[0]):
            out_ref[a, y : y + 1, :] = held[y, a : a + 1, :].astype(BF16)


def rpn(before, features, after, w_rpn, w_anchor):
    rows, width, channels = features.shape[1:]
    anchors = w_anchor.shape[1]
    out = pl.pallas_call(
        rpn_kernel,
        out_shape=jax.ShapeDtypeStruct((anchors, rows, width), BF16),
        in_specs=vmem_spec(5),
        out_specs=pl.BlockSpec(memory_space=pltpu.VMEM),
        scratch_shapes=[
            pltpu.VMEM((rows + 2, width, channels), BF16),
            pltpu.VMEM((rows, anchors, width), F32),
        ],
        compiler_params=pltpu.CompilerParams(vmem_limit_bytes=40 * 2**20),
        cost_estimate=pl.CostEstimate(flops=9 * 10**9, bytes_accessed=4 * 10**6, transcendentals=0),
        name="rpn",
    )(before, features[0], after, w_rpn, w_anchor.T)
    return out[None]


def vmem_spec(count):
    return [pl.BlockSpec(memory_space=pltpu.VMEM)] * count


SMEM_SPEC = pl.BlockSpec(memory_space=pltpu.SMEM)


def exchange(array, groups):
    return lax.all_to_all(
        array, "band", split_axis=0, concat_axis=0, tiled=True, axis_index_groups=groups
    )


def dot(left, right, contract):
    return lax.dot_general(left, right, ((contract[:1], contract[1:]), ((), ())), preferred_element_type=F32)


def shift_img(array, step):
    size = lax.axis_size("img")
    return lax.ppermute(array, "img", [(i, (i + step) % size) for i in range(size)])


def gelu_parts(value):
    cubic = 0.044715 * (value * value * value)
    tanh = jnp.tanh(0.7978845608028654 * (value + cubic))
    return tanh


def gelu_of(value):
    return 0.5 * value * (1.0 + gelu_parts(value))


def slope_of(value):
    tanh = gelu_parts(value)
    inner = 0.7978845608028654 * (1.0 + 3.0 * 0.044715 * (value * value))
    return 0.5 * (1.0 + tanh) + 0.5 * value * (1.0 - tanh * tanh) * inner


ROW_BLOCK = 128


def join_halves(core, mine_ref, other_ref, whole_ref):
    half = mine_ref.shape[1]
    whole_ref[:, pl.ds(pl.multiple_of(core * half, half), half)] = mine_ref[...]
    whole_ref[:, pl.ds(pl.multiple_of((1 - core) * half, half), half)] = other_ref[...]


def head_kernel(classes, place, mine_ref, other_ref, labels_ref, fc2_ref, class_ref,
                da2_ref, own_ref, s1_ref, s2_ref, s3_ref, a1, h1, h2, dlog):
    core, image = place[0], place[1]
    join_halves(core, mine_ref, other_ref, a1)
    count, hid = a1.shape
    lanes = class_ref.shape[1]

    def block(step, carry):
        rows = pl.ds(pl.multiple_of(step * ROW_BLOCK, ROW_BLOCK), ROW_BLOCK)
        hidden = gelu_of(a1[rows, :].astype(F32)).astype(BF16)
        h1[rows, :] = hidden
        a2 = dot(hidden, fc2_ref[...], (1, 0))
        second = gelu_of(a2).astype(BF16)
        h2[rows, :] = second
        logits = dot(second, class_ref[...], (1, 0))
        column = lax.broadcasted_iota(jnp.int32, (ROW_BLOCK, lanes), 1)
        expo = jnp.where(column < classes, jnp.exp(logits), 0.0)
        prob = expo / jnp.sum(expo, axis=1, keepdims=True)
        onehot = (labels_ref[rows, :] == column).astype(F32)
        dlogits = (prob - onehot).astype(BF16)
        dlog[rows, :] = dlogits
        dh2 = dot(dlogits, class_ref[...], (1, 1))
        da2_ref[rows, :] = (dh2 * slope_of(a2)).astype(BF16)
        return carry

    lax.fori_loop(0, count // ROW_BLOCK, block, 0)
    images = 4
    wide = hid // NC // images
    for step, out in enumerate((own_ref, s1_ref, s2_ref, s3_ref)):
        chunk = lax.rem(image + step, images)
        cols = pl.ds(pl.multiple_of(core * (hid // NC) + chunk * wide, wide), wide)
        out[:, :hid] = dot(h1[:, cols], da2_ref[...], (0, 0)).astype(out.dtype)
        out[:, hid:] = dot(dlog[...], h2[:, cols], (0, 0)).astype(out.dtype)


def head(place, mine, other, labels, w_fc2, w_class, classes):
    count, half = mine.shape
    hid = w_fc2.shape[0]
    lanes = w_class.shape[1]
    wide = half // 4
    struct = jax.ShapeDtypeStruct
    return pl.pallas_call(
        functools.partial(head_kernel, classes),
        out_shape=[struct((count, hid), BF16), struct((wide, hid + lanes), F32)]
        + [struct((wide, hid + lanes), BF16)] * 3,
        in_specs=[SMEM_SPEC] + vmem_spec(5),
        out_specs=vmem_spec(5),
        scratch_shapes=[
            pltpu.VMEM((count, hid), BF16),
            pltpu.VMEM((count, hid), BF16),
            pltpu.VMEM((count, hid), BF16),
            pltpu.VMEM((count, lanes), BF16),
        ],
        compiler_params=pltpu.CompilerParams(vmem_limit_bytes=40 * 2**20),
        name="head",
    )(place, mine, other, labels, w_fc2, w_class)


def first_kernel(place, mine_ref, other_ref, da2_ref, fc2_ref, x_ref,
                 own_ref, s1_ref, s2_ref, s3_ref, a1, da1):
    core, image = place[0], place[1]
    join_halves(core, mine_ref, other_ref, a1)
    count, hid = a1.shape

    def block(step, carry):
        rows = pl.ds(pl.multiple_of(step * ROW_BLOCK, ROW_BLOCK), ROW_BLOCK)
        dh1 = dot(da2_ref[rows, :], fc2_ref[...], (1, 1))
        da1[rows, :] = (dh1 * slope_of(a1[rows, :].astype(F32))).astype(BF16)
        return carry

    lax.fori_loop(0, count // ROW_BLOCK, block, 0)
    images = 4
    wide = hid // images
    for step, out in enumerate((own_ref, s1_ref, s2_ref, s3_ref)):
        chunk = lax.rem(image + step, images)
        cols = pl.ds(pl.multiple_of(chunk * wide, wide), wide)
        out[...] = dot(x_ref[...], da1[:, cols], (0, 0)).astype(out.dtype)


def first_layer(place, mine, other, da2, w_fc2, x_cols):
    count, hid = da2.shape
    depth = x_cols.shape[1]
    wide = hid // 4
    struct = jax.ShapeDtypeStruct
    return pl.pallas_call(
        first_kernel,
        out_shape=[struct((depth, wide), F32)] + [struct((depth, wide), BF16)] * 3,
        in_specs=[SMEM_SPEC] + vmem_spec(5),
        out_specs=vmem_spec(4),
        scratch_shapes=[pltpu.VMEM((count, hid), BF16), pltpu.VMEM((count, hid), BF16)],
        compiler_params=pltpu.CompilerParams(vmem_limit_bytes=40 * 2**20),
        name="first_layer",
    )(place, mine, other, da2, w_fc2, x_cols)


SUM_ROWS = 192


def sum_kernel(*refs):
    heads, firsts, out_ref = refs[:4], refs[4:8], refs[8]
    tall, wide = heads[0].shape
    total = heads[0][...]
    for ref in heads[1:]:
        total = total + ref[...].astype(F32)
    out_ref[:tall, :] = total.astype(BF16)
    first = firsts[0][...]
    for ref in firsts[1:]:
        first = first + ref[...].astype(F32)
    depth, cols = first.shape
    quarter = depth // 4
    rest = jnp.zeros((SUM_ROWS - tall, wide), BF16)
    out_ref[tall:, :] = rest
    for q in range(4):
        part = first[q * quarter : (q + 1) * quarter].astype(BF16)
        out_ref[tall : tall + quarter, q * cols : (q + 1) * cols] = part


def sum_parts(heads, firsts):
    wide = heads[0].shape[1]
    return pl.pallas_call(
        sum_kernel,
        out_shape=jax.ShapeDtypeStruct((SUM_ROWS, wide), BF16),
        in_specs=vmem_spec(8),
        out_specs=pl.BlockSpec(memory_space=pltpu.VMEM),
        compiler_params=pltpu.CompilerParams(vmem_limit_bytes=40 * 2**20),
        name="sum_parts",
    )(*heads, *firsts)


def assemble_kernel(place, *refs):
    core, image = place[0], place[1]
    mine, other = refs[:4], refs[4:8]
    fc1_ref, fc2_ref, class_ref = refs[8:]
    hid = fc2_ref.shape[1]
    images = 4
    classes = class_ref.shape[0]
    tall = other[0].shape[0]
    depth = fc1_ref.shape[0]
    quarter = depth // 4
    wide = hid // images
    for step in range(images):
        chunk = lax.rem(image + images - step, images)
        for side, ref in ((core, mine[step]), (1 - core, other[step])):
            at = pl.ds(pl.multiple_of(side * (hid // NC) + chunk * tall, tall), tall)
            fc2_ref[at, :] = ref[:tall, :hid].astype(F32)
            class_ref[:, at] = ref[:classes, hid:].astype(F32)
        cols = pl.ds(pl.multiple_of(chunk * wide, wide), wide)
        for q in range(4):
            part = mine[step][tall : tall + quarter, q * wide : (q + 1) * wide]
            fc1_ref[q * quarter : (q + 1) * quarter, cols] = part.astype(F32)


def assemble(place, mine, other, depth, classes):
    hid = mine[0].shape[1] - 128
    struct = jax.ShapeDtypeStruct
    return pl.pallas_call(
        assemble_kernel,
        out_shape=[struct((depth, hid), F32), struct((hid, hid), F32), struct((classes, hid), F32)],
        in_specs=[SMEM_SPEC] + vmem_spec(8),
        out_specs=vmem_spec(3),
        compiler_params=pltpu.CompilerParams(vmem_limit_bytes=40 * 2**20),
        name="assemble",
    )(place, *mine, *other)


def shift_all(sent):
    return [shift_img(part, step) for step, part in enumerate(sent, 1)]


def shards(
    features,
    w_rpn,
    w_anchor,
    pixel_slots,
    sample_slot,
    sample_weight,
    roi_labels,
    w_fc1,
    w_fc2,
    w_class,
):
    rows, width, channels = features.shape[1:]
    nband = lax.axis_size("band")
    band, image = lax.axis_index("band"), lax.axis_index("img")
    core = band % NC
    hid = w_fc2.shape[0]
    half = hid // NC
    place = jnp.stack([core, image]).astype(jnp.int32)

    flat = features.reshape(rows * width, channels)
    capacity = pixel_slots.shape[3]
    wanted = pixel_slots[0, :, 0, :].reshape(nband * capacity)
    sending = flat[wanted].reshape(nband, capacity, channels)
    received = lax.all_to_all(sending, "band", split_axis=0, concat_axis=0, tiled=True)

    edges, w_first = lax.optimization_barrier((features, w_fc1, sending))[:2]
    before, after = halo(edges)
    rpn_out = rpn(before, features, after, w_rpn, w_anchor)
    w_mine = lax.dynamic_slice_in_dim(w_first, core * half, half, 1)
    w_theirs = lax.dynamic_slice_in_dim(w_first, (1 - core) * half, half, 1)
    w_other = lax.ppermute(w_theirs, "band", CORE_SWAP)
    received, rpn_out, w_other = lax.optimization_barrier((received, rpn_out, w_other))

    received = received.reshape(nband * capacity, channels).astype(F32)
    roi_count, bins = sample_slot.shape[1:3]
    corner_slots = sample_slot[0].reshape(roi_count * bins, 4)
    corner_weights = sample_weight[0].reshape(roi_count * bins, 4)
    slot_ids = jnp.arange(nband * capacity, dtype=jnp.int32)[None, :]
    pooling = jnp.zeros((roi_count * bins, nband * capacity), F32)
    for corner in range(4):
        hits = (corner_slots[:, corner : corner + 1] == slot_ids).astype(F32)
        pooling = pooling + hits * corner_weights[:, corner : corner + 1]
    pooled = jnp.dot(pooling, received, precision=lax.Precision.HIGHEST, preferred_element_type=F32)
    pooled = pooled.astype(BF16).reshape(roi_count, bins, channels)
    depth = w_fc1.shape[0]
    x_local = jnp.transpose(pooled, (0, 2, 1)).reshape(roi_count, nband, depth)
    label_column = jnp.broadcast_to(roi_labels[0].astype(BF16)[:, None, None], (roi_count, nband, 1))
    x_local = jnp.concatenate([x_local, label_column], axis=2).reshape(roi_count, nband * (depth + 1))
    x_cols = lax.all_to_all(x_local, "band", split_axis=1, concat_axis=0, tiled=True)
    labels = x_cols[:, depth:].astype(jnp.int32)
    x_cols = x_cols[:, :depth]

    x_other = lax.ppermute(x_cols, "band", CORE_SWAP)
    partial = dot(x_cols, w_mine, (1, 0)) + dot(x_other, w_other, (1, 0))
    count = x_cols.shape[0]
    by_y = exchange(partial.astype(BF16).reshape(NY, count // NY, half), Y_GROUPS)
    by_y = jnp.sum(by_y.astype(F32), axis=0).astype(BF16)
    by_z = exchange(by_y.reshape(NZ, count // NY // NZ, half), Z_GROUPS)
    a1_own = jnp.sum(by_z.astype(F32), axis=0).astype(BF16)
    a1_z = exchange(jnp.broadcast_to(a1_own[None], (NZ,) + a1_own.shape), Z_GROUPS)
    a1_z = a1_z.reshape(1, count // NY, half)
    a1_mine = exchange(jnp.broadcast_to(a1_z, (NY,) + a1_z.shape[1:]), Y_GROUPS).reshape(count, half)
    a1_other = lax.ppermute(a1_mine, "band", CORE_SWAP)
    classes = w_class.shape[1]
    class_wide = jnp.pad(w_class, ((0, 0), (0, 128 - classes)))
    da2, *parts = head(place, a1_mine, a1_other, labels, w_fc2, class_wide, classes)
    head_own, head_got = parts[0], shift_all(parts[1:])
    parts = first_layer(place, a1_mine, a1_other, da2, w_fc2, x_cols)
    total = sum_parts([head_own] + head_got, [parts[0]] + shift_all(parts[1:]))
    mine = [total] + [shift_img(total, step) for step in range(1, 4)]
    tall = head_own.shape[0]
    other = [lax.ppermute(part[:tall], "band", CORE_SWAP) for part in mine]
    grad_fc1, grad_fc2, grad_class = assemble(place, mine, other, depth, classes)
    return (rpn_out, grad_fc1, grad_fc2, grad_class.T)


def solution(mesh):
    return jax.shard_map(
        shards,
        mesh=mesh,
        in_specs=(
            P("img", "band", None, None),
            P(),
            P(),
            P("img", None, "band", None),
            P("img", "band", None, None),
            P("img", "band", None, None),
            P("img", "band"),
            P("band", None),
            P(),
            P(),
        ),
        out_specs=(P("img", None, "band", None), P("band", None), P(), P()),
        check_vma=False,
    )
```

```python
import functools

import jax
import jax.numpy as jnp
from jax import lax
from jax.experimental import pallas as pl
from jax.experimental.pallas import tpu as pltpu
from jax.sharding import PartitionSpec as P

NY, NZ, NC = 4, 8, 2
BAND = NY * NZ * NC
F32, BF16 = jnp.float32, jnp.bfloat16
CORE_SWAP = [(b, b ^ 1) for b in range(BAND)]
Z_GROUPS = [[(y * NZ + z) * NC + c for z in range(NZ)] for y in range(NY) for c in range(NC)]
Y_GROUPS = [[(y * NZ + z) * NC + c for y in range(NY)] for z in range(NZ) for c in range(NC)]


def halo(array):
    devices = lax.axis_size("band")
    up = [(i, i + 1) for i in range(devices - 1)]
    down = [(j, i) for i, j in up]
    before = lax.ppermute(array[0, -1:], "band", up)
    after = lax.ppermute(array[0, :1], "band", down)
    return before, after


def rpn_kernel(before_ref, feat_ref, after_ref, rpn_ref, anchor_ref, out_ref, rows, held):
    count = feat_ref.shape[0]
    width = feat_ref.shape[1]
    rows[0] = before_ref[0]
    rows[pl.ds(1, count)] = feat_ref[...]
    rows[count + 1] = after_ref[0]

    def line(y, carry):
        sides = []
        for dx in range(3):
            total = dot(rows[y], rpn_ref[0, dx], (1, 0))
            total = total + dot(rows[y + 1], rpn_ref[1, dx], (1, 0))
            sides.append(total + dot(rows[y + 2], rpn_ref[2, dx], (1, 0)))
        place = lax.broadcasted_iota(jnp.int32, sides[0].shape, 0)
        left = jnp.where(place == 0, 0.0, pltpu.roll(sides[0], 1, 0))
        right = jnp.where(place == width - 1, 0.0, pltpu.roll(sides[2], width - 1, 0))
        hidden = jnp.maximum(left + sides[1] + right, 0.0).astype(BF16)
        held[y] = dot(anchor_ref[...], hidden, (1, 1))
        return carry

    lax.fori_loop(0, count, line, 0)
    for y in range(count):
        for a in range(out_ref.shape[0]):
            out_ref[a, y : y + 1, :] = held[y, a : a + 1, :].astype(BF16)


def rpn(before, features, after, w_rpn, w_anchor):
    rows, width, channels = features.shape[1:]
    anchors = w_anchor.shape[1]
    out = pl.pallas_call(
        rpn_kernel,
        out_shape=jax.ShapeDtypeStruct((anchors, rows, width), BF16),
        in_specs=vmem_spec(5),
        out_specs=pl.BlockSpec(memory_space=pltpu.VMEM),
        scratch_shapes=[
            pltpu.VMEM((rows + 2, width, channels), BF16),
            pltpu.VMEM((rows, anchors, width), F32),
        ],
        compiler_params=pltpu.CompilerParams(vmem_limit_bytes=40 * 2**20),
        cost_estimate=pl.CostEstimate(flops=9 * 10**9, bytes_accessed=4 * 10**6, transcendentals=0),
        name="rpn",
    )(before, features[0], after, w_rpn, w_anchor.T)
    return out[None]


def vmem_spec(count):
    return [pl.BlockSpec(memory_space=pltpu.VMEM)] * count


SMEM_SPEC = pl.BlockSpec(memory_space=pltpu.SMEM)


def exchange(array, groups):
    return lax.all_to_all(
        array, "band", split_axis=0, concat_axis=0, tiled=True, axis_index_groups=groups
    )


def dot(left, right, contract):
    return lax.dot_general(left, right, ((contract[:1], contract[1:]), ((), ())), preferred_element_type=F32)


def shift_img(array, step):
    size = lax.axis_size("img")
    return lax.ppermute(array, "img", [(i, (i + step) % size) for i in range(size)])


def gelu_parts(value):
    cubic = 0.044715 * (value * value * value)
    tanh = jnp.tanh(0.7978845608028654 * (value + cubic))
    return tanh


def gelu_of(value):
    return 0.5 * value * (1.0 + gelu_parts(value))


def slope_of(value):
    tanh = gelu_parts(value)
    inner = 0.7978845608028654 * (1.0 + 3.0 * 0.044715 * (value * value))
    return 0.5 * (1.0 + tanh) + 0.5 * value * (1.0 - tanh * tanh) * inner


ROW_BLOCK = 128


def join_halves(core, mine_ref, other_ref, whole_ref):
    half = mine_ref.shape[1]
    whole_ref[:, pl.ds(pl.multiple_of(core * half, half), half)] = mine_ref[...]
    whole_ref[:, pl.ds(pl.multiple_of((1 - core) * half, half), half)] = other_ref[...]


def head_kernel(classes, place, mine_ref, other_ref, labels_ref, fc2_ref, class_ref,
                da2_ref, own_ref, s1_ref, s2_ref, s3_ref, a1, h1, h2, dlog):
    core, image = place[0], place[1]
    join_halves(core, mine_ref, other_ref, a1)
    count, hid = a1.shape
    lanes = class_ref.shape[1]

    def block(step, carry):
        rows = pl.ds(pl.multiple_of(step * ROW_BLOCK, ROW_BLOCK), ROW_BLOCK)
        hidden = gelu_of(a1[rows, :].astype(F32)).astype(BF16)
        h1[rows, :] = hidden
        a2 = dot(hidden, fc2_ref[...], (1, 0))
        second = gelu_of(a2).astype(BF16)
        h2[rows, :] = second
        logits = dot(second, class_ref[...], (1, 0))
        column = lax.broadcasted_iota(jnp.int32, (ROW_BLOCK, lanes), 1)
        expo = jnp.where(column < classes, jnp.exp(logits), 0.0)
        prob = expo / jnp.sum(expo, axis=1, keepdims=True)
        onehot = (labels_ref[rows, :] == column).astype(F32)
        dlogits = (prob - onehot).astype(BF16)
        dlog[rows, :] = dlogits
        dh2 = dot(dlogits, class_ref[...], (1, 1))
        da2_ref[rows, :] = (dh2 * slope_of(a2)).astype(BF16)
        return carry

    lax.fori_loop(0, count // ROW_BLOCK, block, 0)
    images = 4
    wide = hid // NC // images
    for step, out in enumerate((own_ref, s1_ref, s2_ref, s3_ref)):
        chunk = lax.rem(image + step, images)
        cols = pl.ds(pl.multiple_of(core * (hid // NC) + chunk * wide, wide), wide)
        out[:, :hid] = dot(h1[:, cols], da2_ref[...], (0, 0)).astype(out.dtype)
        out[:, hid:] = dot(dlog[...], h2[:, cols], (0, 0)).astype(out.dtype)


def head(place, mine, other, labels, w_fc2, w_class, classes):
    count, half = mine.shape
    hid = w_fc2.shape[0]
    lanes = w_class.shape[1]
    wide = half // 4
    struct = jax.ShapeDtypeStruct
    return pl.pallas_call(
        functools.partial(head_kernel, classes),
        out_shape=[struct((count, hid), BF16), struct((wide, hid + lanes), F32)]
        + [struct((wide, hid + lanes), BF16)] * 3,
        in_specs=[SMEM_SPEC] + vmem_spec(5),
        out_specs=vmem_spec(5),
        scratch_shapes=[
            pltpu.VMEM((count, hid), BF16),
            pltpu.VMEM((count, hid), BF16),
            pltpu.VMEM((count, hid), BF16),
            pltpu.VMEM((count, lanes), BF16),
        ],
        compiler_params=pltpu.CompilerParams(vmem_limit_bytes=40 * 2**20),
        name="head",
    )(place, mine, other, labels, w_fc2, w_class)


def first_kernel(place, mine_ref, other_ref, da2_ref, fc2_ref, x_ref,
                 own_ref, s1_ref, s2_ref, s3_ref, a1, da1):
    core, image = place[0], place[1]
    join_halves(core, mine_ref, other_ref, a1)
    count, hid = a1.shape

    def block(step, carry):
        rows = pl.ds(pl.multiple_of(step * ROW_BLOCK, ROW_BLOCK), ROW_BLOCK)
        dh1 = dot(da2_ref[rows, :], fc2_ref[...], (1, 1))
        da1[rows, :] = (dh1 * slope_of(a1[rows, :].astype(F32))).astype(BF16)
        return carry

    lax.fori_loop(0, count // ROW_BLOCK, block, 0)
    images = 4
    wide = hid // images
    for step, out in enumerate((own_ref, s1_ref, s2_ref, s3_ref)):
        chunk = lax.rem(image + step, images)
        cols = pl.ds(pl.multiple_of(chunk * wide, wide), wide)
        out[...] = dot(x_ref[...], da1[:, cols], (0, 0)).astype(out.dtype)


def first_layer(place, mine, other, da2, w_fc2, x_cols):
    count, hid = da2.shape
    depth = x_cols.shape[1]
    wide = hid // 4
    struct = jax.ShapeDtypeStruct
    return pl.pallas_call(
        first_kernel,
        out_shape=[struct((depth, wide), F32)] + [struct((depth, wide), BF16)] * 3,
        in_specs=[SMEM_SPEC] + vmem_spec(5),
        out_specs=vmem_spec(4),
        scratch_shapes=[pltpu.VMEM((count, hid), BF16), pltpu.VMEM((count, hid), BF16)],
        compiler_params=pltpu.CompilerParams(vmem_limit_bytes=40 * 2**20),
        name="first_layer",
    )(place, mine, other, da2, w_fc2, x_cols)


SUM_ROWS = 192


def sum_kernel(*refs):
    heads, firsts, out_ref = refs[:4], refs[4:8], refs[8]
    tall, wide = heads[0].shape
    total = heads[0][...]
    for ref in heads[1:]:
        total = total + ref[...].astype(F32)
    out_ref[:tall, :] = total.astype(BF16)
    first = firsts[0][...]
    for ref in firsts[1:]:
        first = first + ref[...].astype(F32)
    depth, cols = first.shape
    quarter = depth // 4
    rest = jnp.zeros((SUM_ROWS - tall, wide), BF16)
    out_ref[tall:, :] = rest
    for q in range(4):
        part = first[q * quarter : (q + 1) * quarter].astype(BF16)
        out_ref[tall : tall + quarter, q * cols : (q + 1) * cols] = part


def sum_parts(heads, firsts):
    wide = heads[0].shape[1]
    return pl.pallas_call(
        sum_kernel,
        out_shape=jax.ShapeDtypeStruct((SUM_ROWS, wide), BF16),
        in_specs=vmem_spec(8),
        out_specs=pl.BlockSpec(memory_space=pltpu.VMEM),
        compiler_params=pltpu.CompilerParams(vmem_limit_bytes=40 * 2**20),
        name="sum_parts",
    )(*heads, *firsts)


def assemble_kernel(place, *refs):
    core, image = place[0], place[1]
    mine, other = refs[:4], refs[4:8]
    fc1_ref, fc2_ref, class_ref = refs[8:]
    hid = fc2_ref.shape[1]
    images = 4
    classes = class_ref.shape[0]
    tall = other[0].shape[0]
    depth = fc1_ref.shape[0]
    quarter = depth // 4
    wide = hid // images
    for step in range(images):
        chunk = lax.rem(image + images - step, images)
        for side, ref in ((core, mine[step]), (1 - core, other[step])):
            at = pl.ds(pl.multiple_of(side * (hid // NC) + chunk * tall, tall), tall)
            fc2_ref[at, :] = ref[:tall, :hid].astype(F32)
            class_ref[:, at] = ref[:classes, hid:].astype(F32)
        cols = pl.ds(pl.multiple_of(chunk * wide, wide), wide)
        for q in range(4):
            part = mine[step][tall : tall + quarter, q * wide : (q + 1) * wide]
            fc1_ref[q * quarter : (q + 1) * quarter, cols] = part.astype(F32)


def assemble(place, mine, other, depth, classes):
    hid = mine[0].shape[1] - 128
    struct = jax.ShapeDtypeStruct
    return pl.pallas_call(
        assemble_kernel,
        out_shape=[struct((depth, hid), F32), struct((hid, hid), F32), struct((classes, hid), F32)],
        in_specs=[SMEM_SPEC] + vmem_spec(8),
        out_specs=vmem_spec(3),
        compiler_params=pltpu.CompilerParams(vmem_limit_bytes=40 * 2**20),
        name="assemble",
    )(place, *mine, *other)


def shift_all(sent):
    return [shift_img(part, step) for step, part in enumerate(sent, 1)]


def shards(
    features,
    w_rpn,
    w_anchor,
    pixel_slots,
    sample_slot,
    sample_weight,
    roi_labels,
    w_fc1,
    w_fc2,
    w_class,
):
    rows, width, channels = features.shape[1:]
    nband = lax.axis_size("band")
    band, image = lax.axis_index("band"), lax.axis_index("img")
    core = band % NC
    hid = w_fc2.shape[0]
    half = hid // NC
    place = jnp.stack([core, image]).astype(jnp.int32)

    flat = features.reshape(rows * width, channels)
    capacity = pixel_slots.shape[3]
    wanted = pixel_slots[0, :, 0, :].reshape(nband * capacity)
    sending = flat[wanted].reshape(nband, capacity, channels)
    received = lax.all_to_all(sending, "band", split_axis=0, concat_axis=0, tiled=True)

    w_first = lax.optimization_barrier((w_fc1, sending))[0]
    w_mine = lax.dynamic_slice_in_dim(w_first, core * half, half, 1)
    w_theirs = lax.dynamic_slice_in_dim(w_first, (1 - core) * half, half, 1)
    w_other = lax.ppermute(w_theirs, "band", CORE_SWAP)
    received, w_other = lax.optimization_barrier((received, w_other))

    received = received.reshape(nband * capacity, channels).astype(F32)
    roi_count, bins = sample_slot.shape[1:3]
    corner_slots = sample_slot[0].reshape(roi_count * bins, 4)
    corner_weights = sample_weight[0].reshape(roi_count * bins, 4)
    slot_ids = jnp.arange(nband * capacity, dtype=jnp.int32)[None, :]
    pooling = jnp.zeros((roi_count * bins, nband * capacity), F32)
    for corner in range(4):
        hits = (corner_slots[:, corner : corner + 1] == slot_ids).astype(F32)
        pooling = pooling + hits * corner_weights[:, corner : corner + 1]
    pooled = jnp.dot(pooling, received, precision=lax.Precision.HIGHEST, preferred_element_type=F32)
    pooled = pooled.astype(BF16).reshape(roi_count, bins, channels)
    depth = w_fc1.shape[0]
    x_local = jnp.transpose(pooled, (0, 2, 1)).reshape(roi_count, nband, depth)
    label_column = jnp.broadcast_to(roi_labels[0].astype(BF16)[:, None, None], (roi_count, nband, 1))
    x_local = jnp.concatenate([x_local, label_column], axis=2).reshape(roi_count, nband * (depth + 1))
    x_cols = lax.all_to_all(x_local, "band", split_axis=1, concat_axis=0, tiled=True)
    labels = x_cols[:, depth:].astype(jnp.int32)
    x_cols = x_cols[:, :depth]

    x_other = lax.ppermute(x_cols, "band", CORE_SWAP)
    partial = dot(x_cols, w_mine, (1, 0)) + dot(x_other, w_other, (1, 0))
    count = x_cols.shape[0]
    by_y = exchange(partial.astype(BF16).reshape(NY, count // NY, half), Y_GROUPS)
    by_y = jnp.sum(by_y.astype(F32), axis=0).astype(BF16)
    by_z = exchange(by_y.reshape(NZ, count // NY // NZ, half), Z_GROUPS)
    a1_own = jnp.sum(by_z.astype(F32), axis=0).astype(BF16)
    a1_z = exchange(jnp.broadcast_to(a1_own[None], (NZ,) + a1_own.shape), Z_GROUPS)
    a1_z = a1_z.reshape(1, count // NY, half)
    a1_mine = exchange(jnp.broadcast_to(a1_z, (NY,) + a1_z.shape[1:]), Y_GROUPS).reshape(count, half)
    a1_other = lax.ppermute(a1_mine, "band", CORE_SWAP)
    classes = w_class.shape[1]
    class_wide = jnp.pad(w_class, ((0, 0), (0, 128 - classes)))
    da2, *parts = head(place, a1_mine, a1_other, labels, w_fc2, class_wide, classes)
    head_own, head_got = parts[0], shift_all(parts[1:])
    parts = first_layer(place, a1_mine, a1_other, da2, w_fc2, x_cols)
    head_got, parts = lax.optimization_barrier((head_got, parts))
    first_got = shift_all(parts[1:])
    total = sum_parts([head_own] + head_got, [parts[0]] + first_got)
    total, inner = lax.optimization_barrier((total, features))
    mine = [total] + [shift_img(total, step) for step in range(1, 4)]
    before, after = halo(inner)
    rpn_out = rpn(before, inner, after, w_rpn, w_anchor)
    mine[2], rpn_out = lax.optimization_barrier((mine[2], rpn_out))
    tall = head_own.shape[0]
    other = [lax.ppermute(part[:tall], "band", CORE_SWAP) for part in mine]
    grad_fc1, grad_fc2, grad_class = assemble(place, mine, other, depth, classes)
    return (rpn_out, grad_fc1, grad_fc2, grad_class.T)


def solution(mesh):
    return jax.shard_map(
        shards,
        mesh=mesh,
        in_specs=(
            P("img", "band", None, None),
            P(),
            P(),
            P("img", None, "band", None),
            P("img", "band", None, None),
            P("img", "band", None, None),
            P("img", "band"),
            P("band", None),
            P(),
            P(),
        ),
        out_specs=(P("img", None, "band", None), P("band", None), P(), P()),
        check_vma=False,
    )
```

```python
import functools

import jax
import jax.numpy as jnp
from jax import lax
from jax.experimental import pallas as pl
from jax.experimental.pallas import tpu as pltpu
from jax.sharding import PartitionSpec as P

NY, NZ, NC = 4, 8, 2
BAND = NY * NZ * NC
F32, BF16 = jnp.float32, jnp.bfloat16
CORE_SWAP = [(b, b ^ 1) for b in range(BAND)]
Z_GROUPS = [[(y * NZ + z) * NC + c for z in range(NZ)] for y in range(NY) for c in range(NC)]
Y_GROUPS = [[(y * NZ + z) * NC + c for y in range(NY)] for z in range(NZ) for c in range(NC)]


def halo(array):
    devices = lax.axis_size("band")
    up = [(i, i + 1) for i in range(devices - 1)]
    down = [(j, i) for i, j in up]
    before = lax.ppermute(array[0, -1:], "band", up)
    after = lax.ppermute(array[0, :1], "band", down)
    return before, after


def rpn_kernel(before_ref, feat_ref, after_ref, rpn_ref, anchor_ref, out_ref, rows, held):
    count = feat_ref.shape[0]
    width = feat_ref.shape[1]
    rows[0] = before_ref[0]
    rows[pl.ds(1, count)] = feat_ref[...]
    rows[count + 1] = after_ref[0]

    def line(y, carry):
        sides = []
        for dx in range(3):
            total = dot(rows[y], rpn_ref[0, dx], (1, 0))
            total = total + dot(rows[y + 1], rpn_ref[1, dx], (1, 0))
            sides.append(total + dot(rows[y + 2], rpn_ref[2, dx], (1, 0)))
        place = lax.broadcasted_iota(jnp.int32, sides[0].shape, 0)
        left = jnp.where(place == 0, 0.0, pltpu.roll(sides[0], 1, 0))
        right = jnp.where(place == width - 1, 0.0, pltpu.roll(sides[2], width - 1, 0))
        hidden = jnp.maximum(left + sides[1] + right, 0.0).astype(BF16)
        held[y] = dot(anchor_ref[...], hidden, (1, 1))
        return carry

    lax.fori_loop(0, count, line, 0)
    for y in range(count):
        for a in range(out_ref.shape[0]):
            out_ref[a, y : y + 1, :] = held[y, a : a + 1, :].astype(BF16)


def rpn(before, features, after, w_rpn, w_anchor):
    rows, width, channels = features.shape[1:]
    anchors = w_anchor.shape[1]
    out = pl.pallas_call(
        rpn_kernel,
        out_shape=jax.ShapeDtypeStruct((anchors, rows, width), BF16),
        in_specs=vmem_spec(5),
        out_specs=pl.BlockSpec(memory_space=pltpu.VMEM),
        scratch_shapes=[
            pltpu.VMEM((rows + 2, width, channels), BF16),
            pltpu.VMEM((rows, anchors, width), F32),
        ],
        compiler_params=pltpu.CompilerParams(vmem_limit_bytes=40 * 2**20),
        cost_estimate=pl.CostEstimate(flops=9 * 10**9, bytes_accessed=4 * 10**6, transcendentals=0),
        name="rpn",
    )(before, features[0], after, w_rpn, w_anchor.T)
    return out[None]


def vmem_spec(count):
    return [pl.BlockSpec(memory_space=pltpu.VMEM)] * count


SMEM_SPEC = pl.BlockSpec(memory_space=pltpu.SMEM)


def exchange(array, groups):
    return lax.all_to_all(
        array, "band", split_axis=0, concat_axis=0, tiled=True, axis_index_groups=groups
    )


def dot(left, right, contract):
    return lax.dot_general(left, right, ((contract[:1], contract[1:]), ((), ())), preferred_element_type=F32)


def shift_img(array, step):
    size = lax.axis_size("img")
    return lax.ppermute(array, "img", [(i, (i + step) % size) for i in range(size)])


def collect_kernel(slots_ref, feat_ref, out_ref, picks, spread):
    pixels = feat_ref.shape[0]
    per_head = slots_ref.shape[0]
    heads = picks.shape[0] // per_head
    column = lax.broadcasted_iota(jnp.int32, (per_head, pixels), 1)
    groups = out_ref.shape[1] // 4
    for part in range(slots_ref.shape[1] // heads):
        for k in range(heads):
            at = part * heads + k
            hit = jnp.broadcast_to(slots_ref[:, at : at + 1], (per_head, pixels)) == column
            picks[k * per_head : (k + 1) * per_head, :] = hit.astype(F32).astype(BF16)
        found = dot(picks[...], feat_ref[...], (1, 0)).T
        lanes = 128
        for k in range(found.shape[1] // lanes):
            group = part * (found.shape[1] // lanes) + k
            spread[pl.ds(group, found.shape[0], stride=groups), :] = found[:, k * lanes : (k + 1) * lanes]
    out_ref[...] = spread[...].reshape(out_ref.shape).astype(BF16)


def collect(slots, flat, nband):
    per_head, heads = slots.shape
    pixels, channels = flat.shape
    rows = channels * per_head * heads // 128
    return pl.pallas_call(
        collect_kernel,
        out_shape=jax.ShapeDtypeStruct((nband, rows // nband, 128), BF16),
        in_specs=vmem_spec(2),
        out_specs=pl.BlockSpec(memory_space=pltpu.VMEM),
        scratch_shapes=[pltpu.VMEM((16 * per_head, pixels), BF16), pltpu.VMEM((rows, 128), F32)],
        compiler_params=pltpu.CompilerParams(vmem_limit_bytes=40 * 2**20),
        cost_estimate=pl.CostEstimate(flops=4 * 10**9, bytes_accessed=3 * 10**6, transcendentals=0),
        name="collect",
    )(slots, flat)


RECIPE_ROWS = 40


def recipe_kernel(slots_ref, weights_ref, labels_ref, out_ref):
    out_ref[...] = jnp.zeros(out_ref.shape, F32)
    bins = slots_ref.shape[2]
    for r in range(slots_ref.shape[0]):
        rows = slice(r // 2 * 4, r // 2 * 4 + 4)
        below = slice(16 + r // 2 * 4, 16 + r // 2 * 4 + 4)
        lanes = slice(r % 2 * 64, r % 2 * 64 + bins)
        out_ref[rows, lanes] = slots_ref[r].astype(F32)
        out_ref[below, lanes] = weights_ref[r]
    out_ref[32:33, : labels_ref.shape[1]] = labels_ref[...].astype(F32)


def recipe(sample_slot, sample_weight, labels):
    return pl.pallas_call(
        recipe_kernel,
        out_shape=jax.ShapeDtypeStruct((RECIPE_ROWS, 128), F32),
        in_specs=vmem_spec(3),
        out_specs=pl.BlockSpec(memory_space=pltpu.VMEM),
        name="recipe",
    )(jnp.transpose(sample_slot, (0, 2, 1)), jnp.transpose(sample_weight, (0, 2, 1)), labels)


def pool_kernel(place, got_ref, recipe_ref, x_ref, label_ref, wide, pooled, marks):
    y0, z0, c0 = place[2], place[3], place[0]
    wide[...] = got_ref[...].astype(F32).reshape(wide.shape)
    lane = lax.broadcasted_iota(jnp.int32, (16, 128), 1)
    chunk_at = lax.broadcasted_iota(jnp.int32, (16, 128), 0)

    def group_step(group, carry):
        rows = []
        for channel in range(4):
            first = channel * 16 + group
            rows.append([wide[pl.ds(first + 64 * b4, 16, stride=256), :] for b4 in range(4)])
        for h4 in range(4):
            head = group * 4 + h4
            y, z, c = head // 16, (head // 2) % 8, head % 2
            entry = entry_of(y, z, c, y0, z0, c0)
            tables = []
            for channel in range(4):
                table = rows[channel][h4]
                for b4 in range(4):
                    if b4 != h4:
                        moved = pltpu.roll(rows[channel][b4], (b4 - h4) * 32 % 128, 1)
                        table = jnp.where(lane // 32 == b4, moved, table)
                tables.append(table)
            marks[pl.ds(head, 1), :] = recipe_ref[entry, 32:33, :]
            for pair in range(4):
                sums = [None] * 4
                for corner in range(4):
                    row = pair * 4 + corner
                    slot = recipe_ref[entry, row : row + 1, :].astype(jnp.int32)
                    weight = recipe_ref[entry, 16 + row : 17 + row, :]
                    slot = jnp.broadcast_to(slot, (16, 128))
                    weight = jnp.broadcast_to(weight, (16, 128))
                    weight = jnp.where(lax.shift_right_logical(slot, 7) == chunk_at, weight, 0.0)
                    place_in = jnp.bitwise_and(slot, 127)
                    for channel in range(4):
                        part = weight * jnp.take_along_axis(tables[channel], place_in, axis=1, mode="promise_in_bounds")
                        sums[channel] = part if corner == 0 else sums[channel] + part
                for channel in range(4):
                    total = jnp.sum(sums[channel], axis=0, keepdims=True)
                    pooled[channel * 4 + pair, pl.ds(head, 1), :] = total
        return carry

    lax.fori_loop(0, 16, group_step, 0)
    low = lax.broadcasted_iota(jnp.int32, (64, 128), 1) < 64
    for r in range(8):
        for block in range(2):
            left, right = pooled[8 * block + r // 2], pooled[8 * block + 4 + r // 2]
            if r % 2 == 0:
                right = pltpu.roll(right, 64, 1)
            else:
                left = pltpu.roll(left, 64, 1)
            both = jnp.where(low, left, right).astype(BF16)
            x_ref[r * 64 : (r + 1) * 64, block * 128 : (block + 1) * 128] = both
        label_ref[r * 64 : (r + 1) * 64, :] = marks[:, r : r + 1].astype(jnp.int32)


def pool(place, got, recipes):
    struct = jax.ShapeDtypeStruct
    nband = got.shape[0]
    return pl.pallas_call(
        pool_kernel,
        out_shape=[struct((8 * nband, 256), BF16), struct((8 * nband, 1), jnp.int32)],
        in_specs=[SMEM_SPEC] + vmem_spec(2),
        out_specs=vmem_spec(2),
        scratch_shapes=[
            pltpu.VMEM((got.shape[0] * got.shape[1], 128), F32),
            pltpu.VMEM((16, nband, 128), F32),
            pltpu.VMEM((nband, 128), F32),
        ],
        compiler_params=pltpu.CompilerParams(vmem_limit_bytes=40 * 2**20),
        name="pool",
    )(place, got, recipes)


def entry_of(y, z, c, y0, z0, c0):
    dz = jnp.bitwise_xor(z, z0)
    dy = jnp.bitwise_xor(y, y0)
    d1, d2 = lax.shift_right_logical(dz, 1), lax.shift_right_logical(dz, 2)
    z_bits = jnp.bitwise_and(jnp.bitwise_xor(dz, d1), 1) * 4
    z_bits = z_bits + jnp.bitwise_and(jnp.bitwise_xor(d1, d2), 1) * 2 + d2
    e1 = lax.shift_right_logical(dy, 1)
    y_bits = jnp.bitwise_and(jnp.bitwise_xor(dy, e1), 1) * 2 + e1
    return jnp.bitwise_xor(c, c0) * 32 + y_bits * 8 + z_bits


def swap_bands(array, pattern):
    y, z, c = pattern
    perm = [(b, b ^ (y * NZ * NC + z * NC + c)) for b in range(BAND)]
    return lax.ppermute(array, "band", perm)


def doubled(array, pattern):
    return jnp.concatenate([array, swap_bands(array, pattern)], axis=0)


def gelu_parts(value):
    cubic = 0.044715 * (value * value * value)
    tanh = jnp.tanh(0.7978845608028654 * (value + cubic))
    return tanh


def gelu_of(value):
    return 0.5 * value * (1.0 + gelu_parts(value))


def slope_of(value):
    tanh = gelu_parts(value)
    inner = 0.7978845608028654 * (1.0 + 3.0 * 0.044715 * (value * value))
    return 0.5 * (1.0 + tanh) + 0.5 * value * (1.0 - tanh * tanh) * inner


ROW_BLOCK = 128


def join_halves(core, mine_ref, other_ref, whole_ref):
    half = mine_ref.shape[1]
    whole_ref[:, pl.ds(pl.multiple_of(core * half, half), half)] = mine_ref[...]
    whole_ref[:, pl.ds(pl.multiple_of((1 - core) * half, half), half)] = other_ref[...]


def head_kernel(classes, place, mine_ref, other_ref, labels_ref, fc2_ref, class_ref,
                da2_ref, own_ref, s1_ref, s2_ref, s3_ref, a1, h1, h2, dlog):
    core, image = place[0], place[1]
    join_halves(core, mine_ref, other_ref, a1)
    count, hid = a1.shape
    lanes = class_ref.shape[1]

    def block(step, carry):
        rows = pl.ds(pl.multiple_of(step * ROW_BLOCK, ROW_BLOCK), ROW_BLOCK)
        hidden = gelu_of(a1[rows, :].astype(F32)).astype(BF16)
        h1[rows, :] = hidden
        a2 = dot(hidden, fc2_ref[...], (1, 0))
        second = gelu_of(a2).astype(BF16)
        h2[rows, :] = second
        logits = dot(second, class_ref[...], (1, 0))
        column = lax.broadcasted_iota(jnp.int32, (ROW_BLOCK, lanes), 1)
        expo = jnp.where(column < classes, jnp.exp(logits), 0.0)
        prob = expo / jnp.sum(expo, axis=1, keepdims=True)
        onehot = (labels_ref[rows, :] == column).astype(F32)
        dlogits = (prob - onehot).astype(BF16)
        dlog[rows, :] = dlogits
        dh2 = dot(dlogits, class_ref[...], (1, 1))
        da2_ref[rows, :] = (dh2 * slope_of(a2)).astype(BF16)
        return carry

    lax.fori_loop(0, count // ROW_BLOCK, block, 0)
    images = 4
    wide = hid // NC // images
    for step, out in enumerate((own_ref, s1_ref, s2_ref, s3_ref)):
        chunk = lax.rem(image + step, images)
        cols = pl.ds(pl.multiple_of(core * (hid // NC) + chunk * wide, wide), wide)
        out[:, :hid] = dot(h1[:, cols], da2_ref[...], (0, 0)).astype(out.dtype)
        out[:, hid:] = dot(dlog[...], h2[:, cols], (0, 0)).astype(out.dtype)


def head(place, mine, other, labels, w_fc2, w_class, classes):
    count, half = mine.shape
    hid = w_fc2.shape[0]
    lanes = w_class.shape[1]
    wide = half // 4
    struct = jax.ShapeDtypeStruct
    return pl.pallas_call(
        functools.partial(head_kernel, classes),
        out_shape=[struct((count, hid), BF16), struct((wide, hid + lanes), F32)]
        + [struct((wide, hid + lanes), BF16)] * 3,
        in_specs=[SMEM_SPEC] + vmem_spec(5),
        out_specs=vmem_spec(5),
        scratch_shapes=[
            pltpu.VMEM((count, hid), BF16),
            pltpu.VMEM((count, hid), BF16),
            pltpu.VMEM((count, hid), BF16),
            pltpu.VMEM((count, lanes), BF16),
        ],
        compiler_params=pltpu.CompilerParams(vmem_limit_bytes=40 * 2**20),
        name="head",
    )(place, mine, other, labels, w_fc2, w_class)


def first_kernel(place, mine_ref, other_ref, da2_ref, fc2_ref, x_ref,
                 own_ref, s1_ref, s2_ref, s3_ref, a1, da1):
    core, image = place[0], place[1]
    join_halves(core, mine_ref, other_ref, a1)
    count, hid = a1.shape

    def block(step, carry):
        rows = pl.ds(pl.multiple_of(step * ROW_BLOCK, ROW_BLOCK), ROW_BLOCK)
        dh1 = dot(da2_ref[rows, :], fc2_ref[...], (1, 1))
        da1[rows, :] = (dh1 * slope_of(a1[rows, :].astype(F32))).astype(BF16)
        return carry

    lax.fori_loop(0, count // ROW_BLOCK, block, 0)
    images = 4
    wide = hid // images
    for step, out in enumerate((own_ref, s1_ref, s2_ref, s3_ref)):
        chunk = lax.rem(image + step, images)
        cols = pl.ds(pl.multiple_of(chunk * wide, wide), wide)
        out[...] = dot(x_ref[...], da1[:, cols], (0, 0)).astype(out.dtype)


def first_layer(place, mine, other, da2, w_fc2, x_cols):
    count, hid = da2.shape
    depth = x_cols.shape[1]
    wide = hid // 4
    struct = jax.ShapeDtypeStruct
    return pl.pallas_call(
        first_kernel,
        out_shape=[struct((depth, wide), F32)] + [struct((depth, wide), BF16)] * 3,
        in_specs=[SMEM_SPEC] + vmem_spec(5),
        out_specs=vmem_spec(4),
        scratch_shapes=[pltpu.VMEM((count, hid), BF16), pltpu.VMEM((count, hid), BF16)],
        compiler_params=pltpu.CompilerParams(vmem_limit_bytes=40 * 2**20),
        name="first_layer",
    )(place, mine, other, da2, w_fc2, x_cols)


SUM_ROWS = 192


def sum_kernel(*refs):
    heads, firsts, out_ref = refs[:4], refs[4:8], refs[8]
    tall, wide = heads[0].shape
    total = heads[0][...]
    for ref in heads[1:]:
        total = total + ref[...].astype(F32)
    out_ref[:tall, :] = total.astype(BF16)
    first = firsts[0][...]
    for ref in firsts[1:]:
        first = first + ref[...].astype(F32)
    depth, cols = first.shape
    quarter = depth // 4
    rest = jnp.zeros((SUM_ROWS - tall, wide), BF16)
    out_ref[tall:, :] = rest
    for q in range(4):
        part = first[q * quarter : (q + 1) * quarter].astype(BF16)
        out_ref[tall : tall + quarter, q * cols : (q + 1) * cols] = part


def sum_parts(heads, firsts):
    wide = heads[0].shape[1]
    return pl.pallas_call(
        sum_kernel,
        out_shape=jax.ShapeDtypeStruct((SUM_ROWS, wide), BF16),
        in_specs=vmem_spec(8),
        out_specs=pl.BlockSpec(memory_space=pltpu.VMEM),
        compiler_params=pltpu.CompilerParams(vmem_limit_bytes=40 * 2**20),
        name="sum_parts",
    )(*heads, *firsts)


def assemble_kernel(place, *refs):
    core, image = place[0], place[1]
    mine, other = refs[:4], refs[4:8]
    fc1_ref, fc2_ref, class_ref = refs[8:]
    hid = fc2_ref.shape[1]
    images = 4
    classes = class_ref.shape[0]
    tall = other[0].shape[0]
    depth = fc1_ref.shape[0]
    quarter = depth // 4
    wide = hid // images
    for step in range(images):
        chunk = lax.rem(image + images - step, images)
        for side, ref in ((core, mine[step]), (1 - core, other[step])):
            at = pl.ds(pl.multiple_of(side * (hid // NC) + chunk * tall, tall), tall)
            fc2_ref[at, :] = ref[:tall, :hid].astype(F32)
            class_ref[:, at] = ref[:classes, hid:].astype(F32)
        cols = pl.ds(pl.multiple_of(chunk * wide, wide), wide)
        for q in range(4):
            part = mine[step][tall : tall + quarter, q * wide : (q + 1) * wide]
            fc1_ref[q * quarter : (q + 1) * quarter, cols] = part.astype(F32)


def assemble(place, mine, other, depth, classes):
    hid = mine[0].shape[1] - 128
    struct = jax.ShapeDtypeStruct
    return pl.pallas_call(
        assemble_kernel,
        out_shape=[struct((depth, hid), F32), struct((hid, hid), F32), struct((classes, hid), F32)],
        in_specs=[SMEM_SPEC] + vmem_spec(8),
        out_specs=vmem_spec(3),
        compiler_params=pltpu.CompilerParams(vmem_limit_bytes=40 * 2**20),
        name="assemble",
    )(place, *mine, *other)


def shift_all(sent):
    return [shift_img(part, step) for step, part in enumerate(sent, 1)]


def shards(
    features,
    w_rpn,
    w_anchor,
    pixel_slots,
    sample_slot,
    sample_weight,
    roi_labels,
    w_fc1,
    w_fc2,
    w_class,
):
    rows, width, channels = features.shape[1:]
    nband = lax.axis_size("band")
    band, image = lax.axis_index("band"), lax.axis_index("img")
    core = band % NC
    hid = w_fc2.shape[0]
    half = hid // NC
    z_at, y_at = (band // NC) % NZ, band // (NC * NZ)
    place = jnp.stack([core, image, y_at, z_at]).astype(jnp.int32)

    flat = features.reshape(rows * width, channels)
    recipes = recipe(sample_slot[0], sample_weight[0], roi_labels)[None]
    for pattern in ((0, 7, 0), (0, 3, 0), (0, 1, 0)):
        recipes = doubled(recipes, pattern)
    sending = collect(jnp.transpose(pixel_slots[0, :, 0, :]), flat, nband)
    sending, recipes = lax.optimization_barrier((sending, recipes))
    received = lax.all_to_all(sending, "band", split_axis=0, concat_axis=0, tiled=True)
    for pattern in ((3, 0, 0), (1, 0, 0), (0, 0, 1)):
        recipes = doubled(recipes, pattern)

    w_first = lax.optimization_barrier((w_fc1, sending))[0]
    depth = w_first.shape[0]
    w_first = jnp.pad(w_first.reshape(4, depth // 4, hid), ((0, 0), (0, 64 - depth // 4), (0, 0)))
    w_first = w_first.reshape(256, hid)
    w_mine = lax.dynamic_slice_in_dim(w_first, core * half, half, 1)
    w_theirs = lax.dynamic_slice_in_dim(w_first, (1 - core) * half, half, 1)
    w_other = lax.ppermute(w_theirs, "band", CORE_SWAP)
    received, w_other, recipes = lax.optimization_barrier((received, w_other, recipes))
    x_cols, labels = pool(place, received, recipes)

    x_other = lax.ppermute(x_cols, "band", CORE_SWAP)
    partial = dot(x_cols, w_mine, (1, 0)) + dot(x_other, w_other, (1, 0))
    count = x_cols.shape[0]
    by_y = exchange(partial.astype(BF16).reshape(NY, count // NY, half), Y_GROUPS)
    by_y = jnp.sum(by_y.astype(F32), axis=0).astype(BF16)
    by_z = exchange(by_y.reshape(NZ, count // NY // NZ, half), Z_GROUPS)
    a1_own = jnp.sum(by_z.astype(F32), axis=0).astype(BF16)
    a1_z = exchange(jnp.broadcast_to(a1_own[None], (NZ,) + a1_own.shape), Z_GROUPS)
    a1_z = a1_z.reshape(1, count // NY, half)
    a1_mine = exchange(jnp.broadcast_to(a1_z, (NY,) + a1_z.shape[1:]), Y_GROUPS).reshape(count, half)
    a1_other = lax.ppermute(a1_mine, "band", CORE_SWAP)
    classes = w_class.shape[1]
    class_wide = jnp.pad(w_class, ((0, 0), (0, 128 - classes)))
    da2, *parts = head(place, a1_mine, a1_other, labels, w_fc2, class_wide, classes)
    head_own, head_got = parts[0], shift_all(parts[1:])
    parts = first_layer(place, a1_mine, a1_other, da2, w_fc2, x_cols)
    head_got, parts = lax.optimization_barrier((head_got, parts))
    first_got = shift_all(parts[1:])
    total = sum_parts([head_own] + head_got, [parts[0]] + first_got)
    total, inner = lax.optimization_barrier((total, features))
    mine = [total] + [shift_img(total, step) for step in range(1, 4)]
    before, after = halo(inner)
    rpn_out = rpn(before, inner, after, w_rpn, w_anchor)
    mine[2], rpn_out = lax.optimization_barrier((mine[2], rpn_out))
    tall = head_own.shape[0]
    other = [lax.ppermute(part[:tall], "band", CORE_SWAP) for part in mine]
    grad_fc1, grad_fc2, grad_class = assemble(place, mine, other, depth, classes)
    return (rpn_out, grad_fc1, grad_fc2, grad_class.T)


def solution(mesh):
    return jax.shard_map(
        shards,
        mesh=mesh,
        in_specs=(
            P("img", "band", None, None),
            P(),
            P(),
            P("img", None, "band", None),
            P("img", "band", None, None),
            P("img", "band", None, None),
            P("img", "band"),
            P("band", None),
            P(),
            P(),
        ),
        out_specs=(P("img", None, "band", None), P("band", None), P(), P()),
        check_vma=False,
    )
```

```python
import functools

import jax
import jax.numpy as jnp
from jax import lax
from jax.experimental import pallas as pl
from jax.experimental.pallas import tpu as pltpu
from jax.sharding import PartitionSpec as P

NY, NZ, NC = 4, 8, 2
BAND = NY * NZ * NC
F32, BF16 = jnp.float32, jnp.bfloat16
CORE_SWAP = [(b, b ^ 1) for b in range(BAND)]
Z_GROUPS = [[(y * NZ + z) * NC + c for z in range(NZ)] for y in range(NY) for c in range(NC)]
ZC_GROUPS = [[y * NZ * NC + k for k in range(NZ * NC)] for y in range(NY)]
Y_GROUPS = [[(y * NZ + z) * NC + c for y in range(NY)] for z in range(NZ) for c in range(NC)]


def halo(array):
    devices = lax.axis_size("band")
    up = [(i, i + 1) for i in range(devices - 1)]
    down = [(j, i) for i, j in up]
    before = lax.ppermute(array[0, -1:], "band", up)
    after = lax.ppermute(array[0, :1], "band", down)
    return before, after


def rpn_kernel(before_ref, feat_ref, after_ref, rpn_ref, anchor_ref, out_ref, rows, held):
    count = feat_ref.shape[0]
    width = feat_ref.shape[1]
    rows[0] = before_ref[0]
    rows[pl.ds(1, count)] = feat_ref[...]
    rows[count + 1] = after_ref[0]

    def line(y, carry):
        sides = []
        for dx in range(3):
            total = dot(rows[y], rpn_ref[0, dx], (1, 0))
            total = total + dot(rows[y + 1], rpn_ref[1, dx], (1, 0))
            sides.append(total + dot(rows[y + 2], rpn_ref[2, dx], (1, 0)))
        place = lax.broadcasted_iota(jnp.int32, sides[0].shape, 0)
        left = jnp.where(place == 0, 0.0, pltpu.roll(sides[0], 1, 0))
        right = jnp.where(place == width - 1, 0.0, pltpu.roll(sides[2], width - 1, 0))
        hidden = jnp.maximum(left + sides[1] + right, 0.0).astype(BF16)
        held[y] = dot(anchor_ref[...], hidden, (1, 1))
        return carry

    lax.fori_loop(0, count, line, 0)
    for y in range(count):
        for a in range(out_ref.shape[0]):
            out_ref[a, y : y + 1, :] = held[y, a : a + 1, :].astype(BF16)


def rpn(before, features, after, w_rpn, w_anchor):
    rows, width, channels = features.shape[1:]
    anchors = w_anchor.shape[1]
    out = pl.pallas_call(
        rpn_kernel,
        out_shape=jax.ShapeDtypeStruct((anchors, rows, width), BF16),
        in_specs=vmem_spec(5),
        out_specs=pl.BlockSpec(memory_space=pltpu.VMEM),
        scratch_shapes=[
            pltpu.VMEM((rows + 2, width, channels), BF16),
            pltpu.VMEM((rows, anchors, width), F32),
        ],
        compiler_params=pltpu.CompilerParams(vmem_limit_bytes=40 * 2**20),
        cost_estimate=pl.CostEstimate(flops=9 * 10**9, bytes_accessed=4 * 10**6, transcendentals=0),
        name="rpn",
    )(before, features[0], after, w_rpn, w_anchor.T)
    return out[None]


def vmem_spec(count):
    return [pl.BlockSpec(memory_space=pltpu.VMEM)] * count


SMEM_SPEC = pl.BlockSpec(memory_space=pltpu.SMEM)


def exchange(array, groups):
    return lax.all_to_all(
        array, "band", split_axis=0, concat_axis=0, tiled=True, axis_index_groups=groups
    )


def dot(left, right, contract):
    return lax.dot_general(left, right, ((contract[:1], contract[1:]), ((), ())), preferred_element_type=F32)


def shift_img(array, step):
    size = lax.axis_size("img")
    return lax.ppermute(array, "img", [(i, (i + step) % size) for i in range(size)])


def collect_kernel(slots_ref, feat_ref, out_ref, picks):
    pixels = feat_ref.shape[0]
    per_head = slots_ref.shape[0]
    heads = picks.shape[0] // per_head
    column = lax.broadcasted_iota(jnp.int32, (per_head, pixels), 1)
    for part in range(slots_ref.shape[1] // heads):
        for k in range(heads):
            at = part * heads + k
            hit = jnp.broadcast_to(slots_ref[:, at : at + 1], (per_head, pixels)) == column
            picks[k * per_head : (k + 1) * per_head, :] = hit.astype(F32).astype(BF16)
        found = dot(picks[...], feat_ref[...], (1, 0)).astype(BF16)
        out_ref[part * heads : (part + 1) * heads] = found.reshape((heads, per_head, found.shape[1]))


def collect(slots, flat):
    per_head, heads = slots.shape
    pixels, channels = flat.shape
    return pl.pallas_call(
        collect_kernel,
        out_shape=jax.ShapeDtypeStruct((heads, per_head, channels), BF16),
        in_specs=vmem_spec(2),
        out_specs=pl.BlockSpec(memory_space=pltpu.VMEM),
        scratch_shapes=[pltpu.VMEM((16 * per_head, pixels), BF16)],
        compiler_params=pltpu.CompilerParams(vmem_limit_bytes=40 * 2**20),
        cost_estimate=pl.CostEstimate(flops=4 * 10**9, bytes_accessed=3 * 10**6, transcendentals=0),
        name="collect",
    )(slots, flat)


def partial_kernel(place, mine_ref, other_ref, *refs):
    y_at = place[2]
    weights, out_ref = refs[:NY], refs[NY]
    depth = weights[0].shape[1]
    total = None
    for step in range(NY):
        start = lax.rem(y_at + NY - step, NY) * PITCH
        cols = pl.ds(pl.multiple_of(start, PITCH), PITCH)
        for ref, weight in ((mine_ref, weights[step][0]), (other_ref, weights[step][1])):
            part = dot(ref[:, cols][:, :depth], weight, (1, 0))
            total = part if total is None else total + part
    out_ref[...] = total.astype(BF16)


PITCH = 256


def partial_sums(place, mine, other, weights):
    return pl.pallas_call(
        partial_kernel,
        out_shape=jax.ShapeDtypeStruct((mine.shape[0], weights[0].shape[2]), BF16),
        in_specs=[SMEM_SPEC] + vmem_spec(2 + NY),
        out_specs=pl.BlockSpec(memory_space=pltpu.VMEM),
        compiler_params=pltpu.CompilerParams(vmem_limit_bytes=40 * 2**20),
        name="partial_sums",
    )(place, mine, other, *weights)


def shift_y(array, step):
    row = NZ * NC
    return lax.ppermute(array, "band", [(b, (b + step * row) % BAND) for b in range(BAND)])


def gelu_parts(value):
    cubic = 0.044715 * (value * value * value)
    tanh = jnp.tanh(0.7978845608028654 * (value + cubic))
    return tanh


def gelu_of(value):
    return 0.5 * value * (1.0 + gelu_parts(value))


def slope_of(value):
    tanh = gelu_parts(value)
    inner = 0.7978845608028654 * (1.0 + 3.0 * 0.044715 * (value * value))
    return 0.5 * (1.0 + tanh) + 0.5 * value * (1.0 - tanh * tanh) * inner


ROW_BLOCK = 128


def join_halves(core, mine_ref, other_ref, whole_ref):
    half = mine_ref.shape[1]
    whole_ref[:, pl.ds(pl.multiple_of(core * half, half), half)] = mine_ref[...]
    whole_ref[:, pl.ds(pl.multiple_of((1 - core) * half, half), half)] = other_ref[...]


def head_kernel(classes, place, mine_ref, other_ref, labels_ref, fc2_ref, class_ref,
                da2_ref, own_ref, s1_ref, s2_ref, s3_ref, a1, h1, h2, dlog):
    core, image = place[0], place[1]
    join_halves(core, mine_ref, other_ref, a1)
    count, hid = a1.shape
    lanes = class_ref.shape[1]

    def block(step, carry):
        rows = pl.ds(pl.multiple_of(step * ROW_BLOCK, ROW_BLOCK), ROW_BLOCK)
        hidden = gelu_of(a1[rows, :].astype(F32)).astype(BF16)
        h1[rows, :] = hidden
        a2 = dot(hidden, fc2_ref[...], (1, 0))
        second = gelu_of(a2).astype(BF16)
        h2[rows, :] = second
        logits = dot(second, class_ref[...], (1, 0))
        column = lax.broadcasted_iota(jnp.int32, (ROW_BLOCK, lanes), 1)
        expo = jnp.where(column < classes, jnp.exp(logits), 0.0)
        prob = expo / jnp.sum(expo, axis=1, keepdims=True)
        onehot = (labels_ref[rows, :] == column).astype(F32)
        dlogits = (prob - onehot).astype(BF16)
        dlog[rows, :] = dlogits
        dh2 = dot(dlogits, class_ref[...], (1, 1))
        da2_ref[rows, :] = (dh2 * slope_of(a2)).astype(BF16)
        return carry

    lax.fori_loop(0, count // ROW_BLOCK, block, 0)
    images = 4
    wide = hid // NC // images
    for step, out in enumerate((own_ref, s1_ref, s2_ref, s3_ref)):
        chunk = lax.rem(image + step, images)
        cols = pl.ds(pl.multiple_of(core * (hid // NC) + chunk * wide, wide), wide)
        out[:, :hid] = dot(h1[:, cols], da2_ref[...], (0, 0)).astype(out.dtype)
        out[:, hid:] = dot(dlog[...], h2[:, cols], (0, 0)).astype(out.dtype)


def head(place, mine, other, labels, w_fc2, w_class, classes):
    count, half = mine.shape
    hid = w_fc2.shape[0]
    lanes = w_class.shape[1]
    wide = half // 4
    struct = jax.ShapeDtypeStruct
    return pl.pallas_call(
        functools.partial(head_kernel, classes),
        out_shape=[struct((count, hid), BF16), struct((wide, hid + lanes), F32)]
        + [struct((wide, hid + lanes), BF16)] * 3,
        in_specs=[SMEM_SPEC] + vmem_spec(5),
        out_specs=vmem_spec(5),
        scratch_shapes=[
            pltpu.VMEM((count, hid), BF16),
            pltpu.VMEM((count, hid), BF16),
            pltpu.VMEM((count, hid), BF16),
            pltpu.VMEM((count, lanes), BF16),
        ],
        compiler_params=pltpu.CompilerParams(vmem_limit_bytes=40 * 2**20),
        name="head",
    )(place, mine, other, labels, w_fc2, w_class)


def first_kernel(place, mine_ref, other_ref, da2_ref, fc2_ref, *refs):
    core, image, y_at = place[0], place[1], place[2]
    x_refs, outs, a1, da1 = refs[:NY], refs[NY : NY + 4], refs[NY + 4], refs[NY + 5]
    join_halves(core, mine_ref, other_ref, a1)
    count, hid = a1.shape

    def block(step, carry):
        rows = pl.ds(pl.multiple_of(step * ROW_BLOCK, ROW_BLOCK), ROW_BLOCK)
        dh1 = dot(da2_ref[rows, :], fc2_ref[...], (1, 1))
        da1[rows, :] = (dh1 * slope_of(a1[rows, :].astype(F32))).astype(BF16)
        return carry

    lax.fori_loop(0, count // ROW_BLOCK, block, 0)
    images = 4
    wide = hid // images
    tall = count // NY
    depth = outs[0].shape[0]
    for step, out in enumerate(outs):
        chunk = lax.rem(image + step, images)
        cols = pl.ds(pl.multiple_of(chunk * wide, wide), wide)
        total = None
        for back in range(NY):
            start = lax.rem(y_at + NY - back, NY) * tall
            part = dot(x_refs[back][...], da1[pl.ds(pl.multiple_of(start, tall), tall), cols], (0, 0))
            total = part if total is None else total + part
        out[...] = total[:depth].astype(out.dtype)


def first_layer(place, mine, other, da2, w_fc2, x_blocks, depth):
    count, hid = da2.shape
    wide = hid // 4
    struct = jax.ShapeDtypeStruct
    return pl.pallas_call(
        first_kernel,
        out_shape=[struct((depth, wide), F32)] + [struct((depth, wide), BF16)] * 3,
        in_specs=[SMEM_SPEC] + vmem_spec(4 + NY),
        out_specs=vmem_spec(4),
        scratch_shapes=[pltpu.VMEM((count, hid), BF16), pltpu.VMEM((count, hid), BF16)],
        compiler_params=pltpu.CompilerParams(vmem_limit_bytes=40 * 2**20),
        name="first_layer",
    )(place, mine, other, da2, w_fc2, *x_blocks)


SUM_ROWS = 192


def sum_kernel(*refs):
    heads, firsts, out_ref = refs[:4], refs[4:8], refs[8]
    tall, wide = heads[0].shape
    total = heads[0][...]
    for ref in heads[1:]:
        total = total + ref[...].astype(F32)
    out_ref[:tall, :] = total.astype(BF16)
    first = firsts[0][...]
    for ref in firsts[1:]:
        first = first + ref[...].astype(F32)
    depth, cols = first.shape
    quarter = depth // 4
    rest = jnp.zeros((SUM_ROWS - tall, wide), BF16)
    out_ref[tall:, :] = rest
    for q in range(4):
        part = first[q * quarter : (q + 1) * quarter].astype(BF16)
        out_ref[tall : tall + quarter, q * cols : (q + 1) * cols] = part


def sum_parts(heads, firsts):
    wide = heads[0].shape[1]
    return pl.pallas_call(
        sum_kernel,
        out_shape=jax.ShapeDtypeStruct((SUM_ROWS, wide), BF16),
        in_specs=vmem_spec(8),
        out_specs=pl.BlockSpec(memory_space=pltpu.VMEM),
        compiler_params=pltpu.CompilerParams(vmem_limit_bytes=40 * 2**20),
        name="sum_parts",
    )(*heads, *firsts)


def assemble_kernel(place, *refs):
    core, image = place[0], place[1]
    mine, other = refs[:4], refs[4:8]
    fc1_ref, fc2_ref, class_ref = refs[8:]
    hid = fc2_ref.shape[1]
    images = 4
    classes = class_ref.shape[0]
    tall = other[0].shape[0]
    depth = fc1_ref.shape[0]
    quarter = depth // 4
    wide = hid // images
    for step in range(images):
        chunk = lax.rem(image + images - step, images)
        for side, ref in ((core, mine[step]), (1 - core, other[step])):
            at = pl.ds(pl.multiple_of(side * (hid // NC) + chunk * tall, tall), tall)
            fc2_ref[at, :] = ref[:tall, :hid].astype(F32)
            class_ref[:, at] = ref[:classes, hid:].astype(F32)
        cols = pl.ds(pl.multiple_of(chunk * wide, wide), wide)
        for q in range(4):
            part = mine[step][tall : tall + quarter, q * wide : (q + 1) * wide]
            fc1_ref[q * quarter : (q + 1) * quarter, cols] = part.astype(F32)


def assemble(place, mine, other, depth, classes):
    hid = mine[0].shape[1] - 128
    struct = jax.ShapeDtypeStruct
    return pl.pallas_call(
        assemble_kernel,
        out_shape=[struct((depth, hid), F32), struct((hid, hid), F32), struct((classes, hid), F32)],
        in_specs=[SMEM_SPEC] + vmem_spec(8),
        out_specs=vmem_spec(3),
        compiler_params=pltpu.CompilerParams(vmem_limit_bytes=40 * 2**20),
        name="assemble",
    )(place, *mine, *other)


def shift_all(sent):
    return [shift_img(part, step) for step, part in enumerate(sent, 1)]


def shards(
    features,
    w_rpn,
    w_anchor,
    pixel_slots,
    sample_slot,
    sample_weight,
    roi_labels,
    w_fc1,
    w_fc2,
    w_class,
):
    rows, width, channels = features.shape[1:]
    nband = lax.axis_size("band")
    band, image = lax.axis_index("band"), lax.axis_index("img")
    core = band % NC
    hid = w_fc2.shape[0]
    half = hid // NC
    y_at = band // (NC * NZ)
    place = jnp.stack([core, image, y_at]).astype(jnp.int32)

    flat = features.reshape(rows * width, channels)
    capacity = pixel_slots.shape[3]
    sending = collect(jnp.transpose(pixel_slots[0, :, 0, :]), flat)
    received = lax.all_to_all(sending, "band", split_axis=0, concat_axis=0, tiled=True)

    w_first, labels = lax.optimization_barrier((w_fc1, roi_labels, sending))[:2]
    depth = w_first.shape[0]
    w_mine = lax.dynamic_slice_in_dim(w_first, core * half, half, 1)
    w_theirs = lax.dynamic_slice_in_dim(w_first, (1 - core) * half, half, 1)
    w_pair = jnp.stack([w_mine, lax.ppermute(w_theirs, "band", CORE_SWAP)])
    weights = [w_pair] + [shift_y(w_pair, step) for step in range(1, NY)]
    labels = lax.all_gather(labels[0], "band", axis=0, tiled=True)[:, None]
    received, weights, labels = lax.optimization_barrier((received, weights, labels))

    received = received.reshape(nband * capacity, channels).astype(F32)
    roi_count, bins = sample_slot.shape[1:3]
    corner_slots = sample_slot[0].reshape(roi_count * bins, 4)
    corner_weights = sample_weight[0].reshape(roi_count * bins, 4)
    slot_ids = jnp.arange(nband * capacity, dtype=jnp.int32)[None, :]
    pooling = jnp.zeros((roi_count * bins, nband * capacity), F32)
    for corner in range(4):
        hits = (corner_slots[:, corner : corner + 1] == slot_ids).astype(F32)
        pooling = pooling + hits * corner_weights[:, corner : corner + 1]
    pooled = jnp.dot(pooling, received, precision=lax.Precision.HIGHEST, preferred_element_type=F32)
    pooled = pooled.astype(BF16).reshape(roi_count, bins, channels)
    x_local = jnp.transpose(pooled, (0, 2, 1)).reshape(roi_count, nband, depth)
    x_local = jnp.pad(x_local, ((0, 0), (0, 0), (0, PITCH - depth)))
    x_local = x_local.reshape(roi_count, NY, NZ * NC, PITCH).transpose(2, 0, 1, 3)
    x_part = exchange(x_local.reshape(NZ * NC, roi_count, NY * PITCH), ZC_GROUPS)
    x_part = x_part.reshape(NZ * NC * roi_count, NY * PITCH)

    x_other = lax.ppermute(x_part, "band", CORE_SWAP)
    partial = partial_sums(place, x_part, x_other, weights)
    count = roi_count * nband
    by_z = exchange(partial.reshape(NZ, count // NY // NZ, half), Z_GROUPS)
    a1_own = jnp.sum(by_z.astype(F32), axis=0).astype(BF16)
    a1_z = exchange(jnp.broadcast_to(a1_own[None], (NZ,) + a1_own.shape), Z_GROUPS)
    a1_z = a1_z.reshape(1, count // NY, half)
    a1_mine = exchange(jnp.broadcast_to(a1_z, (NY,) + a1_z.shape[1:]), Y_GROUPS).reshape(count, half)
    a1_other = lax.ppermute(a1_mine, "band", CORE_SWAP)
    classes = w_class.shape[1]
    class_wide = jnp.pad(w_class, ((0, 0), (0, 128 - classes)))
    da2, *parts = head(place, a1_mine, a1_other, labels, w_fc2, class_wide, classes)
    head_own, head_got = parts[0], shift_all(parts[1:])
    x_part = lax.optimization_barrier((x_part, da2))[0]
    x_blocks = [lax.dynamic_slice_in_dim(x_part, y_at * PITCH, PITCH, 1)]
    for step in range(1, NY):
        to = (y_at + step) % NY
        x_blocks.append(shift_y(lax.dynamic_slice_in_dim(x_part, to * PITCH, PITCH, 1), step))
    parts = first_layer(place, a1_mine, a1_other, da2, w_fc2, x_blocks, depth)
    head_got, parts = lax.optimization_barrier((head_got, parts))
    first_got = shift_all(parts[1:])
    total = sum_parts([head_own] + head_got, [parts[0]] + first_got)
    total, inner = lax.optimization_barrier((total, features))
    mine = [total] + [shift_img(total, step) for step in range(1, 4)]
    before, after = halo(inner)
    rpn_out = rpn(before, inner, after, w_rpn, w_anchor)
    mine[2], rpn_out = lax.optimization_barrier((mine[2], rpn_out))
    tall = head_own.shape[0]
    other = [lax.ppermute(part[:tall], "band", CORE_SWAP) for part in mine]
    grad_fc1, grad_fc2, grad_class = assemble(place, mine, other, depth, classes)
    return (rpn_out, grad_fc1, grad_fc2, grad_class.T)


def solution(mesh):
    return jax.shard_map(
        shards,
        mesh=mesh,
        in_specs=(
            P("img", "band", None, None),
            P(),
            P(),
            P("img", None, "band", None),
            P("img", "band", None, None),
            P("img", "band", None, None),
            P("img", "band"),
            P("band", None),
            P(),
            P(),
        ),
        out_specs=(P("img", None, "band", None), P("band", None), P(), P()),
        check_vma=False,
    )
```

```python
import functools

import jax
import jax.numpy as jnp
from jax import lax
from jax.experimental import pallas as pl
from jax.experimental.pallas import tpu as pltpu
from jax.sharding import PartitionSpec as P

NY, NZ, NC = 4, 8, 2
BAND = NY * NZ * NC
F32, BF16 = jnp.float32, jnp.bfloat16
VMEM = 24 * 2**20
CORE_SWAP = [(b, b ^ 1) for b in range(BAND)]
Z_GROUPS = [[(y * NZ + z) * NC + c for z in range(NZ)] for y in range(NY) for c in range(NC)]
Y_GROUPS = [[(y * NZ + z) * NC + c for y in range(NY)] for z in range(NZ) for c in range(NC)]


def halo(array):
    devices = lax.axis_size("band")
    up = [(i, i + 1) for i in range(devices - 1)]
    down = [(j, i) for i, j in up]
    before = lax.ppermute(array[0, -1:], "band", up)
    after = lax.ppermute(array[0, :1], "band", down)
    return before, after


def rpn_kernel(before_ref, feat_ref, after_ref, rpn_ref, anchor_ref, out_ref, rows, held):
    count = feat_ref.shape[0]
    width = feat_ref.shape[1]
    rows[0] = before_ref[0]
    rows[pl.ds(1, count)] = feat_ref[...]
    rows[count + 1] = after_ref[0]

    def line(y, carry):
        sides = []
        for dx in range(3):
            total = dot(rows[y], rpn_ref[0, dx], (1, 0))
            total = total + dot(rows[y + 1], rpn_ref[1, dx], (1, 0))
            sides.append(total + dot(rows[y + 2], rpn_ref[2, dx], (1, 0)))
        place = lax.broadcasted_iota(jnp.int32, sides[0].shape, 0)
        left = jnp.where(place == 0, 0.0, pltpu.roll(sides[0], 1, 0))
        right = jnp.where(place == width - 1, 0.0, pltpu.roll(sides[2], width - 1, 0))
        hidden = jnp.maximum(left + sides[1] + right, 0.0).astype(BF16)
        held[y] = dot(anchor_ref[...], hidden, (1, 1))
        return carry

    lax.fori_loop(0, count, line, 0)
    for y in range(count):
        for a in range(out_ref.shape[0]):
            out_ref[a, y : y + 1, :] = held[y, a : a + 1, :].astype(BF16)


def rpn(before, features, after, w_rpn, w_anchor):
    rows, width, channels = features.shape[1:]
    anchors = w_anchor.shape[1]
    out = pl.pallas_call(
        rpn_kernel,
        out_shape=jax.ShapeDtypeStruct((anchors, rows, width), BF16),
        in_specs=vmem_spec(5),
        out_specs=pl.BlockSpec(memory_space=pltpu.VMEM),
        scratch_shapes=[
            pltpu.VMEM((rows + 2, width, channels), BF16),
            pltpu.VMEM((rows, anchors, width), F32),
        ],
        compiler_params=pltpu.CompilerParams(vmem_limit_bytes=VMEM),
        cost_estimate=pl.CostEstimate(flops=9 * 10**9, bytes_accessed=4 * 10**6, transcendentals=0),
        name="rpn",
    )(before, features[0], after, w_rpn, w_anchor.T)
    return out[None]


def vmem_spec(count):
    return [pl.BlockSpec(memory_space=pltpu.VMEM)] * count


SMEM_SPEC = pl.BlockSpec(memory_space=pltpu.SMEM)


def exchange(array, groups):
    return lax.all_to_all(
        array, "band", split_axis=0, concat_axis=0, tiled=True, axis_index_groups=groups
    )


def dot(left, right, contract):
    return lax.dot_general(left, right, ((contract[:1], contract[1:]), ((), ())), preferred_element_type=F32)


def shift_img(array, step):
    size = lax.axis_size("img")
    return lax.ppermute(array, "img", [(i, (i + step) % size) for i in range(size)])


def collect_kernel(slots_ref, feat_ref, out_ref, picks):
    pixels = feat_ref.shape[0]
    per_head = slots_ref.shape[0]
    heads = picks.shape[0] // per_head
    column = lax.broadcasted_iota(jnp.int32, (per_head, pixels), 1)
    for part in range(slots_ref.shape[1] // heads):
        for k in range(heads):
            at = part * heads + k
            hit = jnp.broadcast_to(slots_ref[:, at : at + 1], (per_head, pixels)) == column
            picks[k * per_head : (k + 1) * per_head, :] = hit.astype(F32).astype(BF16)
        found = dot(picks[...], feat_ref[...], (1, 0)).astype(BF16)
        out_ref[part * heads : (part + 1) * heads] = found.reshape((heads, per_head, found.shape[1]))


def collect(slots, flat):
    per_head, heads = slots.shape
    pixels, channels = flat.shape
    return pl.pallas_call(
        collect_kernel,
        out_shape=jax.ShapeDtypeStruct((heads, per_head, channels), BF16),
        in_specs=vmem_spec(2),
        out_specs=pl.BlockSpec(memory_space=pltpu.VMEM),
        scratch_shapes=[pltpu.VMEM((16 * per_head, pixels), BF16)],
        compiler_params=pltpu.CompilerParams(vmem_limit_bytes=VMEM),
        cost_estimate=pl.CostEstimate(flops=4 * 10**9, bytes_accessed=3 * 10**6, transcendentals=0),
        name="collect",
    )(slots, flat)


def pair_kernel(mine_ref, other_ref, out_ref):
    depth = mine_ref.shape[0]
    out_ref[...] = jnp.zeros_like(out_ref)
    out_ref[:depth, :] = mine_ref[...]
    out_ref[TALL : TALL + depth, :] = other_ref[...]


def pair(mine, other):
    return pl.pallas_call(
        pair_kernel,
        out_shape=jax.ShapeDtypeStruct((TALL + SHORT,) + mine.shape[1:], BF16),
        in_specs=vmem_spec(2),
        out_specs=pl.BlockSpec(memory_space=pltpu.VMEM),
        name="pair",
    )(mine, other)


def partial_kernel(place, x_ref, *refs):
    core, y_at = place[0], place[2]
    weights, out_ref = refs[:NY], refs[NY]
    total = None
    for step in range(NY):
        row = lax.rem(y_at + NY - step, NY)
        for index, side in enumerate((core, 1 - core)):
            start = (side * NY + row) * PITCH
            cols = pl.ds(pl.multiple_of(start, PITCH), PITCH)
            size = (TALL, SHORT)[index]
            weight = weights[step][index * TALL : index * TALL + size, :]
            part = dot(x_ref[:, cols][:, :size], weight, (1, 0))
            total = part if total is None else total + part
    out_ref[...] = total.astype(BF16)


PITCH = 256
TALL, SHORT = 208, 200


def partial_sums(place, x_part, weights):
    return pl.pallas_call(
        partial_kernel,
        out_shape=jax.ShapeDtypeStruct((x_part.shape[0], weights[0].shape[1]), BF16),
        in_specs=[SMEM_SPEC] + vmem_spec(1 + NY),
        out_specs=pl.BlockSpec(memory_space=pltpu.VMEM),
        compiler_params=pltpu.CompilerParams(vmem_limit_bytes=VMEM),
        name="partial_sums",
    )(place, x_part, *weights)


def shift_y(array, step):
    row = NZ * NC
    return lax.ppermute(array, "band", [(b, (b + step * row) % BAND) for b in range(BAND)])


def gelu_parts(value):
    cubic = 0.044715 * (value * value * value)
    tanh = jnp.tanh(0.7978845608028654 * (value + cubic))
    return tanh


def gelu_of(value):
    return 0.5 * value * (1.0 + gelu_parts(value))


def slope_of(value):
    tanh = gelu_parts(value)
    inner = 0.7978845608028654 * (1.0 + 3.0 * 0.044715 * (value * value))
    return 0.5 * (1.0 + tanh) + 0.5 * value * (1.0 - tanh * tanh) * inner


ROW_BLOCK = 128


def order_rows(y_at, x_refs, whole_ref, lanes):
    tall = x_refs[0].shape[0] // NC
    for back, ref in enumerate(x_refs):
        row = lax.rem(y_at + NY - back, NY) * tall
        for side in range(NC):
            at = pl.ds(pl.multiple_of(side * NY * tall + row, tall), tall)
            whole_ref[at, :] = ref[side * tall : (side + 1) * tall, lanes].astype(whole_ref.dtype)


def head_kernel(place, mine_ref, other_ref, fc2_ref, class_ref, da2_ref, *refs):
    sends, (h1, h2, dlog) = refs[:4], refs[4:]
    core, image = place[0], place[1]
    classes = class_ref.shape[0]
    hid = fc2_ref.shape[0]
    for step in range(da2_ref.shape[0] // ROW_BLOCK):
        rows = slice(step * ROW_BLOCK, (step + 1) * ROW_BLOCK)
        steps = mine_ref.shape[0] // ROW_BLOCK
        ref = mine_ref if step < steps else other_ref
        at = step % steps * ROW_BLOCK
        hidden = gelu_of(ref[at : at + ROW_BLOCK, :hid].astype(F32)).astype(BF16)
        h1[rows, :] = hidden
        a2 = dot(hidden, fc2_ref[...], (1, 0))
        second = gelu_of(a2).astype(BF16)
        h2[rows, :] = second
        logits = dot(second, class_ref[...], (1, 1))
        column = lax.broadcasted_iota(jnp.int32, (ROW_BLOCK, classes), 1)
        expo = jnp.exp(logits)
        prob = expo / jnp.sum(expo, axis=1, keepdims=True)
        labels = ref[at : at + ROW_BLOCK, hid:].astype(F32)[:, :1].astype(jnp.int32)
        onehot = (labels == column).astype(F32)
        dlogits = (prob - onehot).astype(BF16)
        dlog[rows, :] = dlogits
        dh2 = dot(dlogits, class_ref[...], (1, 0))
        da2_ref[rows, :] = (dh2 * slope_of(a2)).astype(BF16)
    images = 4
    wide = hid // NC // images
    for step, out in enumerate(sends):
        chunk = lax.rem(image + step, images)
        cols = pl.ds(pl.multiple_of(core * (hid // NC) + chunk * wide, wide), wide)
        out[:, :hid] = dot(h1[:, cols], da2_ref[...], (0, 0)).astype(out.dtype)
        out[:, hid:] = jnp.zeros((wide, out.shape[1] - hid), out.dtype)
        out[:classes, hid:] = dot(dlog[...], h2[:, cols], (0, 0)).astype(out.dtype)


def head(place, mine, other, w_fc2, w_class):
    count, hid = 2 * mine.shape[0], w_fc2.shape[0]
    classes = w_class.shape[1]
    wide = hid // NC // 4
    struct = jax.ShapeDtypeStruct
    return pl.pallas_call(
        head_kernel,
        out_shape=[struct((count, hid), BF16), struct((wide, hid + 128), F32)]
        + [struct((wide, hid + 128), BF16)] * 3,
        in_specs=[SMEM_SPEC] + vmem_spec(4),
        out_specs=vmem_spec(5),
        scratch_shapes=[
            pltpu.VMEM((count, hid), BF16),
            pltpu.VMEM((count, hid), BF16),
            pltpu.VMEM((count, classes), BF16),
        ],
        compiler_params=pltpu.CompilerParams(vmem_limit_bytes=VMEM),
        name="head",
    )(place, mine, other, w_fc2, w_class.T)


def back_kernel(mine_ref, other_ref, da2_ref, fc2_ref, da1_ref):
    count, hid = da2_ref.shape
    for step in range(count // ROW_BLOCK):
        rows = slice(step * ROW_BLOCK, (step + 1) * ROW_BLOCK)
        steps = mine_ref.shape[0] // ROW_BLOCK
        ref = mine_ref if step < steps else other_ref
        at = step % steps * ROW_BLOCK
        dh1 = dot(da2_ref[rows, :], fc2_ref[...], (1, 1))
        da1_ref[rows, :] = (dh1 * slope_of(ref[at : at + ROW_BLOCK, :hid].astype(F32))).astype(BF16)


def back(mine, other, da2, w_fc2):
    return pl.pallas_call(
        back_kernel,
        out_shape=jax.ShapeDtypeStruct(da2.shape, BF16),
        in_specs=vmem_spec(4),
        out_specs=pl.BlockSpec(memory_space=pltpu.VMEM),
        compiler_params=pltpu.CompilerParams(vmem_limit_bytes=VMEM),
        cost_estimate=pl.CostEstimate(flops=2 * 10**9, bytes_accessed=5 * 10**6, transcendentals=0),
        name="back",
    )(mine, other, da2, w_fc2)


def first_kernel(place, da1_ref, *refs):
    image, y_at = place[1], place[2]
    x_refs, outs, rois = refs[:NY], refs[NY : NY + 4], refs[NY + 4]
    order_rows(y_at, x_refs, rois, slice(None))
    images = 4
    wide = da1_ref.shape[1] // images
    depth = outs[0].shape[0]
    for step, out in enumerate(outs):
        chunk = lax.rem(image + step, images)
        cols = pl.ds(pl.multiple_of(chunk * wide, wide), wide)
        out[...] = dot(rois[...], da1_ref[:, cols], (0, 0))[:depth].astype(out.dtype)


def first_layer(place, da1, x_blocks, depth):
    count, hid = da1.shape
    wide = hid // 4
    struct = jax.ShapeDtypeStruct
    return pl.pallas_call(
        first_kernel,
        out_shape=[struct((depth, wide), F32)] + [struct((depth, wide), BF16)] * 3,
        in_specs=[SMEM_SPEC] + vmem_spec(1 + NY),
        out_specs=vmem_spec(4),
        scratch_shapes=[pltpu.VMEM((count, PITCH), BF16)],
        compiler_params=pltpu.CompilerParams(vmem_limit_bytes=VMEM),
        name="first_layer",
    )(place, da1, *x_blocks)


SUM_ROWS = 192


def sum_kernel(*refs):
    heads, firsts, out_ref = refs[:4], refs[4:8], refs[8]
    tall, wide = heads[0].shape
    total = heads[0][...]
    for ref in heads[1:]:
        total = total + ref[...].astype(F32)
    out_ref[:tall, :] = total.astype(BF16)
    first = firsts[0][...]
    for ref in firsts[1:]:
        first = first + ref[...].astype(F32)
    depth, cols = first.shape
    quarter = depth // 4
    rest = jnp.zeros((SUM_ROWS - tall, wide), BF16)
    out_ref[tall:, :] = rest
    for q in range(4):
        part = first[q * quarter : (q + 1) * quarter].astype(BF16)
        out_ref[tall : tall + quarter, q * cols : (q + 1) * cols] = part


def sum_parts(heads, firsts):
    wide = heads[0].shape[1]
    return pl.pallas_call(
        sum_kernel,
        out_shape=jax.ShapeDtypeStruct((SUM_ROWS, wide), BF16),
        in_specs=vmem_spec(8),
        out_specs=pl.BlockSpec(memory_space=pltpu.VMEM),
        compiler_params=pltpu.CompilerParams(vmem_limit_bytes=VMEM),
        name="sum_parts",
    )(*heads, *firsts)


def assemble_kernel(place, *refs):
    core, image = place[0], place[1]
    mine, other = refs[:4], refs[4:8]
    fc1_ref, fc2_ref, class_ref = refs[8:]
    hid = fc2_ref.shape[1]
    images = 4
    classes = class_ref.shape[0]
    tall = other[0].shape[0]
    depth = fc1_ref.shape[0]
    quarter = depth // 4
    wide = hid // images
    for step in range(images):
        chunk = lax.rem(image + images - step, images)
        for side, ref in ((core, mine[step]), (1 - core, other[step])):
            at = pl.ds(pl.multiple_of(side * (hid // NC) + chunk * tall, tall), tall)
            fc2_ref[at, :] = ref[:tall, :hid].astype(F32)
            class_ref[:, at] = ref[:classes, hid:].astype(F32)
        cols = pl.ds(pl.multiple_of(chunk * wide, wide), wide)
        for q in range(4):
            part = mine[step][tall : tall + quarter, q * wide : (q + 1) * wide]
            fc1_ref[q * quarter : (q + 1) * quarter, cols] = part.astype(F32)


def assemble(place, mine, other, depth, classes):
    hid = mine[0].shape[1] - 128
    struct = jax.ShapeDtypeStruct
    return pl.pallas_call(
        assemble_kernel,
        out_shape=[struct((depth, hid), F32), struct((hid, hid), F32), struct((classes, hid), F32)],
        in_specs=[SMEM_SPEC] + vmem_spec(8),
        out_specs=vmem_spec(3),
        compiler_params=pltpu.CompilerParams(vmem_limit_bytes=VMEM),
        name="assemble",
    )(place, *mine, *other)


def shift_all(sent):
    return [shift_img(part, step) for step, part in enumerate(sent, 1)]


def shards(
    features,
    w_rpn,
    w_anchor,
    pixel_slots,
    sample_slot,
    sample_weight,
    roi_labels,
    w_fc1,
    w_fc2,
    w_class,
):
    rows, width, channels = features.shape[1:]
    nband = lax.axis_size("band")
    band, image = lax.axis_index("band"), lax.axis_index("img")
    core = band % NC
    hid = w_fc2.shape[0]
    y_at = band // (NC * NZ)
    place = jnp.stack([core, image, y_at]).astype(jnp.int32)

    flat = features.reshape(rows * width, channels)
    capacity = pixel_slots.shape[3]
    sending = collect(jnp.transpose(pixel_slots[0, :, 0, :]), flat)
    received = lax.all_to_all(sending, "band", split_axis=0, concat_axis=0, tiled=True)

    w_first = lax.optimization_barrier((w_fc1, sending))[0]
    depth = w_first.shape[0]
    w_pair = pair(w_first, lax.ppermute(w_first, "band", CORE_SWAP))
    weights = [w_pair] + [shift_y(w_pair, step) for step in range(1, NY)]
    received, weights = lax.optimization_barrier((received, weights))

    received = received.reshape(nband * capacity, channels).astype(F32)
    roi_count, bins = sample_slot.shape[1:3]
    corner_slots = sample_slot[0].reshape(roi_count * bins, 4)
    corner_weights = sample_weight[0].reshape(roi_count * bins, 4)
    slot_ids = jnp.arange(nband * capacity, dtype=jnp.int32)[None, :]
    pooling = jnp.zeros((roi_count * bins, nband * capacity), F32)
    for corner in range(4):
        hits = (corner_slots[:, corner : corner + 1] == slot_ids).astype(F32)
        pooling = pooling + hits * corner_weights[:, corner : corner + 1]
    pooled = jnp.dot(pooling, received, precision=lax.Precision.HIGHEST, preferred_element_type=F32)
    pooled = pooled.astype(BF16).reshape(roi_count, bins, channels)
    x_local = jnp.transpose(pooled, (0, 2, 1)).reshape(roi_count, nband, depth)
    x_local = jnp.pad(x_local, ((0, 0), (0, 0), (0, PITCH - depth)))
    x_local = x_local.reshape(roi_count, NY, NZ, NC, PITCH).transpose(2, 0, 3, 1, 4)
    x_part = exchange(x_local.reshape(NZ, roi_count, NC * NY * PITCH), Z_GROUPS)
    x_part = x_part.reshape(NZ * roi_count, NC * NY * PITCH)

    across = NY * PITCH
    x_mine = lax.dynamic_slice_in_dim(x_part, core * across, across, 1)
    x_theirs = lax.dynamic_slice_in_dim(x_part, (1 - core) * across, across, 1)
    x_both = jnp.concatenate([x_mine, lax.ppermute(x_theirs, "band", CORE_SWAP)], axis=0)
    partial = partial_sums(place, x_part, weights)
    partial, x_both = lax.optimization_barrier((partial, x_both))
    by_z = exchange(partial.reshape(NZ, roi_count, hid), Z_GROUPS)
    a1_own = jnp.sum(by_z.astype(F32), axis=0).astype(BF16)
    marks = jnp.broadcast_to(roi_labels[0].astype(BF16)[:, None], (roi_count, 128))
    a1_own = jnp.concatenate([a1_own, marks], axis=1)
    a1_z = exchange(jnp.broadcast_to(a1_own[None], (NZ,) + a1_own.shape), Z_GROUPS)
    a1_z = a1_z.reshape(1, NZ * roi_count, hid + 128)
    a1_mine = exchange(jnp.broadcast_to(a1_z, (NY,) + a1_z.shape[1:]), Y_GROUPS)
    a1_mine = a1_mine.reshape(NY * NZ * roi_count, hid + 128)
    a1_other = lax.ppermute(a1_mine, "band", CORE_SWAP)
    classes = w_class.shape[1]
    da2, *parts = head(place, a1_mine, a1_other, w_fc2, w_class)
    head_own, head_got = parts[0], shift_all(parts[1:])
    x_both = lax.optimization_barrier((x_both, da2))[0]
    x_blocks = [lax.dynamic_slice_in_dim(x_both, y_at * PITCH, PITCH, 1)]
    for step in range(1, NY):
        to = (y_at + step) % NY
        x_blocks.append(shift_y(lax.dynamic_slice_in_dim(x_both, to * PITCH, PITCH, 1), step))
    da1 = back(a1_mine, a1_other, da2, w_fc2)
    parts = first_layer(place, da1, x_blocks, depth)
    inner = lax.optimization_barrier((features, parts[0]))[0]
    before, after = halo(inner)
    head_got, parts = lax.optimization_barrier((head_got, parts))
    first_got = shift_all(parts[1:])
    total = sum_parts([head_own] + head_got, [parts[0]] + first_got)
    total, inner = lax.optimization_barrier((total, inner))
    mine = [total] + [shift_img(total, step) for step in range(1, 4)]
    rpn_out = rpn(before, inner, after, w_rpn, w_anchor)
    mine[2], rpn_out = lax.optimization_barrier((mine[2], rpn_out))
    tall = head_own.shape[0]
    other = [lax.ppermute(part[:tall], "band", CORE_SWAP) for part in mine]
    grad_fc1, grad_fc2, grad_class = assemble(place, mine, other, depth, classes)
    return (rpn_out, grad_fc1, grad_fc2, grad_class.T)


def solution(mesh):
    return jax.shard_map(
        shards,
        mesh=mesh,
        in_specs=(
            P("img", "band", None, None),
            P(),
            P(),
            P("img", None, "band", None),
            P("img", "band", None, None),
            P("img", "band", None, None),
            P("img", "band"),
            P("band", None),
            P(),
            P(),
        ),
        out_specs=(P("img", None, "band", None), P("band", None), P(), P()),
        check_vma=False,
    )
```

```python
import functools

import jax
import jax.numpy as jnp
from jax import lax
from jax.experimental import pallas as pl
from jax.experimental.pallas import tpu as pltpu
from jax.sharding import PartitionSpec as P

NY, NZ, NC = 4, 8, 2
BAND = NY * NZ * NC
F32, BF16 = jnp.float32, jnp.bfloat16
CORE_SWAP = [(b, b ^ 1) for b in range(BAND)]
Z_GROUPS = [[(y * NZ + z) * NC + c for z in range(NZ)] for y in range(NY) for c in range(NC)]
Y_GROUPS = [[(y * NZ + z) * NC + c for y in range(NY)] for z in range(NZ) for c in range(NC)]


def halo(array):
    devices = lax.axis_size("band")
    up = [(i, i + 1) for i in range(devices - 1)]
    down = [(j, i) for i, j in up]
    before = lax.ppermute(array[0, -1:], "band", up)
    after = lax.ppermute(array[0, :1], "band", down)
    return before, after


def rpn_kernel(before_ref, feat_ref, after_ref, rpn_ref, anchor_ref, out_ref, rows, held):
    count = feat_ref.shape[0]
    width = feat_ref.shape[1]
    rows[0] = before_ref[0]
    rows[pl.ds(1, count)] = feat_ref[...]
    rows[count + 1] = after_ref[0]

    def line(y, carry):
        sides = []
        for dx in range(3):
            total = dot(rows[y], rpn_ref[0, dx], (1, 0))
            total = total + dot(rows[y + 1], rpn_ref[1, dx], (1, 0))
            sides.append(total + dot(rows[y + 2], rpn_ref[2, dx], (1, 0)))
        place = lax.broadcasted_iota(jnp.int32, sides[0].shape, 0)
        left = jnp.where(place == 0, 0.0, pltpu.roll(sides[0], 1, 0))
        right = jnp.where(place == width - 1, 0.0, pltpu.roll(sides[2], width - 1, 0))
        hidden = jnp.maximum(left + sides[1] + right, 0.0).astype(BF16)
        held[y] = dot(anchor_ref[...], hidden, (1, 1))
        return carry

    lax.fori_loop(0, count, line, 0)
    for y in range(count):
        for a in range(out_ref.shape[0]):
            out_ref[a, y : y + 1, :] = held[y, a : a + 1, :].astype(BF16)


def rpn(before, features, after, w_rpn, w_anchor):
    rows, width, channels = features.shape[1:]
    anchors = w_anchor.shape[1]
    out = pl.pallas_call(
        rpn_kernel,
        out_shape=jax.ShapeDtypeStruct((anchors, rows, width), BF16),
        in_specs=vmem_spec(5),
        out_specs=pl.BlockSpec(memory_space=pltpu.VMEM),
        scratch_shapes=[
            pltpu.VMEM((rows + 2, width, channels), BF16),
            pltpu.VMEM((rows, anchors, width), F32),
        ],
        compiler_params=pltpu.CompilerParams(vmem_limit_bytes=40 * 2**20),
        cost_estimate=pl.CostEstimate(flops=9 * 10**9, bytes_accessed=4 * 10**6, transcendentals=0),
        name="rpn",
    )(before, features[0], after, w_rpn, w_anchor.T)
    return out[None]


def vmem_spec(count):
    return [pl.BlockSpec(memory_space=pltpu.VMEM)] * count


SMEM_SPEC = pl.BlockSpec(memory_space=pltpu.SMEM)


def exchange(array, groups):
    return lax.all_to_all(
        array, "band", split_axis=0, concat_axis=0, tiled=True, axis_index_groups=groups
    )


def dot(left, right, contract):
    return lax.dot_general(left, right, ((contract[:1], contract[1:]), ((), ())), preferred_element_type=F32)


def shift_img(array, step):
    size = lax.axis_size("img")
    return lax.ppermute(array, "img", [(i, (i + step) % size) for i in range(size)])


def collect_kernel(slots_ref, feat_ref, out_ref, picks):
    pixels = feat_ref.shape[0]
    per_head = slots_ref.shape[0]
    heads = picks.shape[0] // per_head
    column = lax.broadcasted_iota(jnp.int32, (per_head, pixels), 1)
    for part in range(slots_ref.shape[1] // heads):
        for k in range(heads):
            at = part * heads + k
            hit = jnp.broadcast_to(slots_ref[:, at : at + 1], (per_head, pixels)) == column
            picks[k * per_head : (k + 1) * per_head, :] = hit.astype(F32).astype(BF16)
        found = dot(picks[...], feat_ref[...], (1, 0)).astype(BF16)
        out_ref[part * heads : (part + 1) * heads] = found.reshape((heads, per_head, found.shape[1]))


def collect(slots, flat):
    per_head, heads = slots.shape
    pixels, channels = flat.shape
    return pl.pallas_call(
        collect_kernel,
        out_shape=jax.ShapeDtypeStruct((heads, per_head, channels), BF16),
        in_specs=vmem_spec(2),
        out_specs=pl.BlockSpec(memory_space=pltpu.VMEM),
        scratch_shapes=[pltpu.VMEM((16 * per_head, pixels), BF16)],
        compiler_params=pltpu.CompilerParams(vmem_limit_bytes=40 * 2**20),
        cost_estimate=pl.CostEstimate(flops=4 * 10**9, bytes_accessed=3 * 10**6, transcendentals=0),
        name="collect",
    )(slots, flat)


def gelu_parts(value):
    cubic = 0.044715 * (value * value * value)
    tanh = jnp.tanh(0.7978845608028654 * (value + cubic))
    return tanh


def gelu_of(value):
    return 0.5 * value * (1.0 + gelu_parts(value))


def slope_of(value):
    tanh = gelu_parts(value)
    inner = 0.7978845608028654 * (1.0 + 3.0 * 0.044715 * (value * value))
    return 0.5 * (1.0 + tanh) + 0.5 * value * (1.0 - tanh * tanh) * inner


ROW_BLOCK = 128


def join_halves(core, mine_ref, other_ref, whole_ref):
    half = mine_ref.shape[1]
    whole_ref[:, pl.ds(pl.multiple_of(core * half, half), half)] = mine_ref[...]
    whole_ref[:, pl.ds(pl.multiple_of((1 - core) * half, half), half)] = other_ref[...]


def head_kernel(place, mine_ref, other_ref, labels_ref, fc2_ref, class_ref, da2_ref, *refs):
    sends, (a1, h1, h2, dlog) = refs[:4], refs[4:]
    core, image = place[0], place[1]
    join_halves(core, mine_ref, other_ref, a1)
    classes = class_ref.shape[0]
    count, hid = a1.shape
    for step in range(count // ROW_BLOCK):
        rows = slice(step * ROW_BLOCK, (step + 1) * ROW_BLOCK)
        hidden = gelu_of(a1[rows, :].astype(F32)).astype(BF16)
        h1[rows, :] = hidden
        a2 = dot(hidden, fc2_ref[...], (1, 0))
        second = gelu_of(a2).astype(BF16)
        h2[rows, :] = second
        logits = dot(second, class_ref[...], (1, 1))
        column = lax.broadcasted_iota(jnp.int32, (ROW_BLOCK, classes), 1)
        expo = jnp.exp(logits)
        prob = expo / jnp.sum(expo, axis=1, keepdims=True)
        onehot = (labels_ref[rows, :] == column).astype(F32)
        dlogits = (prob - onehot).astype(BF16)
        dlog[rows, :] = dlogits
        dh2 = dot(dlogits, class_ref[...], (1, 0))
        da2_ref[rows, :] = (dh2 * slope_of(a2)).astype(BF16)
    images = 4
    wide = hid // NC // images
    for step, out in enumerate(sends):
        chunk = lax.rem(image + step, images)
        cols = pl.ds(pl.multiple_of(core * (hid // NC) + chunk * wide, wide), wide)
        out[:, :hid] = dot(h1[:, cols], da2_ref[...], (0, 0)).astype(out.dtype)
        out[:, hid:] = jnp.zeros((wide, out.shape[1] - hid), out.dtype)
        out[:classes, hid:] = dot(dlog[...], h2[:, cols], (0, 0)).astype(out.dtype)


def head(place, mine, other, labels, w_fc2, w_class):
    count, half = mine.shape
    hid = w_fc2.shape[0]
    classes = w_class.shape[1]
    wide = half // 4
    struct = jax.ShapeDtypeStruct
    return pl.pallas_call(
        head_kernel,
        out_shape=[struct((count, hid), BF16), struct((wide, hid + 128), F32)]
        + [struct((wide, hid + 128), BF16)] * 3,
        in_specs=[SMEM_SPEC] + vmem_spec(5),
        out_specs=vmem_spec(5),
        scratch_shapes=[
            pltpu.VMEM((count, hid), BF16),
            pltpu.VMEM((count, hid), BF16),
            pltpu.VMEM((count, hid), BF16),
            pltpu.VMEM((count, classes), BF16),
        ],
        compiler_params=pltpu.CompilerParams(vmem_limit_bytes=40 * 2**20),
        name="head",
    )(place, mine, other, labels, w_fc2, w_class.T)


def first_kernel(place, mine_ref, other_ref, da2_ref, fc2_ref, x_ref,
                 own_ref, s1_ref, s2_ref, s3_ref, a1, da1):
    core, image = place[0], place[1]
    join_halves(core, mine_ref, other_ref, a1)
    count, hid = a1.shape

    for step in range(count // ROW_BLOCK):
        rows = slice(step * ROW_BLOCK, (step + 1) * ROW_BLOCK)
        dh1 = dot(da2_ref[rows, :], fc2_ref[...], (1, 1))
        da1[rows, :] = (dh1 * slope_of(a1[rows, :].astype(F32))).astype(BF16)
    images = 4
    wide = hid // images
    for step, out in enumerate((own_ref, s1_ref, s2_ref, s3_ref)):
        chunk = lax.rem(image + step, images)
        cols = pl.ds(pl.multiple_of(chunk * wide, wide), wide)
        out[...] = dot(x_ref[...], da1[:, cols], (0, 0)).astype(out.dtype)


def first_layer(place, mine, other, da2, w_fc2, x_cols):
    count, hid = da2.shape
    depth = x_cols.shape[1]
    wide = hid // 4
    struct = jax.ShapeDtypeStruct
    return pl.pallas_call(
        first_kernel,
        out_shape=[struct((depth, wide), F32)] + [struct((depth, wide), BF16)] * 3,
        in_specs=[SMEM_SPEC] + vmem_spec(5),
        out_specs=vmem_spec(4),
        scratch_shapes=[pltpu.VMEM((count, hid), BF16), pltpu.VMEM((count, hid), BF16)],
        compiler_params=pltpu.CompilerParams(vmem_limit_bytes=40 * 2**20),
        name="first_layer",
    )(place, mine, other, da2, w_fc2, x_cols)


SUM_ROWS = 192


def sum_kernel(*refs):
    heads, firsts, out_ref = refs[:4], refs[4:8], refs[8]
    tall, wide = heads[0].shape
    total = heads[0][...]
    for ref in heads[1:]:
        total = total + ref[...].astype(F32)
    out_ref[:tall, :] = total.astype(BF16)
    first = firsts[0][...]
    for ref in firsts[1:]:
        first = first + ref[...].astype(F32)
    depth, cols = first.shape
    quarter = depth // 4
    rest = jnp.zeros((SUM_ROWS - tall, wide), BF16)
    out_ref[tall:, :] = rest
    for q in range(4):
        part = first[q * quarter : (q + 1) * quarter].astype(BF16)
        out_ref[tall : tall + quarter, q * cols : (q + 1) * cols] = part


def sum_parts(heads, firsts):
    wide = heads[0].shape[1]
    return pl.pallas_call(
        sum_kernel,
        out_shape=jax.ShapeDtypeStruct((SUM_ROWS, wide), BF16),
        in_specs=vmem_spec(8),
        out_specs=pl.BlockSpec(memory_space=pltpu.VMEM),
        compiler_params=pltpu.CompilerParams(vmem_limit_bytes=40 * 2**20),
        name="sum_parts",
    )(*heads, *firsts)


def assemble_kernel(place, *refs):
    core, image = place[0], place[1]
    mine, other = refs[:4], refs[4:8]
    fc1_ref, fc2_ref, class_ref = refs[8:]
    hid = fc2_ref.shape[1]
    images = 4
    classes = class_ref.shape[0]
    tall = other[0].shape[0]
    depth = fc1_ref.shape[0]
    quarter = depth // 4
    wide = hid // images
    for step in range(images):
        chunk = lax.rem(image + images - step, images)
        for side, ref in ((core, mine[step]), (1 - core, other[step])):
            at = pl.ds(pl.multiple_of(side * (hid // NC) + chunk * tall, tall), tall)
            fc2_ref[at, :] = ref[:tall, :hid].astype(F32)
            class_ref[:, at] = ref[:classes, hid:].astype(F32)
        cols = pl.ds(pl.multiple_of(chunk * wide, wide), wide)
        for q in range(4):
            part = mine[step][tall : tall + quarter, q * wide : (q + 1) * wide]
            fc1_ref[q * quarter : (q + 1) * quarter, cols] = part.astype(F32)


def assemble(place, mine, other, depth, classes):
    hid = mine[0].shape[1] - 128
    struct = jax.ShapeDtypeStruct
    return pl.pallas_call(
        assemble_kernel,
        out_shape=[struct((depth, hid), F32), struct((hid, hid), F32), struct((classes, hid), F32)],
        in_specs=[SMEM_SPEC] + vmem_spec(8),
        out_specs=vmem_spec(3),
        compiler_params=pltpu.CompilerParams(vmem_limit_bytes=40 * 2**20),
        name="assemble",
    )(place, *mine, *other)


def shift_all(sent):
    return [shift_img(part, step) for step, part in enumerate(sent, 1)]


def shards(
    features,
    w_rpn,
    w_anchor,
    pixel_slots,
    sample_slot,
    sample_weight,
    roi_labels,
    w_fc1,
    w_fc2,
    w_class,
):
    rows, width, channels = features.shape[1:]
    nband = lax.axis_size("band")
    band, image = lax.axis_index("band"), lax.axis_index("img")
    core = band % NC
    hid = w_fc2.shape[0]
    half = hid // NC
    place = jnp.stack([core, image]).astype(jnp.int32)

    flat = features.reshape(rows * width, channels)
    capacity = pixel_slots.shape[3]
    sending = collect(jnp.transpose(pixel_slots[0, :, 0, :]), flat)
    received = lax.all_to_all(sending, "band", split_axis=0, concat_axis=0, tiled=True)

    w_first, edges = lax.optimization_barrier((w_fc1, features, sending))[:2]
    before, after = halo(edges)
    w_mine = lax.dynamic_slice_in_dim(w_first, core * half, half, 1)
    w_theirs = lax.dynamic_slice_in_dim(w_first, (1 - core) * half, half, 1)
    w_other = lax.ppermute(w_theirs, "band", CORE_SWAP)
    received, w_other, before, after = lax.optimization_barrier((received, w_other, before, after))

    received = received.reshape(nband * capacity, channels).astype(F32)
    roi_count, bins = sample_slot.shape[1:3]
    corner_slots = sample_slot[0].reshape(roi_count * bins, 4)
    corner_weights = sample_weight[0].reshape(roi_count * bins, 4)
    slot_ids = jnp.arange(nband * capacity, dtype=jnp.int32)[None, :]
    pooling = jnp.zeros((roi_count * bins, nband * capacity), F32)
    for corner in range(4):
        hits = (corner_slots[:, corner : corner + 1] == slot_ids).astype(F32)
        pooling = pooling + hits * corner_weights[:, corner : corner + 1]
    pooled = jnp.dot(pooling, received, precision=lax.Precision.HIGHEST, preferred_element_type=F32)
    pooled = pooled.astype(BF16).reshape(roi_count, bins, channels)
    depth = w_fc1.shape[0]
    x_local = jnp.transpose(pooled, (0, 2, 1)).reshape(roi_count, nband, depth)
    label_column = jnp.broadcast_to(roi_labels[0].astype(BF16)[:, None, None], (roi_count, nband, 1))
    x_local = jnp.concatenate([x_local, label_column], axis=2).reshape(roi_count, nband * (depth + 1))
    x_cols = lax.all_to_all(x_local, "band", split_axis=1, concat_axis=0, tiled=True)
    labels = x_cols[:, depth:].astype(jnp.int32)
    x_cols = x_cols[:, :depth]

    x_other = lax.ppermute(x_cols, "band", CORE_SWAP)
    partial = dot(x_cols, w_mine, (1, 0)) + dot(x_other, w_other, (1, 0))
    count = x_cols.shape[0]
    by_y = exchange(partial.astype(BF16).reshape(NY, count // NY, half), Y_GROUPS)
    by_y = jnp.sum(by_y.astype(F32), axis=0).astype(BF16)
    by_z = exchange(by_y.reshape(NZ, count // NY // NZ, half), Z_GROUPS)
    a1_own = jnp.sum(by_z.astype(F32), axis=0).astype(BF16)
    a1_z = exchange(jnp.broadcast_to(a1_own[None], (NZ,) + a1_own.shape), Z_GROUPS)
    a1_z = a1_z.reshape(1, count // NY, half)
    a1_mine = exchange(jnp.broadcast_to(a1_z, (NY,) + a1_z.shape[1:]), Y_GROUPS).reshape(count, half)
    a1_other = lax.ppermute(a1_mine, "band", CORE_SWAP)
    classes = w_class.shape[1]
    da2, *parts = head(place, a1_mine, a1_other, labels, w_fc2, w_class)
    head_own, head_got = parts[0], shift_all(parts[1:])
    parts = first_layer(place, a1_mine, a1_other, da2, w_fc2, x_cols)
    first_got = [shift_img(parts[1], 1), None, shift_img(parts[3], 3)]
    held, head_got[0], head_got[2] = lax.optimization_barrier((parts[2], head_got[0], head_got[2]))
    first_got[1] = shift_img(held, 2)
    total = sum_parts([head_own] + head_got, [parts[0]] + first_got)
    total, inner = lax.optimization_barrier((total, features))
    mine = [total] + [shift_img(total, step) for step in range(1, 4)]
    rpn_out = rpn(before, inner, after, w_rpn, w_anchor)
    mine[2], rpn_out = lax.optimization_barrier((mine[2], rpn_out))
    tall = head_own.shape[0]
    other = [lax.ppermute(part[:tall], "band", CORE_SWAP) for part in mine]
    grad_fc1, grad_fc2, grad_class = assemble(place, mine, other, depth, classes)
    return (rpn_out, grad_fc1, grad_fc2, grad_class.T)


def solution(mesh):
    return jax.shard_map(
        shards,
        mesh=mesh,
        in_specs=(
            P("img", "band", None, None),
            P(),
            P(),
            P("img", None, "band", None),
            P("img", "band", None, None),
            P("img", "band", None, None),
            P("img", "band"),
            P("band", None),
            P(),
            P(),
        ),
        out_specs=(P("img", None, "band", None), P("band", None), P(), P()),
        check_vma=False,
    )
```

```python
import functools

import jax
import jax.numpy as jnp
from jax import lax
from jax.experimental import pallas as pl
from jax.experimental.pallas import tpu as pltpu
from jax.sharding import PartitionSpec as P

NY, NZ, NC = 4, 8, 2
BAND = NY * NZ * NC
F32, BF16 = jnp.float32, jnp.bfloat16
VMEM = 40 * 2**20
CORE_SWAP = [(b, b ^ 1) for b in range(BAND)]
Z_GROUPS = [[(y * NZ + z) * NC + c for z in range(NZ)] for y in range(NY) for c in range(NC)]
ZC_GROUPS = [[y * NZ * NC + k for k in range(NZ * NC)] for y in range(NY)]
Y_GROUPS = [[(y * NZ + z) * NC + c for y in range(NY)] for z in range(NZ) for c in range(NC)]


def halo(array):
    devices = lax.axis_size("band")
    up = [(i, i + 1) for i in range(devices - 1)]
    down = [(j, i) for i, j in up]
    before = lax.ppermute(array[0, -1:], "band", up)
    after = lax.ppermute(array[0, :1], "band", down)
    return before, after


def rpn_kernel(before_ref, feat_ref, after_ref, rpn_ref, anchor_ref, out_ref, rows, held):
    count = feat_ref.shape[0]
    width = feat_ref.shape[1]
    rows[0] = before_ref[0]
    rows[pl.ds(1, count)] = feat_ref[...]
    rows[count + 1] = after_ref[0]

    def line(y, carry):
        sides = []
        for dx in range(3):
            total = dot(rows[y], rpn_ref[0, dx], (1, 0))
            total = total + dot(rows[y + 1], rpn_ref[1, dx], (1, 0))
            sides.append(total + dot(rows[y + 2], rpn_ref[2, dx], (1, 0)))
        place = lax.broadcasted_iota(jnp.int32, sides[0].shape, 0)
        left = jnp.where(place == 0, 0.0, pltpu.roll(sides[0], 1, 0))
        right = jnp.where(place == width - 1, 0.0, pltpu.roll(sides[2], width - 1, 0))
        hidden = jnp.maximum(left + sides[1] + right, 0.0).astype(BF16)
        held[y] = dot(anchor_ref[...], hidden, (1, 1))
        return carry

    lax.fori_loop(0, count, line, 0)
    for y in range(count):
        for a in range(out_ref.shape[0]):
            out_ref[a, y : y + 1, :] = held[y, a : a + 1, :].astype(BF16)


def rpn(before, features, after, w_rpn, w_anchor):
    rows, width, channels = features.shape[1:]
    anchors = w_anchor.shape[1]
    out = pl.pallas_call(
        rpn_kernel,
        out_shape=jax.ShapeDtypeStruct((anchors, rows, width), BF16),
        in_specs=vmem_spec(5),
        out_specs=pl.BlockSpec(memory_space=pltpu.VMEM),
        scratch_shapes=[
            pltpu.VMEM((rows + 2, width, channels), BF16),
            pltpu.VMEM((rows, anchors, width), F32),
        ],
        compiler_params=pltpu.CompilerParams(vmem_limit_bytes=VMEM),
        cost_estimate=pl.CostEstimate(flops=9 * 10**9, bytes_accessed=4 * 10**6, transcendentals=0),
        name="rpn",
    )(before, features[0], after, w_rpn, w_anchor.T)
    return out[None]


def vmem_spec(count):
    return [pl.BlockSpec(memory_space=pltpu.VMEM)] * count


SMEM_SPEC = pl.BlockSpec(memory_space=pltpu.SMEM)


def exchange(array, groups):
    return lax.all_to_all(
        array, "band", split_axis=0, concat_axis=0, tiled=True, axis_index_groups=groups
    )


def dot(left, right, contract):
    return lax.dot_general(left, right, ((contract[:1], contract[1:]), ((), ())), preferred_element_type=F32)


def shift_img(array, step):
    size = lax.axis_size("img")
    return lax.ppermute(array, "img", [(i, (i + step) % size) for i in range(size)])


def collect_kernel(slots_ref, feat_ref, out_ref, picks):
    pixels = feat_ref.shape[0]
    per_head = slots_ref.shape[0]
    heads = picks.shape[0] // per_head
    column = lax.broadcasted_iota(jnp.int32, (per_head, pixels), 1)
    for part in range(slots_ref.shape[1] // heads):
        for k in range(heads):
            at = part * heads + k
            hit = jnp.broadcast_to(slots_ref[:, at : at + 1], (per_head, pixels)) == column
            picks[k * per_head : (k + 1) * per_head, :] = hit.astype(F32).astype(BF16)
        found = dot(picks[...], feat_ref[...], (1, 0)).astype(BF16)
        out_ref[part * heads : (part + 1) * heads] = found.reshape((heads, per_head, found.shape[1]))


def collect(slots, flat):
    per_head, heads = slots.shape
    pixels, channels = flat.shape
    return pl.pallas_call(
        collect_kernel,
        out_shape=jax.ShapeDtypeStruct((heads, per_head, channels), BF16),
        in_specs=vmem_spec(2),
        out_specs=pl.BlockSpec(memory_space=pltpu.VMEM),
        scratch_shapes=[pltpu.VMEM((16 * per_head, pixels), BF16)],
        compiler_params=pltpu.CompilerParams(vmem_limit_bytes=VMEM),
        cost_estimate=pl.CostEstimate(flops=4 * 10**9, bytes_accessed=3 * 10**6, transcendentals=0),
        name="collect",
    )(slots, flat)


PITCH = 256
SHORT = 200


def halves_kernel(place, *refs):
    core = place[0]
    sources, keep_ref, send_ref = refs[:NY], refs[NY], refs[NY + 1]
    depth = sources[0].shape[0]
    wide = keep_ref.shape[1]
    for ref, side in ((keep_ref, core), (send_ref, 1 - core)):
        ref[...] = jnp.zeros_like(ref)
        for k, source in enumerate(sources):
            cols = pl.ds(pl.multiple_of(side * wide, wide), wide)
            ref[k * SHORT : k * SHORT + depth, :] = source[:, cols]


def halves(place, slices):
    shape = (NY * SHORT + 8, slices[0].shape[1] // NC)
    return pl.pallas_call(
        halves_kernel,
        out_shape=[jax.ShapeDtypeStruct(shape, BF16)] * 2,
        in_specs=[SMEM_SPEC] + vmem_spec(NY),
        out_specs=vmem_spec(2),
        compiler_params=pltpu.CompilerParams(vmem_limit_bytes=VMEM),
        name="halves",
    )(place, *slices)


def partial_kernel(place, mine_ref, other_ref, keep_ref, got_ref, out_ref):
    y_at = place[2]
    total = None
    for step in range(NY):
        start = lax.rem(y_at + NY - step, NY) * PITCH
        cols = pl.ds(pl.multiple_of(start, PITCH), PITCH)
        rows = slice(step * SHORT, (step + 1) * SHORT)
        for ref, weight in ((mine_ref, keep_ref), (other_ref, got_ref)):
            part = dot(ref[:, cols][:, :SHORT], weight[rows, :], (1, 0))
            total = part if total is None else total + part
    out_ref[...] = total.astype(BF16)


def partial_sums(place, mine, other, keep, got):
    return pl.pallas_call(
        partial_kernel,
        out_shape=jax.ShapeDtypeStruct((mine.shape[0], keep.shape[1]), BF16),
        in_specs=[SMEM_SPEC] + vmem_spec(4),
        out_specs=pl.BlockSpec(memory_space=pltpu.VMEM),
        compiler_params=pltpu.CompilerParams(vmem_limit_bytes=VMEM),
        name="partial_sums",
    )(place, mine, other, keep, got)


def shift_y(array, step):
    row = NZ * NC
    return lax.ppermute(array, "band", [(b, (b + step * row) % BAND) for b in range(BAND)])


def gelu_parts(value):
    cubic = 0.044715 * (value * value * value)
    tanh = jnp.tanh(0.7978845608028654 * (value + cubic))
    return tanh


def gelu_of(value):
    return 0.5 * value * (1.0 + gelu_parts(value))


def slope_of(value):
    tanh = gelu_parts(value)
    inner = 0.7978845608028654 * (1.0 + 3.0 * 0.044715 * (value * value))
    return 0.5 * (1.0 + tanh) + 0.5 * value * (1.0 - tanh * tanh) * inner


ROW_BLOCK = 128


def join_halves(core, mine_ref, other_ref, whole_ref):
    half = whole_ref.shape[1] // NC
    whole_ref[:, pl.ds(pl.multiple_of(core * half, half), half)] = mine_ref[:, :half]
    whole_ref[:, pl.ds(pl.multiple_of((1 - core) * half, half), half)] = other_ref[:, :half]


def head_kernel(place, mine_ref, other_ref, fc2_ref, class_ref, da2_ref, *refs):
    sends, (a1, h1, h2, dlog) = refs[:4], refs[4:]
    core, image = place[0], place[1]
    join_halves(core, mine_ref, other_ref, a1)
    classes = class_ref.shape[0]
    count, hid = a1.shape
    for step in range(count // ROW_BLOCK):
        rows = slice(step * ROW_BLOCK, (step + 1) * ROW_BLOCK)
        hidden = gelu_of(a1[rows, :].astype(F32)).astype(BF16)
        h1[rows, :] = hidden
        a2 = dot(hidden, fc2_ref[...], (1, 0))
        second = gelu_of(a2).astype(BF16)
        h2[rows, :] = second
        logits = dot(second, class_ref[...], (1, 1))
        column = lax.broadcasted_iota(jnp.int32, (ROW_BLOCK, classes), 1)
        expo = jnp.exp(logits)
        prob = expo / jnp.sum(expo, axis=1, keepdims=True)
        labels = mine_ref[rows, hid // NC :].astype(F32)[:, :1].astype(jnp.int32)
        onehot = (labels == column).astype(F32)
        dlogits = (prob - onehot).astype(BF16)
        dlog[rows, :] = dlogits
        dh2 = dot(dlogits, class_ref[...], (1, 0))
        da2_ref[rows, :] = (dh2 * slope_of(a2)).astype(BF16)
    images = 4
    wide = hid // NC // images
    for step, out in enumerate(sends):
        chunk = lax.rem(image + step, images)
        cols = pl.ds(pl.multiple_of(core * (hid // NC) + chunk * wide, wide), wide)
        out[:, :hid] = dot(h1[:, cols], da2_ref[...], (0, 0)).astype(out.dtype)
        out[:, hid:] = jnp.zeros((wide, out.shape[1] - hid), out.dtype)
        out[:classes, hid:] = dot(dlog[...], h2[:, cols], (0, 0)).astype(out.dtype)


def head(place, mine, other, w_fc2, w_class):
    count, half = mine.shape[0], w_fc2.shape[0] // NC
    hid = w_fc2.shape[0]
    classes = w_class.shape[1]
    wide = half // 4
    struct = jax.ShapeDtypeStruct
    return pl.pallas_call(
        head_kernel,
        out_shape=[struct((count, hid), BF16), struct((wide, hid + 128), F32)]
        + [struct((wide, hid + 128), BF16)] * 3,
        in_specs=[SMEM_SPEC] + vmem_spec(4),
        out_specs=vmem_spec(5),
        scratch_shapes=[
            pltpu.VMEM((count, hid), BF16),
            pltpu.VMEM((count, hid), BF16),
            pltpu.VMEM((count, hid), BF16),
            pltpu.VMEM((count, classes), BF16),
        ],
        compiler_params=pltpu.CompilerParams(vmem_limit_bytes=VMEM),
        name="head",
    )(place, mine, other, w_fc2, w_class.T)


def back_kernel(place, mine_ref, other_ref, da2_ref, fc2_ref, da1_ref, a1):
    join_halves(place[0], mine_ref, other_ref, a1)
    for step in range(a1.shape[0] // ROW_BLOCK):
        rows = slice(step * ROW_BLOCK, (step + 1) * ROW_BLOCK)
        dh1 = dot(da2_ref[rows, :], fc2_ref[...], (1, 1))
        da1_ref[rows, :] = (dh1 * slope_of(a1[rows, :].astype(F32))).astype(BF16)


def back(place, mine, other, da2, w_fc2):
    return pl.pallas_call(
        back_kernel,
        out_shape=jax.ShapeDtypeStruct(da2.shape, BF16),
        in_specs=[SMEM_SPEC] + vmem_spec(4),
        out_specs=pl.BlockSpec(memory_space=pltpu.VMEM),
        scratch_shapes=[pltpu.VMEM(da2.shape, BF16)],
        compiler_params=pltpu.CompilerParams(vmem_limit_bytes=VMEM),
        cost_estimate=pl.CostEstimate(flops=2 * 10**9, bytes_accessed=5 * 10**6, transcendentals=0),
        name="back",
    )(place, mine, other, da2, w_fc2)


def first_kernel(place, da1_ref, *refs):
    image, y_at = place[1], place[2]
    x_refs, outs, rois = refs[:NY], refs[NY : NY + 4], refs[NY + 4]
    tall = x_refs[0].shape[0]
    for step, ref in enumerate(x_refs):
        start = lax.rem(y_at + NY - step, NY) * tall
        rois[pl.ds(pl.multiple_of(start, tall), tall), :] = ref[...]
    images = 4
    wide = da1_ref.shape[1] // images
    depth = outs[0].shape[0]
    for step, out in enumerate(outs):
        chunk = lax.rem(image + step, images)
        cols = pl.ds(pl.multiple_of(chunk * wide, wide), wide)
        out[...] = dot(rois[...], da1_ref[:, cols], (0, 0))[:depth].astype(out.dtype)


def first_layer(place, da1, x_blocks, depth):
    count, hid = da1.shape
    wide = hid // 4
    struct = jax.ShapeDtypeStruct
    return pl.pallas_call(
        first_kernel,
        out_shape=[struct((depth, wide), F32)] + [struct((depth, wide), BF16)] * 3,
        in_specs=[SMEM_SPEC] + vmem_spec(1 + NY),
        out_specs=vmem_spec(4),
        scratch_shapes=[pltpu.VMEM((count, PITCH), BF16)],
        compiler_params=pltpu.CompilerParams(vmem_limit_bytes=VMEM),
        name="first_layer",
    )(place, da1, *x_blocks)


SUM_ROWS = 192


def sum_kernel(*refs):
    heads, firsts, out_ref = refs[:4], refs[4:8], refs[8]
    tall, wide = heads[0].shape
    total = heads[0][...]
    for ref in heads[1:]:
        total = total + ref[...].astype(F32)
    out_ref[:tall, :] = total.astype(BF16)
    first = firsts[0][...]
    for ref in firsts[1:]:
        first = first + ref[...].astype(F32)
    depth, cols = first.shape
    quarter = depth // 4
    rest = jnp.zeros((SUM_ROWS - tall, wide), BF16)
    out_ref[tall:, :] = rest
    for q in range(4):
        part = first[q * quarter : (q + 1) * quarter].astype(BF16)
        out_ref[tall : tall + quarter, q * cols : (q + 1) * cols] = part


def sum_parts(heads, firsts):
    wide = heads[0].shape[1]
    return pl.pallas_call(
        sum_kernel,
        out_shape=jax.ShapeDtypeStruct((SUM_ROWS, wide), BF16),
        in_specs=vmem_spec(8),
        out_specs=pl.BlockSpec(memory_space=pltpu.VMEM),
        compiler_params=pltpu.CompilerParams(vmem_limit_bytes=VMEM),
        name="sum_parts",
    )(*heads, *firsts)


def assemble_kernel(place, *refs):
    core, image = place[0], place[1]
    mine, other = refs[:4], refs[4:8]
    fc1_ref, fc2_ref, class_ref = refs[8:]
    hid = fc2_ref.shape[1]
    images = 4
    classes = class_ref.shape[0]
    tall = other[0].shape[0]
    depth = fc1_ref.shape[0]
    quarter = depth // 4
    wide = hid // images
    for step in range(images):
        chunk = lax.rem(image + images - step, images)
        for side, ref in ((core, mine[step]), (1 - core, other[step])):
            at = pl.ds(pl.multiple_of(side * (hid // NC) + chunk * tall, tall), tall)
            fc2_ref[at, :] = ref[:tall, :hid].astype(F32)
            class_ref[:, at] = ref[:classes, hid:].astype(F32)
        cols = pl.ds(pl.multiple_of(chunk * wide, wide), wide)
        for q in range(4):
            part = mine[step][tall : tall + quarter, q * wide : (q + 1) * wide]
            fc1_ref[q * quarter : (q + 1) * quarter, cols] = part.astype(F32)


def assemble(place, mine, other, depth, classes):
    hid = mine[0].shape[1] - 128
    struct = jax.ShapeDtypeStruct
    return pl.pallas_call(
        assemble_kernel,
        out_shape=[struct((depth, hid), F32), struct((hid, hid), F32), struct((classes, hid), F32)],
        in_specs=[SMEM_SPEC] + vmem_spec(8),
        out_specs=vmem_spec(3),
        compiler_params=pltpu.CompilerParams(vmem_limit_bytes=VMEM),
        name="assemble",
    )(place, *mine, *other)


def shift_all(sent):
    return [shift_img(part, step) for step, part in enumerate(sent, 1)]


def shards(
    features,
    w_rpn,
    w_anchor,
    pixel_slots,
    sample_slot,
    sample_weight,
    roi_labels,
    w_fc1,
    w_fc2,
    w_class,
):
    rows, width, channels = features.shape[1:]
    nband = lax.axis_size("band")
    band, image = lax.axis_index("band"), lax.axis_index("img")
    core = band % NC
    hid = w_fc2.shape[0]
    half = hid // NC
    y_at = band // (NC * NZ)
    place = jnp.stack([core, image, y_at]).astype(jnp.int32)

    flat = features.reshape(rows * width, channels)
    capacity = pixel_slots.shape[3]
    sending = collect(jnp.transpose(pixel_slots[0, :, 0, :]), flat)
    received = lax.all_to_all(sending, "band", split_axis=0, concat_axis=0, tiled=True)

    depth = w_fc1.shape[0]
    w_first, edges, labels = lax.optimization_barrier((w_fc1, features, roi_labels, sending))[:3]
    slices = [w_first] + [shift_y(w_first, step) for step in range(1, NY)]
    before, after = halo(edges)
    marks = jnp.broadcast_to(labels[0].astype(BF16)[:, None], (labels.shape[1], 128))
    others = lax.ppermute(marks, "band", CORE_SWAP)
    marks = jnp.where(core == 0, jnp.concatenate([marks, others]), jnp.concatenate([others, marks]))

    received = received.reshape(nband * capacity, channels).astype(F32)
    roi_count, bins = sample_slot.shape[1:3]
    corner_slots = sample_slot[0].reshape(roi_count * bins, 4)
    corner_weights = sample_weight[0].reshape(roi_count * bins, 4)
    slot_ids = jnp.arange(nband * capacity, dtype=jnp.int32)[None, :]
    pooling = jnp.zeros((roi_count * bins, nband * capacity), F32)
    for corner in range(4):
        hits = (corner_slots[:, corner : corner + 1] == slot_ids).astype(F32)
        pooling = pooling + hits * corner_weights[:, corner : corner + 1]
    pooled = jnp.dot(pooling, received, precision=lax.Precision.HIGHEST, preferred_element_type=F32)
    pooled = pooled.astype(BF16).reshape(roi_count, bins, channels)
    x_local = jnp.transpose(pooled, (0, 2, 1)).reshape(roi_count, nband, depth)
    x_local = jnp.pad(x_local, ((0, 0), (0, 0), (0, PITCH - depth)))
    x_local = x_local.reshape(roi_count, NY, NZ * NC, PITCH).transpose(2, 0, 1, 3)
    x_local, slices, before, after, marks = lax.optimization_barrier(
        (x_local, slices, before, after, marks)
    )
    keep, send = halves(place, slices)
    got = lax.ppermute(send, "band", CORE_SWAP)
    x_part = exchange(x_local.reshape(NZ * NC, roi_count, NY * PITCH), ZC_GROUPS)
    x_part = x_part.reshape(NZ * NC * roi_count, NY * PITCH)

    x_other = lax.ppermute(x_part, "band", CORE_SWAP)
    partial = partial_sums(place, x_part, x_other, keep, got)
    count = roi_count * nband
    by_z = exchange(partial.reshape(NZ, count // NY // NZ, half), Z_GROUPS)
    a1_own = jnp.sum(by_z.astype(F32), axis=0).astype(BF16)
    a1_own = jnp.concatenate([a1_own, marks], axis=1)
    a1_z = exchange(jnp.broadcast_to(a1_own[None], (NZ,) + a1_own.shape), Z_GROUPS)
    a1_z = a1_z.reshape(1, count // NY, half + 128)
    a1_mine = exchange(jnp.broadcast_to(a1_z, (NY,) + a1_z.shape[1:]), Y_GROUPS)
    a1_mine = a1_mine.reshape(count, half + 128)
    a1_other = lax.ppermute(a1_mine, "band", CORE_SWAP)
    da2, *parts = head(place, a1_mine, a1_other, w_fc2, w_class)
    head_own, head_got = parts[0], shift_all(parts[1:])
    x_part = lax.optimization_barrier((x_part, da2))[0]
    x_blocks = [lax.dynamic_slice_in_dim(x_part, y_at * PITCH, PITCH, 1)]
    for step in range(1, NY):
        to = (y_at + step) % NY
        x_blocks.append(shift_y(lax.dynamic_slice_in_dim(x_part, to * PITCH, PITCH, 1), step))
    da1 = back(place, a1_mine, a1_other, da2, w_fc2)
    parts = first_layer(place, da1, x_blocks, depth)
    first_got = [shift_img(parts[1], 1), None, shift_img(parts[3], 3)]
    held, head_got[0], head_got[2] = lax.optimization_barrier((parts[2], head_got[0], head_got[2]))
    first_got[1] = shift_img(held, 2)
    total = sum_parts([head_own] + head_got, [parts[0]] + first_got)
    total, inner = lax.optimization_barrier((total, features))
    mine = [total] + [shift_img(total, step) for step in range(1, 4)]
    rpn_out = rpn(before, inner, after, w_rpn, w_anchor)
    mine[2], rpn_out = lax.optimization_barrier((mine[2], rpn_out))
    tall = head_own.shape[0]
    other = [lax.ppermute(part[:tall], "band", CORE_SWAP) for part in mine]
    grad_fc1, grad_fc2, grad_class = assemble(place, mine, other, depth, w_class.shape[1])
    return (rpn_out, grad_fc1, grad_fc2, grad_class.T)


def solution(mesh):
    return jax.shard_map(
        shards,
        mesh=mesh,
        in_specs=(
            P("img", "band", None, None),
            P(),
            P(),
            P("img", None, "band", None),
            P("img", "band", None, None),
            P("img", "band", None, None),
            P("img", "band"),
            P("band", None),
            P(),
            P(),
        ),
        out_specs=(P("img", None, "band", None), P("band", None), P(), P()),
        check_vma=False,
    )
```

```python
import functools

import jax
import jax.numpy as jnp
from jax import lax
from jax.experimental import pallas as pl
from jax.experimental.pallas import tpu as pltpu
from jax.sharding import PartitionSpec as P

NY, NZ, NC = 4, 8, 2
BAND = NY * NZ * NC
F32, BF16 = jnp.float32, jnp.bfloat16
VMEM = 40 * 2**20
CORE_SWAP = [(b, b ^ 1) for b in range(BAND)]
Z_GROUPS = [[(y * NZ + z) * NC + c for z in range(NZ)] for y in range(NY) for c in range(NC)]
ZC_GROUPS = [[y * NZ * NC + k for k in range(NZ * NC)] for y in range(NY)]
Y_GROUPS = [[(y * NZ + z) * NC + c for y in range(NY)] for z in range(NZ) for c in range(NC)]


def halo(array):
    devices = lax.axis_size("band")
    up = [(i, i + 1) for i in range(devices - 1)]
    down = [(j, i) for i, j in up]
    before = lax.ppermute(array[0, -1:], "band", up)
    after = lax.ppermute(array[0, :1], "band", down)
    return before, after


def rpn_kernel(before_ref, feat_ref, after_ref, rpn_ref, anchor_ref, out_ref, rows, held):
    count = feat_ref.shape[0]
    width = feat_ref.shape[1]
    rows[0] = before_ref[0]
    rows[pl.ds(1, count)] = feat_ref[...]
    rows[count + 1] = after_ref[0]

    def line(y, carry):
        sides = []
        for dx in range(3):
            total = dot(rows[y], rpn_ref[0, dx], (1, 0))
            total = total + dot(rows[y + 1], rpn_ref[1, dx], (1, 0))
            sides.append(total + dot(rows[y + 2], rpn_ref[2, dx], (1, 0)))
        place = lax.broadcasted_iota(jnp.int32, sides[0].shape, 0)
        left = jnp.where(place == 0, 0.0, pltpu.roll(sides[0], 1, 0))
        right = jnp.where(place == width - 1, 0.0, pltpu.roll(sides[2], width - 1, 0))
        hidden = jnp.maximum(left + sides[1] + right, 0.0).astype(BF16)
        held[y] = dot(anchor_ref[...], hidden, (1, 1))
        return carry

    lax.fori_loop(0, count, line, 0)
    for y in range(count):
        for a in range(out_ref.shape[0]):
            out_ref[a, y : y + 1, :] = held[y, a : a + 1, :].astype(BF16)


def rpn(before, features, after, w_rpn, w_anchor):
    rows, width, channels = features.shape[1:]
    anchors = w_anchor.shape[1]
    out = pl.pallas_call(
        rpn_kernel,
        out_shape=jax.ShapeDtypeStruct((anchors, rows, width), BF16),
        in_specs=vmem_spec(5),
        out_specs=pl.BlockSpec(memory_space=pltpu.VMEM),
        scratch_shapes=[
            pltpu.VMEM((rows + 2, width, channels), BF16),
            pltpu.VMEM((rows, anchors, width), F32),
        ],
        compiler_params=pltpu.CompilerParams(vmem_limit_bytes=VMEM),
        cost_estimate=pl.CostEstimate(flops=9 * 10**9, bytes_accessed=4 * 10**6, transcendentals=0),
        name="rpn",
    )(before, features[0], after, w_rpn, w_anchor.T)
    return out[None]


def vmem_spec(count):
    return [pl.BlockSpec(memory_space=pltpu.VMEM)] * count


SMEM_SPEC = pl.BlockSpec(memory_space=pltpu.SMEM)


def exchange(array, groups):
    return lax.all_to_all(
        array, "band", split_axis=0, concat_axis=0, tiled=True, axis_index_groups=groups
    )


def dot(left, right, contract):
    return lax.dot_general(left, right, ((contract[:1], contract[1:]), ((), ())), preferred_element_type=F32)


def shift_img(array, step):
    size = lax.axis_size("img")
    return lax.ppermute(array, "img", [(i, (i + step) % size) for i in range(size)])


def collect_kernel(slots_ref, feat_ref, out_ref, picks):
    pixels = feat_ref.shape[0]
    per_head = slots_ref.shape[0]
    heads = picks.shape[0] // per_head
    column = lax.broadcasted_iota(jnp.int32, (per_head, pixels), 1)
    for part in range(slots_ref.shape[1] // heads):
        for k in range(heads):
            at = part * heads + k
            hit = jnp.broadcast_to(slots_ref[:, at : at + 1], (per_head, pixels)) == column
            picks[k * per_head : (k + 1) * per_head, :] = hit.astype(F32).astype(BF16)
        found = dot(picks[...], feat_ref[...], (1, 0)).astype(BF16)
        out_ref[part * heads : (part + 1) * heads] = found.reshape((heads, per_head, found.shape[1]))


def collect(slots, flat):
    per_head, heads = slots.shape
    pixels, channels = flat.shape
    return pl.pallas_call(
        collect_kernel,
        out_shape=jax.ShapeDtypeStruct((heads, per_head, channels), BF16),
        in_specs=vmem_spec(2),
        out_specs=pl.BlockSpec(memory_space=pltpu.VMEM),
        scratch_shapes=[pltpu.VMEM((16 * per_head, pixels), BF16)],
        compiler_params=pltpu.CompilerParams(vmem_limit_bytes=VMEM),
        cost_estimate=pl.CostEstimate(flops=4 * 10**9, bytes_accessed=3 * 10**6, transcendentals=0),
        name="collect",
    )(slots, flat)


PITCH = 256
SHORT = 200


def halves_kernel(place, *refs):
    core = place[0]
    sources, keep_ref, send_ref = refs[:NY], refs[NY], refs[NY + 1]
    depth = sources[0].shape[0]
    wide = keep_ref.shape[1]
    for ref, side in ((keep_ref, core), (send_ref, 1 - core)):
        ref[...] = jnp.zeros_like(ref)
        for k, source in enumerate(sources):
            cols = pl.ds(pl.multiple_of(side * wide, wide), wide)
            ref[k * SHORT : k * SHORT + depth, :] = source[:, cols]


def halves(place, slices):
    shape = (NY * SHORT + 8, slices[0].shape[1] // NC)
    return pl.pallas_call(
        halves_kernel,
        out_shape=[jax.ShapeDtypeStruct(shape, BF16)] * 2,
        in_specs=[SMEM_SPEC] + vmem_spec(NY),
        out_specs=vmem_spec(2),
        compiler_params=pltpu.CompilerParams(vmem_limit_bytes=VMEM),
        name="halves",
    )(place, *slices)


def partial_kernel(place, mine_ref, other_ref, keep_ref, got_ref, out_ref):
    y_at = place[2]
    total = None
    for step in range(NY):
        start = lax.rem(y_at + NY - step, NY) * PITCH
        cols = pl.ds(pl.multiple_of(start, PITCH), PITCH)
        rows = slice(step * SHORT, (step + 1) * SHORT)
        for ref, weight in ((mine_ref, keep_ref), (other_ref, got_ref)):
            part = dot(ref[:, cols][:, :SHORT], weight[rows, :], (1, 0))
            total = part if total is None else total + part
    out_ref[...] = total.astype(BF16)


def partial_sums(place, mine, other, keep, got):
    return pl.pallas_call(
        partial_kernel,
        out_shape=jax.ShapeDtypeStruct((mine.shape[0], keep.shape[1]), BF16),
        in_specs=[SMEM_SPEC] + vmem_spec(4),
        out_specs=pl.BlockSpec(memory_space=pltpu.VMEM),
        compiler_params=pltpu.CompilerParams(vmem_limit_bytes=VMEM),
        name="partial_sums",
    )(place, mine, other, keep, got)


def shift_y(array, step):
    row = NZ * NC
    return lax.ppermute(array, "band", [(b, (b + step * row) % BAND) for b in range(BAND)])


def gelu_parts(value):
    cubic = 0.044715 * (value * value * value)
    tanh = jnp.tanh(0.7978845608028654 * (value + cubic))
    return tanh


def gelu_of(value):
    return 0.5 * value * (1.0 + gelu_parts(value))


def slope_of(value):
    tanh = gelu_parts(value)
    inner = 0.7978845608028654 * (1.0 + 3.0 * 0.044715 * (value * value))
    return 0.5 * (1.0 + tanh) + 0.5 * value * (1.0 - tanh * tanh) * inner


ROW_BLOCK = 128


def join_halves(core, mine_ref, other_ref, whole_ref):
    half = whole_ref.shape[1] // NC
    whole_ref[:, pl.ds(pl.multiple_of(core * half, half), half)] = mine_ref[:, :half]
    whole_ref[:, pl.ds(pl.multiple_of((1 - core) * half, half), half)] = other_ref[:, :half]


def head_kernel(place, mine_ref, other_ref, fc2_ref, class_ref, da2_ref, *refs):
    sends, (a1, h1, h2, dlog) = refs[:4], refs[4:]
    core, image = place[0], place[1]
    join_halves(core, mine_ref, other_ref, a1)
    classes = class_ref.shape[0]
    count, hid = a1.shape
    for step in range(count // ROW_BLOCK):
        rows = slice(step * ROW_BLOCK, (step + 1) * ROW_BLOCK)
        hidden = gelu_of(a1[rows, :].astype(F32)).astype(BF16)
        h1[rows, :] = hidden
        a2 = dot(hidden, fc2_ref[...], (1, 0))
        second = gelu_of(a2).astype(BF16)
        h2[rows, :] = second
        logits = dot(second, class_ref[...], (1, 1))
        column = lax.broadcasted_iota(jnp.int32, (ROW_BLOCK, classes), 1)
        expo = jnp.exp(logits)
        prob = expo / jnp.sum(expo, axis=1, keepdims=True)
        labels = mine_ref[rows, hid // NC :].astype(F32)[:, :1].astype(jnp.int32)
        onehot = (labels == column).astype(F32)
        dlogits = (prob - onehot).astype(BF16)
        dlog[rows, :] = dlogits
        dh2 = dot(dlogits, class_ref[...], (1, 0))
        da2_ref[rows, :] = (dh2 * slope_of(a2)).astype(BF16)
    images = 4
    wide = hid // NC // images
    for step, out in enumerate(sends):
        chunk = lax.rem(image + step, images)
        cols = pl.ds(pl.multiple_of(core * (hid // NC) + chunk * wide, wide), wide)
        out[:, :hid] = dot(h1[:, cols], da2_ref[...], (0, 0)).astype(out.dtype)
        out[:, hid:] = jnp.zeros((wide, out.shape[1] - hid), out.dtype)
        out[:classes, hid:] = dot(dlog[...], h2[:, cols], (0, 0)).astype(out.dtype)


def head(place, mine, other, w_fc2, w_class):
    count, half = mine.shape[0], w_fc2.shape[0] // NC
    hid = w_fc2.shape[0]
    classes = w_class.shape[1]
    wide = half // 4
    struct = jax.ShapeDtypeStruct
    return pl.pallas_call(
        head_kernel,
        out_shape=[struct((count, hid), BF16), struct((wide, hid + 128), F32)]
        + [struct((wide, hid + 128), BF16)] * 3,
        in_specs=[SMEM_SPEC] + vmem_spec(4),
        out_specs=vmem_spec(5),
        scratch_shapes=[
            pltpu.VMEM((count, hid), BF16),
            pltpu.VMEM((count, hid), BF16),
            pltpu.VMEM((count, hid), BF16),
            pltpu.VMEM((count, classes), BF16),
        ],
        compiler_params=pltpu.CompilerParams(vmem_limit_bytes=VMEM),
        name="head",
    )(place, mine, other, w_fc2, w_class.T)


def back_kernel(place, mine_ref, other_ref, da2_ref, fc2_ref, da1_ref, a1):
    join_halves(place[0], mine_ref, other_ref, a1)
    for step in range(a1.shape[0] // ROW_BLOCK):
        rows = slice(step * ROW_BLOCK, (step + 1) * ROW_BLOCK)
        dh1 = dot(da2_ref[rows, :], fc2_ref[...], (1, 1))
        da1_ref[rows, :] = (dh1 * slope_of(a1[rows, :].astype(F32))).astype(BF16)


def back(place, mine, other, da2, w_fc2):
    return pl.pallas_call(
        back_kernel,
        out_shape=jax.ShapeDtypeStruct(da2.shape, BF16),
        in_specs=[SMEM_SPEC] + vmem_spec(4),
        out_specs=pl.BlockSpec(memory_space=pltpu.VMEM),
        scratch_shapes=[pltpu.VMEM(da2.shape, BF16)],
        compiler_params=pltpu.CompilerParams(vmem_limit_bytes=VMEM),
        cost_estimate=pl.CostEstimate(flops=2 * 10**9, bytes_accessed=5 * 10**6, transcendentals=0),
        name="back",
    )(place, mine, other, da2, w_fc2)


def first_kernel(place, da1_ref, *refs):
    image, y_at = place[1], place[2]
    x_refs, outs, rois = refs[:NY], refs[NY : NY + 4], refs[NY + 4]
    tall = x_refs[0].shape[0]
    for step, ref in enumerate(x_refs):
        start = lax.rem(y_at + NY - step, NY) * tall
        rois[pl.ds(pl.multiple_of(start, tall), tall), :] = ref[...]
    images = 4
    wide = da1_ref.shape[1] // images
    depth = outs[0].shape[0]
    for step, out in enumerate(outs):
        chunk = lax.rem(image + step, images)
        cols = pl.ds(pl.multiple_of(chunk * wide, wide), wide)
        out[...] = dot(rois[...], da1_ref[:, cols], (0, 0))[:depth].astype(out.dtype)


def first_layer(place, da1, x_blocks, depth):
    count, hid = da1.shape
    wide = hid // 4
    struct = jax.ShapeDtypeStruct
    return pl.pallas_call(
        first_kernel,
        out_shape=[struct((depth, wide), F32)] + [struct((depth, wide), BF16)] * 3,
        in_specs=[SMEM_SPEC] + vmem_spec(1 + NY),
        out_specs=vmem_spec(4),
        scratch_shapes=[pltpu.VMEM((count, PITCH), BF16)],
        compiler_params=pltpu.CompilerParams(vmem_limit_bytes=VMEM),
        name="first_layer",
    )(place, da1, *x_blocks)


SUM_ROWS = 192


CLASS_ROWS = 11


def sum_kernel(*refs):
    heads, firsts, out_ref, rest = refs[:4], refs[4:8], refs[8], refs[9]
    tall = heads[0].shape[0]
    hid = out_ref.shape[1]
    total = heads[0][...]
    for ref in heads[1:]:
        total = total + ref[...].astype(F32)
    out_ref[:tall, :] = total[:, :hid].astype(BF16)
    first = firsts[0][...]
    for ref in firsts[1:]:
        first = first + ref[...].astype(F32)
    depth, cols = first.shape
    quarter = depth // 4
    rest[...] = jnp.zeros_like(rest)
    for k in range(hid // 128):
        rest[:CLASS_ROWS, k * 128 : (k + 1) * 128] = total[k * CLASS_ROWS : (k + 1) * CLASS_ROWS, hid:]
    for q in range(4):
        part = first[q * quarter : (q + 1) * quarter]
        rest[CLASS_ROWS : CLASS_ROWS + quarter, q * cols : (q + 1) * cols] = part
    out_ref[tall:, :] = rest[...].astype(BF16)


def sum_parts(heads, firsts):
    tall, wide = heads[0].shape[0], heads[0].shape[1] - 128
    return pl.pallas_call(
        sum_kernel,
        out_shape=jax.ShapeDtypeStruct((SUM_ROWS, wide), BF16),
        in_specs=vmem_spec(8),
        out_specs=pl.BlockSpec(memory_space=pltpu.VMEM),
        scratch_shapes=[pltpu.VMEM((SUM_ROWS - tall, wide), F32)],
        compiler_params=pltpu.CompilerParams(vmem_limit_bytes=VMEM),
        name="sum_parts",
    )(*heads, *firsts)


def assemble_kernel(place, *refs):
    core, image = place[0], place[1]
    mine, other = refs[:4], refs[4:8]
    fc1_ref, fc2_ref, class_ref = refs[8:]
    hid = fc2_ref.shape[1]
    images = 4
    classes = class_ref.shape[0]
    tall = hid // NC // images
    depth = fc1_ref.shape[0]
    quarter = depth // 4
    wide = hid // images
    for step in range(images):
        chunk = lax.rem(image + images - step, images)
        for side, ref in ((core, mine[step]), (1 - core, other[step])):
            at = pl.ds(pl.multiple_of(side * (hid // NC) + chunk * tall, tall), tall)
            fc2_ref[at, :] = ref[:tall, :].astype(F32)
            rest = ref[tall : tall + 16, :].astype(F32)
            for k in range(hid // 128):
                count = min(CLASS_ROWS, classes - k * CLASS_ROWS)
                part = rest[:count, k * 128 : (k + 1) * 128]
                class_ref[k * CLASS_ROWS : k * CLASS_ROWS + count, at] = part
        cols = pl.ds(pl.multiple_of(chunk * wide, wide), wide)
        rest = mine[step][tall:, :].astype(F32)
        for q in range(4):
            part = rest[CLASS_ROWS : CLASS_ROWS + quarter, q * wide : (q + 1) * wide]
            fc1_ref[q * quarter : (q + 1) * quarter, cols] = part


def assemble(place, mine, other, depth, classes):
    hid = mine[0].shape[1]
    struct = jax.ShapeDtypeStruct
    return pl.pallas_call(
        assemble_kernel,
        out_shape=[struct((depth, hid), F32), struct((hid, hid), F32), struct((classes, hid), F32)],
        in_specs=[SMEM_SPEC] + vmem_spec(8),
        out_specs=vmem_spec(3),
        compiler_params=pltpu.CompilerParams(vmem_limit_bytes=VMEM),
        name="assemble",
    )(place, *mine, *other)


def shift_all(sent):
    return [shift_img(part, step) for step, part in enumerate(sent, 1)]


def shards(
    features,
    w_rpn,
    w_anchor,
    pixel_slots,
    sample_slot,
    sample_weight,
    roi_labels,
    w_fc1,
    w_fc2,
    w_class,
):
    rows, width, channels = features.shape[1:]
    nband = lax.axis_size("band")
    band, image = lax.axis_index("band"), lax.axis_index("img")
    core = band % NC
    hid = w_fc2.shape[0]
    half = hid // NC
    y_at = band // (NC * NZ)
    place = jnp.stack([core, image, y_at]).astype(jnp.int32)

    flat = features.reshape(rows * width, channels)
    capacity = pixel_slots.shape[3]
    sending = collect(jnp.transpose(pixel_slots[0, :, 0, :]), flat)
    received = lax.all_to_all(sending, "band", split_axis=0, concat_axis=0, tiled=True)

    depth = w_fc1.shape[0]
    w_first, edges, labels = lax.optimization_barrier((w_fc1, features, roi_labels, sending))[:3]
    slices = [w_first] + [shift_y(w_first, step) for step in range(1, NY)]
    before, after = halo(edges)
    marks = jnp.broadcast_to(labels[0].astype(BF16)[:, None], (labels.shape[1], 128))
    others = lax.ppermute(marks, "band", CORE_SWAP)
    marks = jnp.where(core == 0, jnp.concatenate([marks, others]), jnp.concatenate([others, marks]))

    received = received.reshape(nband * capacity, channels).astype(F32)
    roi_count, bins = sample_slot.shape[1:3]
    corner_slots = sample_slot[0].reshape(roi_count * bins, 4)
    corner_weights = sample_weight[0].reshape(roi_count * bins, 4)
    slot_ids = jnp.arange(nband * capacity, dtype=jnp.int32)[None, :]
    pooling = jnp.zeros((roi_count * bins, nband * capacity), F32)
    for corner in range(4):
        hits = (corner_slots[:, corner : corner + 1] == slot_ids).astype(F32)
        pooling = pooling + hits * corner_weights[:, corner : corner + 1]
    pooled = jnp.dot(pooling, received, precision=lax.Precision.HIGHEST, preferred_element_type=F32)
    pooled = pooled.astype(BF16).reshape(roi_count, bins, channels)
    x_local = jnp.transpose(pooled, (0, 2, 1)).reshape(roi_count, nband, depth)
    x_local = jnp.pad(x_local, ((0, 0), (0, 0), (0, PITCH - depth)))
    x_local = x_local.reshape(roi_count, NY, NZ * NC, PITCH).transpose(2, 0, 1, 3)
    x_local, slices, before, after, marks = lax.optimization_barrier(
        (x_local, slices, before, after, marks)
    )
    keep, send = halves(place, slices)
    got = lax.ppermute(send, "band", CORE_SWAP)
    x_part = exchange(x_local.reshape(NZ * NC, roi_count, NY * PITCH), ZC_GROUPS)
    x_part = x_part.reshape(NZ * NC * roi_count, NY * PITCH)

    x_other = lax.ppermute(x_part, "band", CORE_SWAP)
    partial = partial_sums(place, x_part, x_other, keep, got)
    count = roi_count * nband
    by_z = exchange(partial.reshape(NZ, count // NY // NZ, half), Z_GROUPS)
    a1_own = jnp.sum(by_z.astype(F32), axis=0).astype(BF16)
    a1_own = jnp.concatenate([a1_own, marks], axis=1)
    a1_z = exchange(jnp.broadcast_to(a1_own[None], (NZ,) + a1_own.shape), Z_GROUPS)
    a1_z = a1_z.reshape(1, count // NY, half + 128)
    a1_mine = exchange(jnp.broadcast_to(a1_z, (NY,) + a1_z.shape[1:]), Y_GROUPS)
    a1_mine = a1_mine.reshape(count, half + 128)
    a1_other = lax.ppermute(a1_mine, "band", CORE_SWAP)
    da2, *parts = head(place, a1_mine, a1_other, w_fc2, w_class)
    head_own, head_got = parts[0], shift_all(parts[1:])
    x_part = lax.optimization_barrier((x_part, da2))[0]
    x_blocks = [lax.dynamic_slice_in_dim(x_part, y_at * PITCH, PITCH, 1)]
    for step in range(1, NY):
        to = (y_at + step) % NY
        x_blocks.append(shift_y(lax.dynamic_slice_in_dim(x_part, to * PITCH, PITCH, 1), step))
    da1 = back(place, a1_mine, a1_other, da2, w_fc2)
    parts = first_layer(place, da1, x_blocks, depth)
    first_got = [shift_img(parts[1], 1), None, shift_img(parts[3], 3)]
    held, head_got[0], head_got[2] = lax.optimization_barrier((parts[2], head_got[0], head_got[2]))
    first_got[1] = shift_img(held, 2)
    total = sum_parts([head_own] + head_got, [parts[0]] + first_got)
    total, inner = lax.optimization_barrier((total, features))
    mine = [total] + [shift_img(total, step) for step in range(1, 4)]
    rpn_out = rpn(before, inner, after, w_rpn, w_anchor)
    mine[2], rpn_out = lax.optimization_barrier((mine[2], rpn_out))
    tall = head_own.shape[0] + 16
    other = [lax.ppermute(part[:tall], "band", CORE_SWAP) for part in mine]
    grad_fc1, grad_fc2, grad_class = assemble(place, mine, other, depth, w_class.shape[1])
    return (rpn_out, grad_fc1, grad_fc2, grad_class.T)


def solution(mesh):
    return jax.shard_map(
        shards,
        mesh=mesh,
        in_specs=(
            P("img", "band", None, None),
            P(),
            P(),
            P("img", None, "band", None),
            P("img", "band", None, None),
            P("img", "band", None, None),
            P("img", "band"),
            P("band", None),
            P(),
            P(),
        ),
        out_specs=(P("img", None, "band", None), P("band", None), P(), P()),
        check_vma=False,
    )
```

```python
import functools

import jax
import jax.numpy as jnp
from jax import lax
from jax.experimental import pallas as pl
from jax.experimental.pallas import tpu as pltpu
from jax.sharding import PartitionSpec as P

NY, NZ, NC = 4, 8, 2
BAND = NY * NZ * NC
F32, BF16 = jnp.float32, jnp.bfloat16
VMEM = 40 * 2**20
CORE_SWAP = [(b, b ^ 1) for b in range(BAND)]
Z_GROUPS = [[(y * NZ + z) * NC + c for z in range(NZ)] for y in range(NY) for c in range(NC)]
ZC_GROUPS = [[y * NZ * NC + k for k in range(NZ * NC)] for y in range(NY)]
Y_GROUPS = [[(y * NZ + z) * NC + c for y in range(NY)] for z in range(NZ) for c in range(NC)]


def halo(array):
    devices = lax.axis_size("band")
    up = [(i, i + 1) for i in range(devices - 1)]
    down = [(j, i) for i, j in up]
    before = lax.ppermute(array[0, -1:], "band", up)
    after = lax.ppermute(array[0, :1], "band", down)
    return before, after


def rpn_kernel(before_ref, feat_ref, after_ref, rpn_ref, anchor_ref, out_ref, rows, held):
    count = feat_ref.shape[0]
    width = feat_ref.shape[1]
    rows[0] = before_ref[0]
    rows[pl.ds(1, count)] = feat_ref[...]
    rows[count + 1] = after_ref[0]

    def line(y, carry):
        sides = []
        for dx in range(3):
            total = dot(rows[y], rpn_ref[0, dx], (1, 0))
            total = total + dot(rows[y + 1], rpn_ref[1, dx], (1, 0))
            sides.append(total + dot(rows[y + 2], rpn_ref[2, dx], (1, 0)))
        place = lax.broadcasted_iota(jnp.int32, sides[0].shape, 0)
        left = jnp.where(place == 0, 0.0, pltpu.roll(sides[0], 1, 0))
        right = jnp.where(place == width - 1, 0.0, pltpu.roll(sides[2], width - 1, 0))
        hidden = jnp.maximum(left + sides[1] + right, 0.0).astype(BF16)
        held[y] = dot(anchor_ref[...], hidden, (1, 1))
        return carry

    lax.fori_loop(0, count, line, 0)
    for y in range(count):
        for a in range(out_ref.shape[0]):
            out_ref[a, y : y + 1, :] = held[y, a : a + 1, :].astype(BF16)


def rpn(before, features, after, w_rpn, w_anchor):
    rows, width, channels = features.shape[1:]
    anchors = w_anchor.shape[1]
    out = pl.pallas_call(
        rpn_kernel,
        out_shape=jax.ShapeDtypeStruct((anchors, rows, width), BF16),
        in_specs=vmem_spec(5),
        out_specs=pl.BlockSpec(memory_space=pltpu.VMEM),
        scratch_shapes=[
            pltpu.VMEM((rows + 2, width, channels), BF16),
            pltpu.VMEM((rows, anchors, width), F32),
        ],
        compiler_params=pltpu.CompilerParams(vmem_limit_bytes=VMEM),
        cost_estimate=pl.CostEstimate(flops=9 * 10**9, bytes_accessed=4 * 10**6, transcendentals=0),
        name="rpn",
    )(before, features[0], after, w_rpn, w_anchor.T)
    return out[None]


def vmem_spec(count):
    return [pl.BlockSpec(memory_space=pltpu.VMEM)] * count


SMEM_SPEC = pl.BlockSpec(memory_space=pltpu.SMEM)


def exchange(array, groups):
    return lax.all_to_all(
        array, "band", split_axis=0, concat_axis=0, tiled=True, axis_index_groups=groups
    )


def dot(left, right, contract):
    return lax.dot_general(left, right, ((contract[:1], contract[1:]), ((), ())), preferred_element_type=F32)


def shift_img(array, step):
    size = lax.axis_size("img")
    return lax.ppermute(array, "img", [(i, (i + step) % size) for i in range(size)])


def collect_kernel(slots_ref, feat_ref, out_ref, picks):
    pixels = feat_ref.shape[0]
    per_head = slots_ref.shape[0]
    heads = picks.shape[0] // per_head
    column = lax.broadcasted_iota(jnp.int32, (per_head, pixels), 1)
    for part in range(slots_ref.shape[1] // heads):
        for k in range(heads):
            at = part * heads + k
            hit = jnp.broadcast_to(slots_ref[:, at : at + 1], (per_head, pixels)) == column
            picks[k * per_head : (k + 1) * per_head, :] = hit.astype(F32).astype(BF16)
        found = dot(picks[...], feat_ref[...], (1, 0)).astype(BF16)
        out_ref[part * heads : (part + 1) * heads] = found.reshape((heads, per_head, found.shape[1]))


def collect(slots, flat):
    per_head, heads = slots.shape
    pixels, channels = flat.shape
    return pl.pallas_call(
        collect_kernel,
        out_shape=jax.ShapeDtypeStruct((heads, per_head, channels), BF16),
        in_specs=vmem_spec(2),
        out_specs=pl.BlockSpec(memory_space=pltpu.VMEM),
        scratch_shapes=[pltpu.VMEM((16 * per_head, pixels), BF16)],
        compiler_params=pltpu.CompilerParams(vmem_limit_bytes=VMEM),
        cost_estimate=pl.CostEstimate(flops=4 * 10**9, bytes_accessed=3 * 10**6, transcendentals=0),
        name="collect",
    )(slots, flat)


PITCH = 256


def partial_kernel(place, x_ref, *refs):
    core, y_at = place[0], place[2]
    slices, outs = refs[:NY], refs[NY:]
    depth = slices[0].shape[0]
    blocks = []
    for step in range(NY):
        start = lax.rem(y_at + NY - step, NY) * PITCH
        blocks.append(x_ref[:, pl.ds(pl.multiple_of(start, PITCH), PITCH)][:, :depth])
    for out, side in zip(outs, (core, 1 - core)):
        wide = out.shape[1]
        cols = pl.ds(pl.multiple_of(side * wide, wide), wide)
        total = dot(blocks[0], slices[0][:, cols], (1, 0))
        for step in range(1, NY):
            total = total + dot(blocks[step], slices[step][:, cols], (1, 0))
        out[...] = total.astype(out.dtype)


def partial_sums(place, x_part, slices):
    shape = (x_part.shape[0], slices[0].shape[1] // NC)
    return pl.pallas_call(
        partial_kernel,
        out_shape=[jax.ShapeDtypeStruct(shape, F32), jax.ShapeDtypeStruct(shape, BF16)],
        in_specs=[SMEM_SPEC] + vmem_spec(1 + NY),
        out_specs=vmem_spec(2),
        compiler_params=pltpu.CompilerParams(vmem_limit_bytes=VMEM),
        name="partial_sums",
    )(place, x_part, *slices)


def shift_y(array, step):
    row = NZ * NC
    return lax.ppermute(array, "band", [(b, (b + step * row) % BAND) for b in range(BAND)])


def gelu_parts(value):
    cubic = 0.044715 * (value * value * value)
    tanh = jnp.tanh(0.7978845608028654 * (value + cubic))
    return tanh


def gelu_of(value):
    return 0.5 * value * (1.0 + gelu_parts(value))


def slope_of(value):
    tanh = gelu_parts(value)
    inner = 0.7978845608028654 * (1.0 + 3.0 * 0.044715 * (value * value))
    return 0.5 * (1.0 + tanh) + 0.5 * value * (1.0 - tanh * tanh) * inner


ROW_BLOCK = 128


def join_halves(core, mine_ref, other_ref, whole_ref):
    half = whole_ref.shape[1] // NC
    whole_ref[:, pl.ds(pl.multiple_of(core * half, half), half)] = mine_ref[:, :half]
    whole_ref[:, pl.ds(pl.multiple_of((1 - core) * half, half), half)] = other_ref[:, :half]


def head_kernel(place, mine_ref, other_ref, fc2_ref, class_ref, da2_ref, *refs):
    sends, (a1, h1, h2, dlog) = refs[:4], refs[4:]
    core, image = place[0], place[1]
    join_halves(core, mine_ref, other_ref, a1)
    classes = class_ref.shape[0]
    count, hid = a1.shape
    for step in range(count // ROW_BLOCK):
        rows = slice(step * ROW_BLOCK, (step + 1) * ROW_BLOCK)
        hidden = gelu_of(a1[rows, :].astype(F32)).astype(BF16)
        h1[rows, :] = hidden
        a2 = dot(hidden, fc2_ref[...], (1, 0))
        second = gelu_of(a2).astype(BF16)
        h2[rows, :] = second
        logits = dot(second, class_ref[...], (1, 1))
        column = lax.broadcasted_iota(jnp.int32, (ROW_BLOCK, classes), 1)
        expo = jnp.exp(logits)
        prob = expo / jnp.sum(expo, axis=1, keepdims=True)
        labels = mine_ref[rows, hid // NC :].astype(F32)[:, :1].astype(jnp.int32)
        onehot = (labels == column).astype(F32)
        dlogits = (prob - onehot).astype(BF16)
        dlog[rows, :] = dlogits
        dh2 = dot(dlogits, class_ref[...], (1, 0))
        da2_ref[rows, :] = (dh2 * slope_of(a2)).astype(BF16)
    images = 4
    wide = hid // NC // images
    for step, out in enumerate(sends):
        chunk = lax.rem(image + step, images)
        cols = pl.ds(pl.multiple_of(core * (hid // NC) + chunk * wide, wide), wide)
        out[:, :hid] = dot(h1[:, cols], da2_ref[...], (0, 0)).astype(out.dtype)
        out[:, hid:] = jnp.zeros((wide, out.shape[1] - hid), out.dtype)
        out[:classes, hid:] = dot(dlog[...], h2[:, cols], (0, 0)).astype(out.dtype)


def head(place, mine, other, w_fc2, w_class):
    count, half = mine.shape[0], w_fc2.shape[0] // NC
    hid = w_fc2.shape[0]
    classes = w_class.shape[1]
    wide = half // 4
    struct = jax.ShapeDtypeStruct
    return pl.pallas_call(
        head_kernel,
        out_shape=[struct((count, hid), BF16), struct((wide, hid + 128), F32)]
        + [struct((wide, hid + 128), BF16)] * 3,
        in_specs=[SMEM_SPEC] + vmem_spec(4),
        out_specs=vmem_spec(5),
        scratch_shapes=[
            pltpu.VMEM((count, hid), BF16),
            pltpu.VMEM((count, hid), BF16),
            pltpu.VMEM((count, hid), BF16),
            pltpu.VMEM((count, classes), BF16),
        ],
        compiler_params=pltpu.CompilerParams(vmem_limit_bytes=VMEM),
        name="head",
    )(place, mine, other, w_fc2, w_class.T)


def back_kernel(place, mine_ref, other_ref, da2_ref, fc2_ref, da1_ref, a1):
    join_halves(place[0], mine_ref, other_ref, a1)
    for step in range(a1.shape[0] // ROW_BLOCK):
        rows = slice(step * ROW_BLOCK, (step + 1) * ROW_BLOCK)
        dh1 = dot(da2_ref[rows, :], fc2_ref[...], (1, 1))
        da1_ref[rows, :] = (dh1 * slope_of(a1[rows, :].astype(F32))).astype(BF16)


def back(place, mine, other, da2, w_fc2):
    return pl.pallas_call(
        back_kernel,
        out_shape=jax.ShapeDtypeStruct(da2.shape, BF16),
        in_specs=[SMEM_SPEC] + vmem_spec(4),
        out_specs=pl.BlockSpec(memory_space=pltpu.VMEM),
        scratch_shapes=[pltpu.VMEM(da2.shape, BF16)],
        compiler_params=pltpu.CompilerParams(vmem_limit_bytes=VMEM),
        cost_estimate=pl.CostEstimate(flops=2 * 10**9, bytes_accessed=5 * 10**6, transcendentals=0),
        name="back",
    )(place, mine, other, da2, w_fc2)


def first_kernel(place, da1_ref, *refs):
    image, y_at = place[1], place[2]
    x_refs, outs, rois = refs[:NY], refs[NY : NY + 4], refs[NY + 4]
    tall = x_refs[0].shape[0]
    for step, ref in enumerate(x_refs):
        start = lax.rem(y_at + NY - step, NY) * tall
        rois[pl.ds(pl.multiple_of(start, tall), tall), :] = ref[...]
    images = 4
    wide = da1_ref.shape[1] // images
    depth = outs[0].shape[0]
    for step, out in enumerate(outs):
        chunk = lax.rem(image + step, images)
        cols = pl.ds(pl.multiple_of(chunk * wide, wide), wide)
        out[...] = dot(rois[...], da1_ref[:, cols], (0, 0))[:depth].astype(out.dtype)


def first_layer(place, da1, x_blocks, depth):
    count, hid = da1.shape
    wide = hid // 4
    struct = jax.ShapeDtypeStruct
    return pl.pallas_call(
        first_kernel,
        out_shape=[struct((depth, wide), F32)] + [struct((depth, wide), BF16)] * 3,
        in_specs=[SMEM_SPEC] + vmem_spec(1 + NY),
        out_specs=vmem_spec(4),
        scratch_shapes=[pltpu.VMEM((count, PITCH), BF16)],
        compiler_params=pltpu.CompilerParams(vmem_limit_bytes=VMEM),
        name="first_layer",
    )(place, da1, *x_blocks)


SUM_ROWS = 192


CLASS_ROWS = 11


def sum_kernel(*refs):
    heads, firsts, out_ref, rest = refs[:4], refs[4:8], refs[8], refs[9]
    tall = heads[0].shape[0]
    hid = out_ref.shape[1]
    total = heads[0][...]
    for ref in heads[1:]:
        total = total + ref[...].astype(F32)
    out_ref[:tall, :] = total[:, :hid].astype(BF16)
    first = firsts[0][...]
    for ref in firsts[1:]:
        first = first + ref[...].astype(F32)
    depth, cols = first.shape
    quarter = depth // 4
    rest[...] = jnp.zeros_like(rest)
    for k in range(hid // 128):
        rest[:CLASS_ROWS, k * 128 : (k + 1) * 128] = total[k * CLASS_ROWS : (k + 1) * CLASS_ROWS, hid:]
    for q in range(4):
        part = first[q * quarter : (q + 1) * quarter]
        rest[CLASS_ROWS : CLASS_ROWS + quarter, q * cols : (q + 1) * cols] = part
    out_ref[tall:, :] = rest[...].astype(BF16)


def sum_parts(heads, firsts):
    tall, wide = heads[0].shape[0], heads[0].shape[1] - 128
    return pl.pallas_call(
        sum_kernel,
        out_shape=jax.ShapeDtypeStruct((SUM_ROWS, wide), BF16),
        in_specs=vmem_spec(8),
        out_specs=pl.BlockSpec(memory_space=pltpu.VMEM),
        scratch_shapes=[pltpu.VMEM((SUM_ROWS - tall, wide), F32)],
        compiler_params=pltpu.CompilerParams(vmem_limit_bytes=VMEM),
        name="sum_parts",
    )(*heads, *firsts)


def assemble_kernel(place, *refs):
    core, image = place[0], place[1]
    mine, other = refs[:4], refs[4:8]
    fc1_ref, fc2_ref, class_ref = refs[8:]
    hid = fc2_ref.shape[1]
    images = 4
    classes = class_ref.shape[0]
    tall = hid // NC // images
    depth = fc1_ref.shape[0]
    quarter = depth // 4
    wide = hid // images
    for step in range(images):
        chunk = lax.rem(image + images - step, images)
        for side, ref in ((core, mine[step]), (1 - core, other[step])):
            at = pl.ds(pl.multiple_of(side * (hid // NC) + chunk * tall, tall), tall)
            fc2_ref[at, :] = ref[:tall, :].astype(F32)
            rest = ref[tall : tall + 16, :].astype(F32)
            for k in range(hid // 128):
                count = min(CLASS_ROWS, classes - k * CLASS_ROWS)
                part = rest[:count, k * 128 : (k + 1) * 128]
                class_ref[k * CLASS_ROWS : k * CLASS_ROWS + count, at] = part
        cols = pl.ds(pl.multiple_of(chunk * wide, wide), wide)
        rest = mine[step][tall:, :].astype(F32)
        for q in range(4):
            part = rest[CLASS_ROWS : CLASS_ROWS + quarter, q * wide : (q + 1) * wide]
            fc1_ref[q * quarter : (q + 1) * quarter, cols] = part


def assemble(place, mine, other, depth, classes):
    hid = mine[0].shape[1]
    struct = jax.ShapeDtypeStruct
    return pl.pallas_call(
        assemble_kernel,
        out_shape=[struct((depth, hid), F32), struct((hid, hid), F32), struct((classes, hid), F32)],
        in_specs=[SMEM_SPEC] + vmem_spec(8),
        out_specs=vmem_spec(3),
        compiler_params=pltpu.CompilerParams(vmem_limit_bytes=VMEM),
        name="assemble",
    )(place, *mine, *other)


def shift_all(sent):
    return [shift_img(part, step) for step, part in enumerate(sent, 1)]


def shards(
    features,
    w_rpn,
    w_anchor,
    pixel_slots,
    sample_slot,
    sample_weight,
    roi_labels,
    w_fc1,
    w_fc2,
    w_class,
):
    rows, width, channels = features.shape[1:]
    nband = lax.axis_size("band")
    band, image = lax.axis_index("band"), lax.axis_index("img")
    core = band % NC
    hid = w_fc2.shape[0]
    half = hid // NC
    y_at = band // (NC * NZ)
    place = jnp.stack([core, image, y_at]).astype(jnp.int32)

    flat = features.reshape(rows * width, channels)
    capacity = pixel_slots.shape[3]
    sending = collect(jnp.transpose(pixel_slots[0, :, 0, :]), flat)
    received = lax.all_to_all(sending, "band", split_axis=0, concat_axis=0, tiled=True)

    depth = w_fc1.shape[0]
    w_first, edges, labels = lax.optimization_barrier((w_fc1, features, roi_labels, sending))[:3]
    slices = [w_first] + [shift_y(w_first, step) for step in range(1, NY)]
    before, after = halo(edges)
    marks = jnp.broadcast_to(labels[0].astype(BF16)[:, None], (labels.shape[1], 128))
    others = lax.ppermute(marks, "band", CORE_SWAP)
    marks = jnp.where(core == 0, jnp.concatenate([marks, others]), jnp.concatenate([others, marks]))

    received = received.reshape(nband * capacity, channels).astype(F32)
    roi_count, bins = sample_slot.shape[1:3]
    corner_slots = sample_slot[0].reshape(roi_count * bins, 4)
    corner_weights = sample_weight[0].reshape(roi_count * bins, 4)
    slot_ids = jnp.arange(nband * capacity, dtype=jnp.int32)[None, :]
    pooling = jnp.zeros((roi_count * bins, nband * capacity), F32)
    for corner in range(4):
        hits = (corner_slots[:, corner : corner + 1] == slot_ids).astype(F32)
        pooling = pooling + hits * corner_weights[:, corner : corner + 1]
    pooled = jnp.dot(pooling, received, precision=lax.Precision.HIGHEST, preferred_element_type=F32)
    pooled = pooled.astype(BF16).reshape(roi_count, bins, channels)
    x_local = jnp.transpose(pooled, (0, 2, 1)).reshape(roi_count, nband, depth)
    x_local = jnp.pad(x_local, ((0, 0), (0, 0), (0, PITCH - depth)))
    x_local = x_local.reshape(roi_count, NY, NZ * NC, PITCH).transpose(2, 0, 1, 3)
    x_local, slices, before, after, marks = lax.optimization_barrier(
        (x_local, slices, before, after, marks)
    )
    x_part = exchange(x_local.reshape(NZ * NC, roi_count, NY * PITCH), ZC_GROUPS)
    x_part = x_part.reshape(NZ * NC * roi_count, NY * PITCH)

    keep, send = partial_sums(place, x_part, slices)
    partial = (keep + lax.ppermute(send, "band", CORE_SWAP).astype(F32)).astype(BF16)
    count = roi_count * nband
    by_z = exchange(partial.reshape(NZ, count // NY // NZ, half), Z_GROUPS)
    a1_own = jnp.sum(by_z.astype(F32), axis=0).astype(BF16)
    a1_own = jnp.concatenate([a1_own, marks], axis=1)
    a1_z = exchange(jnp.broadcast_to(a1_own[None], (NZ,) + a1_own.shape), Z_GROUPS)
    a1_z = a1_z.reshape(1, count // NY, half + 128)
    a1_mine = exchange(jnp.broadcast_to(a1_z, (NY,) + a1_z.shape[1:]), Y_GROUPS)
    a1_mine = a1_mine.reshape(count, half + 128)
    a1_other = lax.ppermute(a1_mine, "band", CORE_SWAP)
    da2, *parts = head(place, a1_mine, a1_other, w_fc2, w_class)
    head_own, head_got = parts[0], shift_all(parts[1:])
    x_part = lax.optimization_barrier((x_part, da2))[0]
    x_blocks = [lax.dynamic_slice_in_dim(x_part, y_at * PITCH, PITCH, 1)]
    for step in range(1, NY):
        to = (y_at + step) % NY
        x_blocks.append(shift_y(lax.dynamic_slice_in_dim(x_part, to * PITCH, PITCH, 1), step))
    da1 = back(place, a1_mine, a1_other, da2, w_fc2)
    parts = first_layer(place, da1, x_blocks, depth)
    first_got = [shift_img(parts[1], 1), None, shift_img(parts[3], 3)]
    held, head_got[0], head_got[2] = lax.optimization_barrier((parts[2], head_got[0], head_got[2]))
    first_got[1] = shift_img(held, 2)
    total = sum_parts([head_own] + head_got, [parts[0]] + first_got)
    total, inner = lax.optimization_barrier((total, features))
    mine = [total] + [shift_img(total, step) for step in range(1, 4)]
    rpn_out = rpn(before, inner, after, w_rpn, w_anchor)
    mine[2], rpn_out = lax.optimization_barrier((mine[2], rpn_out))
    tall = head_own.shape[0] + 16
    other = [lax.ppermute(part[:tall], "band", CORE_SWAP) for part in mine]
    grad_fc1, grad_fc2, grad_class = assemble(place, mine, other, depth, w_class.shape[1])
    return (rpn_out, grad_fc1, grad_fc2, grad_class.T)


def solution(mesh):
    return jax.shard_map(
        shards,
        mesh=mesh,
        in_specs=(
            P("img", "band", None, None),
            P(),
            P(),
            P("img", None, "band", None),
            P("img", "band", None, None),
            P("img", "band", None, None),
            P("img", "band"),
            P("band", None),
            P(),
            P(),
        ),
        out_specs=(P("img", None, "band", None), P("band", None), P(), P()),
        check_vma=False,
    )
```
